32 devices in a mesh: lon: 4 (over y, x), lat: 8 (over z, core).
Axes of the slice: x: 2, y: 2, z: 4, core: 2. Of those that a mesh axis runs over, the one named last changes fastest.
Arguments:
- tracer: float32 [16, 512, 5760], P(None, 'lat', 'lon'), may hold values from -6 to 6
- zonal_wind: float32 [16, 512, 5760], P(None, 'lat', 'lon'), may hold values from -1 to 1
- meridional_wind: float32 [16, 512, 5760], P(None, 'lat', 'lon'), may hold values from -1 to 1
- cutoff_wave: int32 [512], P('lat'), may hold values from 1 to 127, as said below
- polar_mask: int32 [512], P('lat'), may hold values from 0 to 1, as said below
Outputs:
- advanced: float32 [16, 512, 5760], P(None, 'lat', 'lon')
The draws below stay inside these ranges and needn't reach their ends.
Inputs may be any that keep to these rules, and one draw needn't show every extreme that they name: `polar_mask`: the rows with value 1 form one contiguous cap at each end of the latitude rows, each cap 512 // 6 rows or somewhat more. `cutoff_wave`: the value is 1 on the first and the last latitude row.
All inputs are finite; a program needn't handle non-finite values.
Results may differ from the reference program's by a relative error of at most 0.0001.
Values sent between devices are 32-bit elements; how exact they have to be, the bound alone decides.
No kernel may reach another device: no remote copies, remote signals or barrier semaphores. Data moves between devices by JAX's collectives and lax.ppermute only.
A program may use at most 192 MiB of HBM per device.

```python
import jax
import jax.numpy as jnp
from jax import lax

NLON = 5760
KMAX = 128
LEV = 16
NLAT = 512


def cap_rows(key):
    base = NLAT // 6
    extra = NLAT // 24 + 2
    caps = jax.random.randint(jax.random.fold_in(key, 7), (2,), 0, extra, dtype=jnp.int32)
    return (base + caps[0], base + caps[1])


def pole_distance(key):
    north_cap, south_cap = cap_rows(key)
    rows = jnp.arange(NLAT, dtype=jnp.int32)
    from_south = rows
    from_north = NLAT - 1 - rows
    in_south = from_south < south_cap
    in_north = from_north < north_cap
    distance = jnp.where(in_south, from_south, from_north)
    span = jnp.where(in_south, south_cap, north_cap)
    inside = jnp.logical_or(in_south, in_north)
    return (distance, span, inside)


def draw_polar_mask(key, part):
    distance, span, inside = pole_distance(key)
    return inside.astype(jnp.int32)


def draw_cutoff_wave(key, part):
    distance, span, inside = pole_distance(key)
    rows = jnp.arange(NLAT, dtype=jnp.int32)
    jitter = jax.random.randint(jax.random.fold_in(key, 11), (NLAT,), 0, 3, dtype=jnp.int32)
    jitter = jnp.where(distance > 0, jitter, 0)
    rising = 1 + distance * (KMAX - 2) // jnp.maximum(span, 1) + jitter
    rising = jnp.clip(rising, 1, KMAX - 1)
    other = jax.random.randint(jax.random.fold_in(key, 13), (NLAT,), 1, KMAX, dtype=jnp.int32)
    other = jnp.where(rows == NLAT // 2, KMAX - 1, other)
    return jnp.where(inside, rising, other).astype(jnp.int32)


def level_of(stream_key, dims, split, least, largest):
    level, own = 1.0, jax.random.fold_in(stream_key, 6)
    for position, parts in split:
        steps = jnp.exp(jax.random.uniform(jax.random.fold_in(own, position), (parts,), jnp.float32, least / len(split), largest / len(split)))
        level = level * jnp.repeat(steps, dims[position] // parts).reshape([-1 if axis == position else 1 for axis in range(len(dims))])
    return level


def scatter_about(own_key, dims, spread, bound, cuts=(), kind=jnp.bfloat16):
    drawn = spread * jax.random.normal(own_key, dims, jnp.float32)
    if cuts:
        drawn = drawn * level_of(own_key, dims, cuts, -0.22, 0.18)
    return jnp.clip(drawn, -bound, bound).astype(kind)


def setup_inputs(seed: int = 0) -> dict:
    key_of = jax.random.split(jax.random.key(seed), 6)
    return {
        "tracer": scatter_about(key_of[0], (LEV, NLAT, NLON), 1.0, 6.0, ((1, 8), (2, 4)), jnp.float32),
        "zonal_wind": scatter_about(key_of[1], (LEV, NLAT, NLON), 0.3, 1.0, ((1, 8), (2, 4)), jnp.float32),
        "meridional_wind": scatter_about(key_of[2], (LEV, NLAT, NLON), 0.3, 1.0, ((1, 8), (2, 4)), jnp.float32),
        "cutoff_wave": draw_cutoff_wave(jax.random.fold_in(key_of[5], 71), 0),
        "polar_mask": draw_polar_mask(jax.random.fold_in(key_of[5], 71), 0),
    }


DIFFUSION = 0.1


def tendency_level(state, zonal, meridional):
    flux_x = zonal * state
    flux_y = meridional * state
    half_turn = NLON // 2
    ghost_first = jnp.roll(state[:1], half_turn, axis=1)
    ghost_last = jnp.roll(state[-1:], half_turn, axis=1)
    flux_first = -jnp.roll(flux_y[:1], half_turn, axis=1)
    flux_last = -jnp.roll(flux_y[-1:], half_turn, axis=1)
    padded_state = jnp.concatenate([ghost_first, state, ghost_last], axis=0)
    padded_flux = jnp.concatenate([flux_first, flux_y, flux_last], axis=0)
    east = jnp.roll(state, -1, axis=1)
    west = jnp.roll(state, 1, axis=1)
    zonal_part = -0.5 * (jnp.roll(flux_x, -1, axis=1) - jnp.roll(flux_x, 1, axis=1))
    merid_part = -0.5 * (padded_flux[2:] - padded_flux[:-2])
    laplace = east + west + padded_state[2:] + padded_state[:-2] - 4.0 * state
    return zonal_part + merid_part + DIFFUSION * laplace


def filter_level(field, cutoff_wave, polar_mask):
    spectrum = jnp.fft.rfft(field, axis=1)
    wave = jnp.arange(NLON // 2 + 1, dtype=jnp.int32)
    keep = wave[None, :] <= cutoff_wave[:, None]
    smooth = jnp.fft.irfft(jnp.where(keep, spectrum, 0.0), n=NLON, axis=1)
    return jnp.where(polar_mask[:, None] == 1, smooth.astype(field.dtype), field)


def reference(tracer, zonal_wind, meridional_wind, cutoff_wave, polar_mask):
    def one_level(items):
        state, zonal, meridional = items
        for substep in range(2):
            moved = state + tendency_level(state, zonal, meridional)
            state = filter_level(moved, cutoff_wave, polar_mask)
        return state

    return lax.map(one_level, (tracer, zonal_wind, meridional_wind))
```

```python
import functools

import jax
import jax.numpy as jnp
import ml_dtypes
import numpy as np
from jax import lax
from jax.experimental import pallas as pl
from jax.experimental.pallas import tpu as pltpu
from jax.sharding import PartitionSpec as P

KMAX = 128
HALF = KMAX // 2
DIFFUSION = 0.1
GROUP = 4
SUB = 8
F32 = jnp.float32
BF16 = jnp.bfloat16
VMEM_LIMIT = 48 * 1024 * 1024


def wide(cells):
    return -(-(cells + 2) // 128) * 128


def split_np(values):
    high = values.astype(ml_dtypes.bfloat16)
    low = (values - high.astype(np.float64)).astype(ml_dtypes.bfloat16)
    return high, low


@functools.lru_cache(maxsize=None)
def wave_tables(cells, ways):
    total = cells * ways
    width = wide(cells)
    lane = np.arange(width)
    start = np.arange(ways)[:, None] * cells
    place = np.where(lane == width - 1, -1, lane)[None, :] + start
    used = (lane <= cells) | (lane == width - 1)
    column = np.arange(2 * KMAX)
    wave = column // KMAX * HALF + column % HALF
    sine = column % KMAX // HALF
    angle = (place[:, :, None] * wave[None, None, :] % total) * (2.0 * np.pi / total)
    table = np.where(sine == 1, np.sin(angle), np.cos(angle))
    project = split_np(np.where(used[None, :, None], table, 0.0))
    inside = np.where((lane < cells)[None, :, None], table, 0.0).transpose(0, 2, 1)
    rebuild = split_np(inside)
    return np.concatenate(project, axis=2), np.concatenate(rebuild, axis=1)


def split(x):
    high = x.astype(BF16)
    return high, (x - high.astype(F32)).astype(BF16)


def project(x, table):
    high, low = split(x)
    both = jnp.dot(high, table, preferred_element_type=F32)
    cross = jnp.dot(low, table[:, : 2 * KMAX], preferred_element_type=F32)
    return both[:, : 2 * KMAX] + both[:, 2 * KMAX :] + cross


def rebuild(coefficients, table):
    high, low = split(coefficients)
    both = jnp.dot(jnp.concatenate([high, high], axis=1), table, preferred_element_type=F32)
    return both + jnp.dot(low, table[: 2 * KMAX], preferred_element_type=F32)


def padded(x, width):
    return jnp.concatenate([x, jnp.zeros((x.shape[0], width - x.shape[1]), F32)], axis=1)


def along_lon(s, u):
    width = s.shape[1]
    spread = DIFFUSION * s
    carry = (0.5 * u) * s
    return (
        (1.0 - 4.0 * DIFFUSION) * s
        + pltpu.roll(spread - carry, width - 1, 1)
        + pltpu.roll(spread + carry, 1, 1)
    )


def moved_rows(s, u, v):
    rows = s.shape[0]
    spread = DIFFUSION * s
    carry = (0.5 * v) * s
    row = lax.broadcasted_iota(jnp.int32, s.shape, 0)
    from_next = jnp.where(row == rows - 1, 0.0, pltpu.roll(spread - carry, rows - 1, 0))
    from_last = jnp.where(row == 0, 0.0, pltpu.roll(spread + carry, 1, 0))
    return along_lon(s, u) + from_next + from_last


def put_halves(ref, at, value):
    for half in range(2):
        ref[half, at, :] = value[:, half * KMAX : (half + 1) * KMAX]


def both_halves(ref, at):
    return jnp.concatenate([ref[0, at, :], ref[1, at, :]], axis=1)


def first_kernel(lon_ref, s_ref, u_ref, v_ref, table_ref, moved_ref, coef_ref):
    del lon_ref
    width = moved_ref.shape[2]
    rows = s_ref.shape[1]
    for g in range(GROUP):
        moved_ref[g] = moved_rows(
            padded(s_ref[g], width), padded(u_ref[g], width), padded(v_ref[g], width)
        )
    x = moved_ref[...].reshape(GROUP * rows, width)
    put_halves(coef_ref, slice(None), project(x, table_ref[...]))


def pack_rows(cut_ref, source_ref, first, out_refs):
    rows = cut_ref.shape[0]

    def body(r, unit):
        cut = cut_ref[r]
        kept = (cut >= 0).astype(jnp.int32)
        more = (cut >= HALF).astype(jnp.int32)

        def put(half, at):
            for part, out_ref in enumerate(out_refs):
                out_ref[at] = source_ref[half, pl.ds(r + part * SUB * rows, SUB, stride=rows), :]

        pl.when(kept == 1)(lambda: put(0, unit))
        pl.when(more == 1)(lambda: put(1, unit + 1))
        return unit + kept + more

    lax.fori_loop(0, rows, body, first)


def weight(half, cut, total):
    lane = lax.broadcasted_iota(jnp.int32, (SUB, KMAX), 1)
    wave = half * HALF + lane % HALF
    scale = jnp.where(wave == 0, 1.0 / total, 2.0 / total)
    return jnp.where(wave <= cut, scale, 0.0)


def unpack_rows(cut_ref, pairs, first, total, out_ref):
    rows = cut_ref.shape[0]
    out_ref[...] = jnp.zeros_like(out_ref)

    def body(r, unit):
        cut = cut_ref[r]
        kept = (cut >= 0).astype(jnp.int32)
        more = (cut >= HALF).astype(jnp.int32)

        def take(half, at):
            scale = weight(half, cut, total)
            for part, (a_ref, b_ref) in enumerate(pairs):
                out_ref[half, pl.ds(r + part * SUB * rows, SUB, stride=rows), :] = (
                    a_ref[at] + b_ref[at]
                ) * scale

        pl.when(kept == 1)(lambda: take(0, unit))
        pl.when(more == 1)(lambda: take(1, unit + 1))
        return unit + kept + more

    lax.fori_loop(0, rows, body, first)


def join_kernel(
    lon_ref, cut_ref, coef_ref, mine_ref, north_ref, south_ref, table_ref,
    flow_ref, a_ref, b_ref, sum_ref,
):
    del lon_ref
    rows = cut_ref.shape[0]
    levels = coef_ref.shape[1] // rows

    def down(s, v):
        return DIFFUSION * s + (0.5 * v) * s

    def up(s, v):
        return DIFFUSION * s - (0.5 * v) * s

    flow_ref[0] = down(north_ref[0], north_ref[2])
    flow_ref[1] = up(south_ref[0], south_ref[2])
    flow_ref[2] = along_lon(north_ref[0], north_ref[1]) + north_ref[3] + up(mine_ref[0], mine_ref[1])
    flow_ref[3] = along_lon(south_ref[0], south_ref[1]) + south_ref[3] + down(mine_ref[2], mine_ref[3])
    extra = project(flow_ref[...].reshape(4 * levels, flow_ref.shape[2]), table_ref[...])
    sum_ref[...] = coef_ref[...]
    for part, out_ref in enumerate((a_ref, b_ref)):
        at = part * SUB
        first = pl.ds(at * rows, SUB, stride=rows)
        last = pl.ds(at * rows + rows - 1, SUB, stride=rows)
        for half in range(2):
            cols = slice(half * KMAX, (half + 1) * KMAX)
            sum_ref[half, first, :] = sum_ref[half, first, :] + extra[at : at + SUB, cols]
            sum_ref[half, last, :] = sum_ref[half, last, :] + extra[levels + at : levels + at + SUB, cols]
            out_ref[half] = extra[2 * levels + at : 2 * levels + at + SUB, cols]
            out_ref[2 + half] = extra[3 * levels + at : 3 * levels + at + SUB, cols]
    pack_rows(cut_ref, sum_ref, 4, (a_ref, b_ref))


def second_kernel(
    total, cells,
    lon_ref, cut_ref, a0_ref, a1_ref, b0_ref, b1_ref, flow_ref, edge_cut_ref, edge_fix_ref, edge_v_ref,
    moved_ref, fix_ref, mask_ref, u_ref, v_ref, table_ref, back_ref,
    out_ref, a_ref, b_ref, coef_ref, sum_ref, step_ref, edge_ref,
):
    del lon_ref
    step = pl.program_id(0)
    rows = cut_ref.shape[0]
    width = out_ref.shape[2]
    levels = step_ref.shape[1]
    pairs = ((a0_ref, a1_ref), (b0_ref, b1_ref))

    @pl.when(step == 0)
    def _():
        unpack_rows(cut_ref, pairs, 4, total, coef_ref)
        for side in range(2):
            for part, (x_ref, y_ref) in enumerate(pairs):
                at = side * levels + part * SUB
                for half in range(2):
                    scale = weight(half, edge_cut_ref[side, :, :], total)
                    edge_ref[at : at + SUB, half * KMAX : (half + 1) * KMAX] = (
                        x_ref[2 * side + half] + y_ref[2 * side + half]
                    ) * scale
        smooth = rebuild(edge_ref[...], back_ref[...])
        lane = lax.broadcasted_iota(jnp.int32, (levels, width), 1)
        for side in range(2):
            plain = flow_ref[2 + side]
            plain = jnp.where(lane == 0, plain + edge_fix_ref[side, :, 0:1], plain)
            plain = jnp.where(lane == cells - 1, plain + edge_fix_ref[side, :, 1:2], plain)
            plain = jnp.where(lane < cells, plain, 0.0)
            filtered = edge_cut_ref[side, 0:1, 0:1] >= 0
            s = jnp.where(filtered, smooth[side * levels : (side + 1) * levels], plain)
            carry = (0.5 * edge_v_ref[side]) * s
            step_ref[side] = DIFFUSION * s + (carry if side == 0 else -carry)

    smooth = rebuild(both_halves(coef_ref, pl.ds(step * (GROUP * rows), GROUP * rows)), back_ref[...])
    lane = lax.broadcasted_iota(jnp.int32, (rows, width), 1)
    row = lax.broadcasted_iota(jnp.int32, (rows, width), 0)
    filtered = mask_ref[...] == 1
    for g in range(GROUP):
        level = step * GROUP + g
        plain = moved_ref[g]
        plain = plain + jnp.where(row == 0, flow_ref[0, pl.ds(level, 1), :], 0.0)
        plain = plain + jnp.where(row == rows - 1, flow_ref[1, pl.ds(level, 1), :], 0.0)
        plain = plain + jnp.where(lane == 0, fix_ref[g][:, 0:1], 0.0)
        plain = plain + jnp.where(lane == cells - 1, fix_ref[g][:, 1:2], 0.0)
        plain = jnp.where(lane < cells, plain, 0.0)
        s = jnp.where(filtered, smooth[g * rows : (g + 1) * rows], plain)
        moved = moved_rows(s, padded(u_ref[g], width), padded(v_ref[g], width))
        moved = moved + jnp.where(row == 0, step_ref[0, pl.ds(level, 1), :], 0.0)
        moved = moved + jnp.where(row == rows - 1, step_ref[1, pl.ds(level, 1), :], 0.0)
        out_ref[g] = moved
    x = out_ref[...].reshape(GROUP * rows, width)
    put_halves(sum_ref, pl.ds(step * (GROUP * rows), GROUP * rows), project(x, table_ref[...]))

    @pl.when(step == pl.num_programs(0) - 1)
    def _():
        pack_rows(cut_ref, sum_ref, 0, (a_ref, b_ref))


def third_kernel(
    total, cells,
    lon_ref, cut_ref, a0_ref, a1_ref, b0_ref, b1_ref, moved_ref, fix_ref, mask_ref, back_ref,
    out_ref, coef_ref,
):
    del lon_ref
    step = pl.program_id(0)
    rows = cut_ref.shape[0]
    width = moved_ref.shape[2]

    @pl.when(step == 0)
    def _():
        unpack_rows(cut_ref, ((a0_ref, a1_ref), (b0_ref, b1_ref)), 0, total, coef_ref)

    smooth = rebuild(both_halves(coef_ref, pl.ds(step * (GROUP * rows), GROUP * rows)), back_ref[...])
    lane = lax.broadcasted_iota(jnp.int32, (rows, width), 1)
    filtered = mask_ref[...] == 1
    for g in range(GROUP):
        plain = moved_ref[g]
        plain = plain + jnp.where(lane == 0, fix_ref[g][:, 0:1], 0.0)
        plain = plain + jnp.where(lane == cells - 1, fix_ref[g][:, 1:2], 0.0)
        out_ref[g] = jnp.where(filtered, smooth[g * rows : (g + 1) * rows], plain)[:, :cells]


def whole(shape):
    return pl.BlockSpec(shape, lambda *_: (0,) * len(shape))


def by_group(shape):
    return pl.BlockSpec((GROUP, *shape[1:]), lambda i, *_: (i, 0, 0))


def own_table(shape):
    return pl.BlockSpec((None, *shape[1:]), lambda i, lon, *_: (lon[0], 0, 0))


def call(kernel, steps, prefetch, inputs, outputs, scratch):
    return pl.pallas_call(
        kernel,
        grid_spec=pltpu.PrefetchScalarGridSpec(
            num_scalar_prefetch=len(prefetch),
            grid=(steps,),
            in_specs=[spec for _, spec in inputs],
            out_specs=[spec for _, spec in outputs],
            scratch_shapes=scratch,
        ),
        out_shape=[jax.ShapeDtypeStruct(shape, F32) for shape, _ in outputs],
        compiler_params=pltpu.CompilerParams(vmem_limit_bytes=VMEM_LIMIT),
    )(*prefetch, *[array for array, _ in inputs])


def swap(x, bit):
    count = lax.axis_size("lon")
    return lax.ppermute(x, "lon", [(i, i ^ (1 << bit)) for i in range(count)])


def sum_over_lon(a, b):
    bits = lax.axis_size("lon").bit_length() - 1
    for i in range(bits):
        a_in, b_in = swap(a, i), swap(b, bits - 1 - i)
        if i == bits - 1:
            return a, a_in, b, b_in
        a, b = a + a_in, b + b_in


def lat_ring(bands, ways, turn):
    pairs = []
    for band in range(bands):
        for l in range(ways):
            east = l < ways // 2
            other = (l + ways // 2) % ways
            step = 1 if east == (turn == 0) else -1
            to = (band + step, l) if 0 <= band + step < bands else (band, other)
            pairs.append((l * bands + band, to[1] * bands + to[0]))
    return pairs


def lon_edges(moved, cells):
    ways = lax.axis_size("lon")
    west = lax.ppermute(moved[..., cells], "lon", [(i, (i + 1) % ways) for i in range(ways)])
    east = lax.ppermute(moved[..., -1], "lon", [(i, (i - 1) % ways) for i in range(ways)])
    return jnp.stack([west, east], axis=-1)


def on_device(tracer, zonal, meridional, cutoff_wave, polar_mask):
    levels, rows, cells = tracer.shape
    ways, bands = lax.axis_size("lon"), lax.axis_size("lat")
    width = wide(cells)
    total = cells * ways
    tables = wave_tables(cells, ways)
    table, back = jnp.asarray(tables[0]), jnp.asarray(tables[1])
    lon = lax.axis_index("lon").reshape(1)
    band = lax.axis_index("lat")
    cut = jnp.where(polar_mask == 1, cutoff_wave, -1)
    mask = polar_mask[:, None]
    steps = levels // GROUP

    def edge_rows(at, beyond, sign):
        s, v = tracer[:, beyond], meridional[:, beyond]
        out = jnp.stack(
            [tracer[:, at], zonal[:, at], meridional[:, at], DIFFUSION * s + sign * (0.5 * v) * s]
        )
        tail = jnp.full((4, levels, width - cells), cut[at].astype(F32))
        return jnp.concatenate([out, tail], axis=2)

    top, bottom = edge_rows(0, 1, -1.0), edge_rows(rows - 1, rows - 2, 1.0)
    near = lon[0] < ways // 2
    ring = ("lon", "lat")
    got0 = lax.ppermute(jnp.where(near, bottom, top), ring, lat_ring(bands, ways, 0))
    got1 = lax.ppermute(jnp.where(near, top, bottom), ring, lat_ring(bands, ways, 1))

    moved, coef = call(
        first_kernel, steps, (lon,),
        [(tracer, by_group(tracer.shape)), (zonal, by_group(tracer.shape)), (meridional, by_group(tracer.shape)),
         (table, own_table(table.shape))],
        [((levels, rows, width), by_group((levels, rows, width))),
         ((2, levels * rows, KMAX), pl.BlockSpec((2, GROUP * rows, KMAX), lambda i, *_: (0, i, 0)))],
        [],
    )

    north = jnp.where(near, got0, got1)
    south = jnp.where(near, got1, got0)
    edge_cut = jnp.stack([north[0, 0, cells], south[0, 0, cells]]).astype(jnp.int32)
    edge_cut = jnp.broadcast_to(edge_cut[:, None, None], (2, SUB, KMAX))
    inside = jnp.arange(width) < cells
    turn = jnp.array([1.0, 1.0, -1.0, 1.0], F32)[:, None, None]
    north = jnp.where(inside, jnp.where(band == 0, turn, 1.0) * north, 0.0)
    south = jnp.where(inside, jnp.where(band == bands - 1, turn, 1.0) * south, 0.0)
    mine = jnp.where(inside, jnp.stack([top[0], top[2], bottom[0], bottom[2]]), 0.0)
    edge_v = jnp.stack([north[2], south[2]])

    units = 2 * rows + 4
    flow, a, b = call(
        join_kernel, 1, (lon, cut),
        [(coef, whole(coef.shape)), (mine, whole(mine.shape)),
         (north, whole(north.shape)), (south, whole(south.shape)), (table, own_table(table.shape))],
        [((4, levels, width), whole((4, levels, width))), ((units, SUB, KMAX), whole((units, SUB, KMAX))),
         ((units, SUB, KMAX), whole((units, SUB, KMAX)))],
        [pltpu.VMEM((2, levels * rows, KMAX), F32)],
    )
    sums = sum_over_lon(a, b)
    fix = lon_edges(jnp.concatenate([moved, flow[2:].transpose(1, 0, 2)], axis=1)[:, :, cells - 1 :], 1)
    edge_fix = fix[:, rows:].transpose(1, 0, 2)
    fix = fix[:, :rows]

    moved, a, b = call(
        functools.partial(second_kernel, total, cells), steps, (lon, cut),
        [*[(x, whole(x.shape)) for x in (*sums, flow, edge_cut, edge_fix, edge_v)],
         (moved, by_group(moved.shape)), (fix, by_group(fix.shape)), (mask, whole(mask.shape)),
         (zonal, by_group(tracer.shape)), (meridional, by_group(tracer.shape)),
         (table, own_table(table.shape)), (back, own_table(back.shape))],
        [((levels, rows, width), by_group((levels, rows, width))), ((2 * rows, SUB, KMAX), whole((2 * rows, SUB, KMAX))),
         ((2 * rows, SUB, KMAX), whole((2 * rows, SUB, KMAX)))],
        [pltpu.VMEM((2, levels * rows, KMAX), F32), pltpu.VMEM((2, levels * rows, KMAX), F32),
         pltpu.VMEM((2, levels, width), F32), pltpu.VMEM((2 * levels, 2 * KMAX), F32)],
    )
    sums = sum_over_lon(a, b)
    fix = lon_edges(moved, cells)

    (out,) = call(
        functools.partial(third_kernel, total, cells), steps, (lon, cut),
        [*[(x, whole(x.shape)) for x in sums], (moved, by_group(moved.shape)), (fix, by_group(fix.shape)),
         (mask, whole(mask.shape)), (back, own_table(back.shape))],
        [(tracer.shape, by_group(tracer.shape))],
        [pltpu.VMEM((2, levels * rows, KMAX), F32)],
    )
    return out


def solution(mesh):
    placed = (
        P(None, "lat", "lon"),
        P(None, "lat", "lon"),
        P(None, "lat", "lon"),
        P("lat"),
        P("lat"),
    )
    return jax.shard_map(
        on_device, mesh=mesh, in_specs=placed, out_specs=P(None, "lat", "lon"), check_vma=False
    )
```

```python
import functools

import jax
import jax.numpy as jnp
import ml_dtypes
import numpy as np
from jax import lax
from jax.experimental import pallas as pl
from jax.experimental.pallas import tpu as pltpu
from jax.sharding import PartitionSpec as P

KMAX = 128
HALF = KMAX // 2
DIFFUSION = 0.1
GROUP = 4
SUB = 8
LIMITS = (48, 68, 92, 128)
F32 = jnp.float32
BF16 = jnp.bfloat16
MIB = 1024 * 1024


def wide(cells):
    return -(-(cells + 2) // 128) * 128


def split_np(values):
    high = values.astype(ml_dtypes.bfloat16)
    low = (values - high.astype(np.float64)).astype(ml_dtypes.bfloat16)
    return high, low


@functools.lru_cache(maxsize=None)
def wave_tables(cells, ways):
    total = cells * ways
    width = wide(cells)
    lane = np.arange(width)
    start = np.arange(ways)[:, None] * cells
    place = np.where(lane == width - 1, -1, lane)[None, :] + start
    used = (lane <= cells) | (lane == width - 1)
    column = np.arange(2 * KMAX)
    wave = column // KMAX * HALF + column % HALF
    sine = column % KMAX // HALF
    angle = (place[:, :, None] * wave[None, None, :] % total) * (2.0 * np.pi / total)
    table = np.where(sine == 1, np.sin(angle), np.cos(angle))
    project = split_np(np.where(used[None, :, None], table, 0.0))
    inside = np.where((lane < cells)[None, :, None], table, 0.0).transpose(0, 2, 1)
    rebuild = split_np(inside)
    return np.concatenate(project, axis=2), np.concatenate(rebuild, axis=1)


def split(x):
    high = x.astype(BF16)
    return high, (x - high.astype(F32)).astype(BF16)


def project(x, table):
    high, low = split(x)
    both = jnp.dot(high, table, preferred_element_type=F32)
    cross = jnp.dot(low, table[:, : 2 * KMAX], preferred_element_type=F32)
    return both[:, : 2 * KMAX] + both[:, 2 * KMAX :] + cross


def rebuild(coefficients, table):
    high, low = split(coefficients)
    both = jnp.dot(jnp.concatenate([high, high], axis=1), table, preferred_element_type=F32)
    return both + jnp.dot(low, table[: 2 * KMAX], preferred_element_type=F32)


def padded(x, width):
    return jnp.concatenate([x, jnp.zeros((x.shape[0], width - x.shape[1]), F32)], axis=1)


def along_lon(s, u):
    width = s.shape[1]
    spread = DIFFUSION * s
    carry = (0.5 * u) * s
    return (
        (1.0 - 4.0 * DIFFUSION) * s
        + pltpu.roll(spread - carry, width - 1, 1)
        + pltpu.roll(spread + carry, 1, 1)
    )


def moved_rows(s, u, v):
    rows = s.shape[0]
    spread = DIFFUSION * s
    carry = (0.5 * v) * s
    row = lax.broadcasted_iota(jnp.int32, s.shape, 0)
    from_next = jnp.where(row == rows - 1, 0.0, pltpu.roll(spread - carry, rows - 1, 0))
    from_last = jnp.where(row == 0, 0.0, pltpu.roll(spread + carry, 1, 0))
    return along_lon(s, u) + from_next + from_last


def put_halves(ref, at, value):
    for half in range(2):
        ref[half, at, :] = value[:, half * KMAX : (half + 1) * KMAX]


def both_halves(ref, at):
    return jnp.concatenate([ref[0, at, :], ref[1, at, :]], axis=1)


def southward(s, v):
    return DIFFUSION * s + (0.5 * v) * s


def northward(s, v):
    return DIFFUSION * s - (0.5 * v) * s


def edge_kernel(
    info_ref, cut_ref, s0_ref, u0_ref, v0_ref, s1_ref, u1_ref, v1_ref, ring0_ref, ring1_ref, own_ref,
):
    levels, width = own_ref.shape[1:]
    rows = cut_ref.shape[0]
    near = info_ref[1] == 1
    last = s1_ref.shape[1] - 1
    sides = []
    for refs, at, beyond, flow, cut in (
        ((s0_ref, u0_ref, v0_ref), 0, 1, northward, cut_ref[0]),
        ((s1_ref, u1_ref, v1_ref), last, last - 1, southward, cut_ref[rows - 1]),
    ):
        s, u, v = (ref[:, at, :] for ref in refs)
        tail = jnp.full((levels, width - s.shape[1]), cut.astype(F32))
        parts = [padded(u, width), padded(v, width), padded(flow(refs[0][:, beyond, :], refs[2][:, beyond, :]), width)]
        sides.append([jnp.concatenate([s, tail], axis=1), *parts])
    own_ref[0] = padded(northward(s0_ref[:, 0, :], v0_ref[:, 0, :]), width)
    own_ref[1] = padded(southward(s1_ref[:, last, :], v1_ref[:, last, :]), width)
    for i in range(4):
        ring0_ref[i] = jnp.where(near, sides[1][i], sides[0][i])
        ring1_ref[i] = jnp.where(near, sides[0][i], sides[1][i])


def group_copies(hbm_refs, buffers, sem, first, i):
    return [
        pltpu.make_async_copy(h.at[pl.ds(first + i * GROUP, GROUP)], b.at[pl.ds(i * GROUP, GROUP)], sem.at[q, i])
        for q, (h, b) in enumerate(zip(hbm_refs, buffers))
    ]


def first_body(first, s_ref, u_ref, v_ref, table_ref, moved_ref, coef_ref, buffers, sem):
    levels, rows, width = moved_ref.shape
    steps = levels // GROUP

    def body(i, _):
        for copy in group_copies((s_ref, u_ref, v_ref), buffers, sem, first, i):
            copy.wait()
        for g in range(GROUP):
            level = i * GROUP + g
            moved_ref[level] = moved_rows(*[padded(b[level], width) for b in buffers])
        x = moved_ref[pl.ds(i * GROUP, GROUP)].reshape(GROUP * rows, width)
        put_halves(coef_ref, pl.ds(i * GROUP * rows, GROUP * rows), project(x, table_ref[...]))
        return 0

    lax.fori_loop(0, steps, body, 0)


def first_kernel(
    first, with_tables, info_ref, s_ref, u_ref, v_ref, *refs
):
    if with_tables:
        (tables_ref, backs_ref, moved_ref, coef_ref, table_ref, back_ref, s_buf, u_buf, v_buf, sem, table_sem) = refs
    else:
        (table_ref, moved_ref, coef_ref, s_buf, u_buf, v_buf, sem) = refs
    buffers = (s_buf, u_buf, v_buf)
    steps = moved_ref.shape[0] // GROUP
    if with_tables:
        lon = info_ref[0]
        loads = [
            pltpu.make_async_copy(tables_ref.at[lon], table_ref, table_sem.at[0]),
            pltpu.make_async_copy(backs_ref.at[lon], back_ref, table_sem.at[1]),
        ]
    for i in range(steps):
        for copy in group_copies((s_ref, u_ref, v_ref), buffers, sem, first, i):
            copy.start()
        if with_tables and i == 0:
            loads[0].start()
    if with_tables:
        loads[1].start()
        loads[0].wait()
    first_body(first, s_ref, u_ref, v_ref, table_ref, moved_ref, coef_ref, buffers, sem)
    if with_tables:
        loads[1].wait()


def pack_rows(cut_ref, source_ref, first, out_ref):
    rows = cut_ref.shape[0]

    def body(r, unit):
        cut = cut_ref[r]
        for half in range(2):
            out_ref[unit + half] = source_ref[half, pl.ds(r, SUB, stride=rows), :]
        return unit + (cut >= 0).astype(jnp.int32) + (cut >= HALF).astype(jnp.int32)

    lax.fori_loop(0, rows, body, first, unroll=8)


def scaled(x, half, cut, total):
    lane = lax.broadcasted_iota(jnp.int32, (SUB, KMAX), 1)
    wave = half * HALF + lane % HALF
    scale = jnp.where(wave == 0, 1.0 / total, 2.0 / total)
    return jnp.where(wave <= cut, x * scale, 0.0)


def unpack_rows(cut_ref, a_ref, b_ref, first, total, out_ref):
    rows = cut_ref.shape[0]
    last = a_ref.shape[0] - 1

    def body(r, unit):
        cut = cut_ref[r]
        for half in range(2):
            at = jnp.minimum(unit + half, last)
            out_ref[half, pl.ds(r, SUB, stride=rows), :] = scaled(a_ref[at] + b_ref[at], half, cut, total)
        return unit + (cut >= 0).astype(jnp.int32) + (cut >= HALF).astype(jnp.int32)

    lax.fori_loop(0, rows, body, first, unroll=8)


def join_kernel(
    cells,
    info_ref, cut_ref, coef_ref, own_ref, ring0_ref, ring1_ref, table_ref, moved_in_ref,
    moved_ref, flow_ref, edge_v_ref, edge_cut_ref, out_ref, sum_ref,
):
    del moved_in_ref
    rows = cut_ref.shape[0]
    levels, width = flow_ref.shape[1:]
    near = info_ref[1] == 1
    lane = lax.broadcasted_iota(jnp.int32, (levels, width), 1)
    for side in range(2):
        got = [jnp.where(near == (side == 0), ring0_ref[i], ring1_ref[i]) for i in range(4)]
        edge_cut_ref[side] = jnp.broadcast_to(got[0][:, cells : cells + 1], (levels, KMAX))
        s = jnp.where(lane < cells, got[0], 0.0)
        v = jnp.where(info_ref[2 + side] == 1, -got[2], got[2])
        edge_v_ref[side] = v
        flow_ref[side] = southward(s, v) if side == 0 else northward(s, v)
        flow_ref[2 + side] = along_lon(s, got[1]) + got[3] + own_ref[side]
    extra = project(flow_ref[...].reshape(4 * levels, width), table_ref[...])
    sum_ref[...] = coef_ref[...]
    first = pl.ds(0, SUB, stride=rows)
    last = pl.ds(rows - 1, SUB, stride=rows)
    for half in range(2):
        part = extra[:, half * KMAX : (half + 1) * KMAX]
        sum_ref[half, first, :] = sum_ref[half, first, :] + part[:levels]
        sum_ref[half, last, :] = sum_ref[half, last, :] + part[levels : 2 * levels]
        out_ref[half] = part[2 * levels : 3 * levels]
        out_ref[2 + half] = part[3 * levels :]
    pack_rows(cut_ref, sum_ref, 4, out_ref)
    for level in range(levels):
        moved_ref[level, 0:1, :] = moved_ref[level, 0:1, :] + flow_ref[0, level : level + 1, :]
        moved_ref[level, rows - 1 : rows, :] = moved_ref[level, rows - 1 : rows, :] + flow_ref[1, level : level + 1, :]


def closed(x, fix, cells):
    end = cells // 128 * 128
    lane = lax.broadcasted_iota(jnp.int32, (x.shape[0], 128), 1)
    head = x[:, :128] + jnp.where(lane == 0, fix[:, 0:1], 0.0)
    tail = x[:, end : end + 128] + jnp.where(lane == cells - 1 - end, fix[:, 1:2], 0.0)
    pieces = [head, x[:, 128:end], jnp.where(lane < cells - end, tail, 0.0)]
    if x.shape[1] > end + 128:
        pieces.append(jnp.zeros((x.shape[0], x.shape[1] - end - 128), F32))
    return jnp.concatenate(pieces, axis=1)


def second_kernel(
    first, total, cells,
    cut_ref, a_ref, b_ref, flow_ref, edge_v_ref, edge_cut_ref, edge_fix_ref, moved_ref, fix_ref, mask_ref,
    table_ref, back_ref, u_ref, v_ref,
    out_ref, pay_ref, coef_ref, sum_ref, step_ref, edge_ref, u_buf, v_buf, sem,
):
    rows = cut_ref.shape[0]
    levels, _, width = out_ref.shape
    steps = levels // GROUP
    for i in range(steps):
        for copy in group_copies((u_ref, v_ref), (u_buf, v_buf), sem, first, i):
            copy.start()
    unpack_rows(cut_ref, a_ref, b_ref, 4, total, coef_ref)
    for side in range(2):
        for half in range(2):
            at = 2 * side + half
            cut = edge_cut_ref[side].astype(jnp.int32)
            edge_ref[side * levels : (side + 1) * levels, half * KMAX : (half + 1) * KMAX] = scaled(
                a_ref[at] + b_ref[at], half, cut, total
            )
    smooth = rebuild(edge_ref[...], back_ref[...])
    for side in range(2):
        plain = closed(flow_ref[2 + side], edge_fix_ref[side], cells)
        filtered = edge_cut_ref[side][:, 0:1] >= 0.0
        s = jnp.where(filtered, smooth[side * levels : (side + 1) * levels], plain)
        step_ref[side] = (southward if side == 0 else northward)(s, edge_v_ref[side])
    filtered = mask_ref[...] == 1

    def body(i, _):
        for copy in group_copies((u_ref, v_ref), (u_buf, v_buf), sem, first, i):
            copy.wait()
        smooth = rebuild(both_halves(coef_ref, pl.ds(i * GROUP * rows, GROUP * rows)), back_ref[...])
        for g in range(GROUP):
            level = i * GROUP + g
            plain = closed(moved_ref[level], fix_ref[level], cells)
            s = jnp.where(filtered, smooth[g * rows : (g + 1) * rows], plain)
            out_ref[level] = moved_rows(s, padded(u_buf[level], width), padded(v_buf[level], width))
            out_ref[level, 0:1, :] = out_ref[level, 0:1, :] + step_ref[0, pl.ds(level, 1), :]
            out_ref[level, rows - 1 : rows, :] = (
                out_ref[level, rows - 1 : rows, :] + step_ref[1, pl.ds(level, 1), :]
            )
        x = out_ref[pl.ds(i * GROUP, GROUP)].reshape(GROUP * rows, width)
        put_halves(sum_ref, pl.ds(i * GROUP * rows, GROUP * rows), project(x, table_ref[...]))
        return 0

    lax.fori_loop(0, steps, body, 0)
    pack_rows(cut_ref, sum_ref, 0, pay_ref)


def third_kernel(
    first, total, cells, cut_ref, a_ref, b_ref, moved_ref, fix_ref, mask_ref, back_ref, *refs
):
    out_ref, coef_ref, buffer, sem = refs[-4:]
    rows = cut_ref.shape[0]
    levels = moved_ref.shape[0]
    unpack_rows(cut_ref, a_ref, b_ref, 0, total, coef_ref)
    filtered = mask_ref[...] == 1

    def store(i):
        return pltpu.make_async_copy(
            buffer.at[pl.ds(i * GROUP, GROUP)], out_ref.at[pl.ds(first + i * GROUP, GROUP)], sem.at[i]
        )

    def body(i, _):
        smooth = rebuild(both_halves(coef_ref, pl.ds(i * GROUP * rows, GROUP * rows)), back_ref[...])
        for g in range(GROUP):
            level = i * GROUP + g
            plain = closed(moved_ref[level], fix_ref[level], cells)
            buffer[level] = jnp.where(filtered, smooth[g * rows : (g + 1) * rows], plain)[:, :cells]
        store(i).start()
        return 0

    lax.fori_loop(0, levels // GROUP, body, 0)
    for i in range(levels // GROUP):
        store(i).wait()


SMEM = pl.BlockSpec(memory_space=pltpu.SMEM)
VMEM = pl.BlockSpec(memory_space=pltpu.VMEM)
HBM = pl.BlockSpec(memory_space=pl.ANY)


def shape(*dims, dtype=F32):
    return jax.ShapeDtypeStruct(dims, dtype)


def call(kernel, inputs, outputs, scratch, mib, aliases=None):
    return pl.pallas_call(
        kernel,
        in_specs=[spec for _, spec in inputs],
        out_specs=[spec for _, spec in outputs],
        out_shape=[what for what, _ in outputs],
        scratch_shapes=scratch,
        input_output_aliases=aliases or {},
        compiler_params=pltpu.CompilerParams(vmem_limit_bytes=mib * MIB),
    )(*[array for array, _ in inputs])


def swap(x, bit):
    count = lax.axis_size("lon")
    return lax.ppermute(x, "lon", [(i, i ^ (1 << bit)) for i in range(count)])


def sum_over_lon(x, upward):
    bits = lax.axis_size("lon").bit_length() - 1
    for i in range(bits):
        got = swap(x, i if upward else bits - 1 - i)
        if i == bits - 1:
            return x, got
        x = x + got


def lat_ring(bands, ways, turn):
    pairs = []
    for band in range(bands):
        for l in range(ways):
            east = l < ways // 2
            other = (l + ways // 2) % ways
            step = 1 if east == (turn == 0) else -1
            to = (band + step, l) if 0 <= band + step < bands else (band, other)
            pairs.append((l * bands + band, to[1] * bands + to[0]))
    return pairs


def lon_edges(arrays, cells):
    ways = lax.axis_size("lon")
    count = [x.shape[:-1] for x in arrays]
    out = []
    for lane, way in ((cells, 1), (-1, -1)):
        column = jnp.concatenate([x[..., lane].reshape(-1) for x in arrays])
        out.append(lax.ppermute(column, "lon", [(i, (i + way) % ways) for i in range(ways)]))
    both = jnp.stack(out, axis=-1)
    pieces, at = [], 0
    for dims in count:
        size = int(np.prod(dims))
        pieces.append(both[at : at + size].reshape(*dims, 2))
        at += size
    return pieces


def on_device(tracer, zonal, meridional, cutoff_wave, polar_mask):
    levels, rows, cells = tracer.shape
    ways, bands = lax.axis_size("lon"), lax.axis_size("lat")
    width = wide(cells)
    total = cells * ways
    tables = wave_tables(cells, ways)
    lon, band = lax.axis_index("lon"), lax.axis_index("lat")
    info = jnp.stack([lon, lon < ways // 2, band == 0, band == bands - 1]).astype(jnp.int32)
    cut = jnp.where(polar_mask == 1, cutoff_wave, -1)
    kept = jnp.sum((cut >= 0).astype(jnp.int32) + (cut >= HALF).astype(jnp.int32))
    mask = polar_mask[:, None]
    parts = levels // SUB
    steps = SUB // GROUP
    winds = (tracer, zonal, meridional)

    top = pl.BlockSpec((levels, SUB, cells), lambda i: (0, 0, 0))
    bottom = pl.BlockSpec((levels, SUB, cells), lambda i: (0, rows // SUB - 1, 0))
    full = pl.BlockSpec((4, levels, width), lambda i: (0, 0, 0))
    ring0, ring1, own = pl.pallas_call(
        edge_kernel,
        grid=(1,),
        in_specs=[SMEM, SMEM, top, top, top, bottom, bottom, bottom],
        out_specs=[full, full, pl.BlockSpec((2, levels, width), lambda i: (0, 0, 0))],
        out_shape=[shape(4, levels, width), shape(4, levels, width), shape(2, levels, width)],
        compiler_params=pltpu.CompilerParams(vmem_limit_bytes=20 * MIB),
    )(info, cut, *winds, *winds)
    ring = ("lon", "lat")
    got0 = lax.ppermute(ring0, ring, lat_ring(bands, ways, 0))
    got1 = lax.ppermute(ring1, ring, lat_ring(bands, ways, 1))

    table_shape, back_shape = tables[0].shape[1:], tables[1].shape[1:]
    grid_shape = shape(SUB, rows, width)
    coef_shape = shape(2, SUB * rows, KMAX)
    buffer = pltpu.VMEM((SUB, rows, cells), F32)

    def first(part, table=None):
        inputs = [(info, SMEM), *[(x, HBM) for x in winds]]
        outputs = [(grid_shape, VMEM), (coef_shape, VMEM)]
        scratch = [buffer] * 3 + [pltpu.SemaphoreType.DMA((3, steps))]
        if table is None:
            inputs += [(jnp.asarray(x), HBM) for x in tables]
            outputs += [(shape(*table_shape, dtype=BF16), VMEM), (shape(*back_shape, dtype=BF16), VMEM)]
            scratch += [pltpu.SemaphoreType.DMA((2,))]
        else:
            inputs += [(table, VMEM)]
        return call(functools.partial(first_kernel, part * SUB, table is None), inputs, outputs, scratch, 24)

    def join(part, moved, coef, table):
        at = slice(part * SUB, (part + 1) * SUB)
        return call(
            functools.partial(join_kernel, cells),
            [(info, SMEM), (cut, SMEM), (coef, VMEM), (own[:, at], VMEM), (got0[:, at], VMEM), (got1[:, at], VMEM),
             (table, VMEM), (moved, VMEM)],
            [(grid_shape, VMEM), (shape(4, SUB, width), VMEM), (shape(2, SUB, width), VMEM),
             (shape(2, SUB, KMAX), VMEM), (shape(2 * rows + 4, SUB, KMAX), VMEM)],
            [pltpu.VMEM(coef_shape.shape, F32)],
            12,
            {7: 0},
        )

    moved, coef, table, back = first(0)

    def rest(limit, moved, coef, table, back):
        joined = [join(0, moved, coef, table)]
        sums = [sum_over_lon(joined[0][4][: limit + 4], True)]
        for part in range(1, parts):
            joined.append(join(part, *first(part, table), table))
            sums.append(sum_over_lon(joined[part][4][: limit + 4], part % 2 == 0))
        fixes = lon_edges([x[0] for x in joined] + [x[1][2:] for x in joined], cells)
        seconds = []
        for part in range(parts):
            grid, flow, edge_v, edge_cut, _ = joined[part]
            seconds.append(call(
                functools.partial(second_kernel, part * SUB, total, cells),
                [(cut, SMEM),
                 *[(x, VMEM) for x in (*sums[part], flow, edge_v, edge_cut, fixes[parts + part], grid, fixes[part],
                                       mask, table, back)],
                 (zonal, HBM), (meridional, HBM)],
                [(grid_shape, VMEM), (shape(2 * rows, SUB, KMAX), VMEM)],
                [pltpu.VMEM(coef_shape.shape, F32), pltpu.VMEM(coef_shape.shape, F32),
                 pltpu.VMEM((2, SUB, width), F32), pltpu.VMEM((2 * SUB, 2 * KMAX), F32), buffer, buffer,
                 pltpu.SemaphoreType.DMA((2, steps))],
                24,
            ))
        sums = [sum_over_lon(x[1][:limit], part % 2 == 0) for part, x in enumerate(seconds)]
        fixes = lon_edges([x[0] for x in seconds], cells)
        out = []
        for part in range(parts):
            out = call(
                functools.partial(third_kernel, part * SUB, total, cells),
                [(cut, SMEM), *[(x, VMEM) for x in (*sums[part], seconds[part][0], fixes[part], mask, back)],
                 *[(x, HBM) for x in out]],
                [(shape(*tracer.shape), HBM)],
                [pltpu.VMEM(coef_shape.shape, F32), buffer, pltpu.SemaphoreType.DMA((steps,))],
                16,
                {7: 0} if part else None,
            )
        return out[0]

    limits = sorted({min(-(-x * rows // 64), 2 * rows) for x in LIMITS})
    choice = sum((kept > x).astype(jnp.int32) for x in limits[:-1])
    return lax.switch(choice, [functools.partial(rest, x) for x in limits], moved, coef, table, back)


def solution(mesh):
    placed = (
        P(None, "lat", "lon"),
        P(None, "lat", "lon"),
        P(None, "lat", "lon"),
        P("lat"),
        P("lat"),
    )
    return jax.shard_map(
        on_device, mesh=mesh, in_specs=placed, out_specs=P(None, "lat", "lon"), check_vma=False
    )
```

```python
import functools

import jax
import jax.numpy as jnp
import ml_dtypes
import numpy as np
from jax import lax
from jax.experimental import pallas as pl
from jax.experimental.pallas import tpu as pltpu
from jax.sharding import PartitionSpec as P

KMAX = 128
HALF = KMAX // 2
DIFFUSION = 0.1
GROUP = 4
SUB = 8
VMEM_MIB = 48
LIMITS = (48, 68, 92, 128)
F32 = jnp.float32
BF16 = jnp.bfloat16
MIB = 1024 * 1024


def wide(cells):
    return -(-(cells + 2) // 128) * 128


def split_np(values):
    high = values.astype(ml_dtypes.bfloat16)
    low = (values - high.astype(np.float64)).astype(ml_dtypes.bfloat16)
    return high, low


@functools.lru_cache(maxsize=None)
def wave_tables(cells, ways):
    total = cells * ways
    width = wide(cells)
    lane = np.arange(width)
    start = np.arange(ways)[:, None] * cells
    place = np.where(lane == width - 1, -1, lane)[None, :] + start
    used = (lane <= cells) | (lane == width - 1)
    column = np.arange(2 * KMAX)
    wave = column // KMAX * HALF + column % HALF
    sine = column % KMAX // HALF
    angle = (place[:, :, None] * wave[None, None, :] % total) * (2.0 * np.pi / total)
    table = np.where(sine == 1, np.sin(angle), np.cos(angle))
    project = split_np(np.where(used[None, :, None], table, 0.0))
    inside = np.where((lane < cells)[None, :, None], table, 0.0).transpose(0, 2, 1)
    rebuild = split_np(inside)
    return np.concatenate(project, axis=2), np.concatenate(rebuild, axis=1)


def split(x):
    high = x.astype(BF16)
    return high, (x - high.astype(F32)).astype(BF16)


def project(x, table):
    high, low = split(x)
    both = jnp.dot(high, table, preferred_element_type=F32)
    cross = jnp.dot(low, table[:, : 2 * KMAX], preferred_element_type=F32)
    return both[:, : 2 * KMAX] + both[:, 2 * KMAX :] + cross


def rebuild(coefficients, table):
    high, low = split(coefficients)
    both = jnp.dot(jnp.concatenate([high, high], axis=1), table, preferred_element_type=F32)
    return both + jnp.dot(low, table[: 2 * KMAX], preferred_element_type=F32)


def padded(x, width):
    return jnp.concatenate([x, jnp.zeros((x.shape[0], width - x.shape[1]), F32)], axis=1)


def along_lon(s, u):
    width = s.shape[1]
    spread = DIFFUSION * s
    carry = (0.5 * u) * s
    return (
        (1.0 - 4.0 * DIFFUSION) * s
        + pltpu.roll(spread - carry, width - 1, 1)
        + pltpu.roll(spread + carry, 1, 1)
    )


def moved_rows(s, u, v):
    rows = s.shape[0]
    spread = DIFFUSION * s
    carry = (0.5 * v) * s
    row = lax.broadcasted_iota(jnp.int32, s.shape, 0)
    from_next = jnp.where(row == rows - 1, 0.0, pltpu.roll(spread - carry, rows - 1, 0))
    from_last = jnp.where(row == 0, 0.0, pltpu.roll(spread + carry, 1, 0))
    return along_lon(s, u) + from_next + from_last


def put_halves(ref, at, value):
    for half in range(2):
        ref[half, at, :] = value[:, half * KMAX : (half + 1) * KMAX]


def both_halves(ref, at):
    return jnp.concatenate([ref[0, at, :], ref[1, at, :]], axis=1)


def southward(s, v):
    return DIFFUSION * s + (0.5 * v) * s


def northward(s, v):
    return DIFFUSION * s - (0.5 * v) * s


def filtered_column(cut_row_ref):
    rows = cut_row_ref.shape[1]
    shape_ = (rows, rows)
    diagonal = lax.broadcasted_iota(jnp.int32, shape_, 0) == lax.broadcasted_iota(jnp.int32, shape_, 1)
    spread = jnp.broadcast_to(cut_row_ref[...].astype(F32), shape_)
    return jnp.sum(jnp.where(diagonal, spread, 0.0), axis=1, keepdims=True) >= 0.0


def edge_kernel(
    info_ref, cutoff_ref, mask_ref, s0_ref, u0_ref, v0_ref, s1_ref, u1_ref, v1_ref, ring0_ref, ring1_ref, own_ref,
):
    levels, width = own_ref.shape[1:]
    rows = cutoff_ref.shape[0]
    near = info_ref[0] < info_ref[1] // 2
    last = s1_ref.shape[1] - 1
    sides = []
    for refs, at, beyond, flow, row in (
        ((s0_ref, u0_ref, v0_ref), 0, 1, northward, 0),
        ((s1_ref, u1_ref, v1_ref), last, last - 1, southward, rows - 1),
    ):
        cut = jnp.where(mask_ref[row] == 1, cutoff_ref[row], -1)
        s, u, v = (ref[:, at, :] for ref in refs)
        tail = jnp.full((levels, width - s.shape[1]), cut.astype(F32))
        parts = [padded(u, width), padded(v, width), padded(flow(refs[0][:, beyond, :], refs[2][:, beyond, :]), width)]
        sides.append([jnp.concatenate([s, tail], axis=1), *parts])
    own_ref[0] = padded(northward(s0_ref[:, 0, :], v0_ref[:, 0, :]), width)
    own_ref[1] = padded(southward(s1_ref[:, last, :], v1_ref[:, last, :]), width)
    for i in range(4):
        ring0_ref[i] = jnp.where(near, sides[1][i], sides[0][i])
        ring1_ref[i] = jnp.where(near, sides[0][i], sides[1][i])


def group_copies(hbm_refs, buffers, sem, first, i):
    return [
        pltpu.make_async_copy(h.at[pl.ds(first + i * GROUP, GROUP)], b.at[pl.ds(i * GROUP, GROUP)], sem.at[q, i])
        for q, (h, b) in enumerate(zip(hbm_refs, buffers))
    ]


def group_stores(buffer, hbm_ref, sem, first, i):
    return pltpu.make_async_copy(
        buffer.at[pl.ds(i * GROUP, GROUP)], hbm_ref.at[pl.ds(first + i * GROUP, GROUP)], sem.at[i]
    )


def outflow(x, cells):
    tile = jnp.transpose(x[:, x.shape[1] - 128 :])
    at = cells - (x.shape[1] - 128)
    return jnp.concatenate([tile[at : at + 1, :], tile[127:128, :]], axis=1)


def pack_rows(cut_ref, source_ref, first, out_ref):
    rows = cut_ref.shape[0]

    def body(r, unit):
        cut = cut_ref[r]
        for half in range(2):
            out_ref[unit + half] = source_ref[half, pl.ds(r, SUB, stride=rows), :]
        return unit + (cut >= 0).astype(jnp.int32) + (cut >= HALF).astype(jnp.int32)

    lax.fori_loop(0, rows, body, first, unroll=8)


def scaled(x, half, cut, total):
    lane = lax.broadcasted_iota(jnp.int32, (SUB, KMAX), 1)
    wave = half * HALF + lane % HALF
    scale = jnp.where(wave == 0, 1.0 / total, 2.0 / total)
    return jnp.where(wave <= cut, x * scale, 0.0)


def unpack_rows(cut_ref, a_ref, b_ref, first, total, out_ref):
    rows = cut_ref.shape[0]
    last = a_ref.shape[0] - 1

    def body(r, unit):
        cut = cut_ref[r]
        for half in range(2):
            at = jnp.minimum(unit + half, last)
            out_ref[half, pl.ds(r, SUB, stride=rows), :] = scaled(a_ref[at] + b_ref[at], half, cut, total)
        return unit + (cut >= 0).astype(jnp.int32) + (cut >= HALF).astype(jnp.int32)

    lax.fori_loop(0, rows, body, first, unroll=8)


def put_slots(out_ref, first, ways, lon, value):
    for i in range(ways):
        out_ref[first + i] = jnp.zeros(value.shape, F32)
    out_ref[first + lon] = value


def inflow(a_ref, b_ref, first, ways, lon, rows, place):
    west, east = first + lax.rem(lon + ways - 1, ways), first + lax.rem(lon + 1, ways)
    place[0:SUB, :] = a_ref[west] + b_ref[west]
    west_columns = jnp.transpose(place[...])[:rows, :]
    place[0:SUB, :] = a_ref[east] + b_ref[east]
    east_columns = jnp.transpose(place[...])[rows : 2 * rows, :]
    return west_columns, east_columns


def first_body(first, cells, hbm_refs, buffers, sem, moved_ref, hbm_moved_ref, out_sem, coef_ref, edge_ref, table_ref, ready):
    levels, rows, width = moved_ref.shape
    for i in range(levels // GROUP):
        for copy in group_copies(hbm_refs, buffers, sem, first, i):
            copy.wait()
        for g in range(GROUP):
            level = i * GROUP + g
            x = moved_rows(*[padded(b[level], width) for b in buffers])
            moved_ref[level] = x
            edge_ref[level : level + 1, :] = outflow(x, cells)
        group_stores(moved_ref, hbm_moved_ref, out_sem, 0, i).start()
        if i == 0:
            ready.wait()
        x = moved_ref[i * GROUP : (i + 1) * GROUP].reshape(GROUP * rows, width)
        put_halves(coef_ref, slice(i * GROUP * rows, (i + 1) * GROUP * rows), project(x, table_ref[...]))


def first_kernel(
    first, cells, info_ref, s_ref, u_ref, v_ref, tables_ref, hbm_moved_ref, coef_ref, edge_ref,
    s_buf, u_buf, v_buf, moved_ref, table_ref, sem, out_sem, table_sem,
):
    hbm_refs, buffers = (s_ref, u_ref, v_ref), (s_buf, u_buf, v_buf)
    steps = moved_ref.shape[0] // GROUP
    ready = pltpu.make_async_copy(tables_ref.at[info_ref[0]], table_ref, table_sem)
    for i in range(steps):
        for copy in group_copies(hbm_refs, buffers, sem, first, i):
            copy.start()
        if i == 0:
            ready.start()
    first_body(first, cells, hbm_refs, buffers, sem, moved_ref, hbm_moved_ref, out_sem, coef_ref, edge_ref, table_ref, ready)
    for i in range(steps):
        group_stores(moved_ref, hbm_moved_ref, out_sem, 0, i).wait()


def join_flows(first, cells, info_ref, own_ref, ring0_ref, ring1_ref, flow_ref, edge_v_ref, edge_cut_ref):
    levels, width = flow_ref.shape[1:]
    at = slice(first, first + levels)
    near = info_ref[0] < info_ref[1] // 2
    lane = lax.broadcasted_iota(jnp.int32, (levels, width), 1)
    for side in range(2):
        got = [jnp.where(near == (side == 0), ring0_ref[i, at, :], ring1_ref[i, at, :]) for i in range(4)]
        edge_cut_ref[side] = jnp.broadcast_to(got[0][:, cells : cells + 1], (levels, KMAX))
        s = jnp.where(lane < cells, got[0], 0.0)
        pole = info_ref[2] == (0 if side == 0 else info_ref[3] - 1)
        v = jnp.where(pole, -got[2], got[2])
        edge_v_ref[side] = v
        flow_ref[side] = southward(s, v) if side == 0 else northward(s, v)
        flow_ref[2 + side] = along_lon(s, got[1]) + got[3] + own_ref[side, at, :]


def join_body(cells, info_ref, cut_ref, ways, coef_ref, edge_ref, flow_ref, table_ref, out_ref):
    rows = cut_ref.shape[0]
    levels, width = flow_ref.shape[1:]
    lon = info_ref[0]
    extra = project(flow_ref[...].reshape(4 * levels, width), table_ref[...])
    first = pl.ds(0, SUB, stride=rows)
    last = pl.ds(rows - 1, SUB, stride=rows)
    for half in range(2):
        part = extra[:, half * KMAX : (half + 1) * KMAX]
        coef_ref[half, first, :] = coef_ref[half, first, :] + part[:levels]
        coef_ref[half, last, :] = coef_ref[half, last, :] + part[levels : 2 * levels]
        out_ref[half] = part[2 * levels : 3 * levels]
        out_ref[2 + half] = part[3 * levels :]
    put_slots(out_ref, 4, ways, lon, edge_ref[...])
    lane = lax.broadcasted_iota(jnp.int32, (SUB, KMAX), 1)
    unit = jnp.zeros((SUB, KMAX), F32)
    for side in range(2):
        for way, at in enumerate((cells, width - 1)):
            unit = jnp.where(lane == 4 * lon + 2 * side + way, flow_ref[2 + side][:, at : at + 1], unit)
    out_ref[4 + ways] = unit
    pack_rows(cut_ref, coef_ref, 5 + ways, out_ref)


def join_kernel(
    first, cells, ways,
    info_ref, cut_ref, coef_in_ref, edge_ref, own_ref, ring0_ref, ring1_ref, tables_ref,
    flow_ref, edge_v_ref, edge_cut_ref, out_ref, coef_ref, table_ref, table_sem,
):
    ready = pltpu.make_async_copy(tables_ref.at[info_ref[0]], table_ref, table_sem)
    ready.start()
    coef_ref[...] = coef_in_ref[...]
    join_flows(first, cells, info_ref, own_ref, ring0_ref, ring1_ref, flow_ref, edge_v_ref, edge_cut_ref)
    ready.wait()
    join_body(cells, info_ref, cut_ref, ways, coef_ref, edge_ref, flow_ref, table_ref, out_ref)


def first_join_kernel(
    first, cells, ways,
    info_ref, cut_ref, s_ref, u_ref, v_ref, own_ref, ring0_ref, ring1_ref, tables_ref,
    hbm_moved_ref, flow_ref, edge_v_ref, edge_cut_ref, out_ref,
    s_buf, u_buf, v_buf, moved_ref, table_ref, coef_ref, edge_ref, sem, out_sem, table_sem,
):
    hbm_refs, buffers = (s_ref, u_ref, v_ref), (s_buf, u_buf, v_buf)
    steps = moved_ref.shape[0] // GROUP
    ready = pltpu.make_async_copy(tables_ref.at[info_ref[0]], table_ref, table_sem)
    for i in range(steps):
        for copy in group_copies(hbm_refs, buffers, sem, first, i):
            copy.start()
        if i == 0:
            ready.start()
    join_flows(first, cells, info_ref, own_ref, ring0_ref, ring1_ref, flow_ref, edge_v_ref, edge_cut_ref)
    first_body(first, cells, hbm_refs, buffers, sem, moved_ref, hbm_moved_ref, out_sem, coef_ref, edge_ref, table_ref, ready)
    join_body(cells, info_ref, cut_ref, ways, coef_ref, edge_ref, flow_ref, table_ref, out_ref)
    for i in range(steps):
        group_stores(moved_ref, hbm_moved_ref, out_sem, 0, i).wait()


def closed(x, west, east, cells):
    end = x.shape[1] - 128
    lane = lax.broadcasted_iota(jnp.int32, (x.shape[0], 128), 1)
    head = x[:, :128] + jnp.where(lane == 0, west, 0.0)
    tail = x[:, end:] + jnp.where(lane == cells - 1 - end, east, 0.0)
    return jnp.concatenate([head, x[:, 128:end], jnp.where(lane < cells - end, tail, 0.0)], axis=1)


def second_kernel(
    first, total, cells, ways,
    info_ref, cut_ref, cut_row_ref, a_ref, b_ref, flow_ref, edge_v_ref, edge_cut_ref,
    hbm_in_ref, tables_ref, backs_ref, u_ref, v_ref,
    hbm_out_ref, pay_ref,
    moved_buf, out_ref, coef_ref, sum_ref, step_ref, edge_ref, place_ref, u_buf, v_buf, table_ref, back_ref,
    sem, in_sem, out_sem, table_sem,
):
    rows = cut_ref.shape[0]
    levels, _, width = out_ref.shape
    steps = levels // GROUP
    lon = info_ref[0]
    loads = [
        pltpu.make_async_copy(backs_ref.at[lon], back_ref, table_sem.at[0]),
        pltpu.make_async_copy(tables_ref.at[lon], table_ref, table_sem.at[1]),
    ]
    loads[0].start()
    for i in range(steps):
        for copy in group_copies((hbm_in_ref,), (moved_buf,), in_sem, 0, i):
            copy.start()
        for copy in group_copies((u_ref, v_ref), (u_buf, v_buf), sem, first, i):
            copy.start()
        if i == 0:
            loads[1].start()
    place_ref[...] = jnp.zeros_like(place_ref)
    unpack_rows(cut_ref, a_ref, b_ref, 5 + ways, total, coef_ref)
    for side in range(2):
        for half in range(2):
            at = 2 * side + half
            cut = edge_cut_ref[side].astype(jnp.int32)
            edge_ref[side * levels : (side + 1) * levels, half * KMAX : (half + 1) * KMAX] = scaled(
                a_ref[at] + b_ref[at], half, cut, total
            )
    west, east = inflow(a_ref, b_ref, 4, ways, lon, rows, place_ref)
    unit = a_ref[4 + ways] + b_ref[4 + ways]
    lane = lax.broadcasted_iota(jnp.int32, (SUB, KMAX), 1)
    loads[0].wait()
    smooth = rebuild(edge_ref[...], back_ref[...])
    for side in range(2):
        came = [
            jnp.sum(jnp.where(lane == 4 * lax.rem(lon + ways + step, ways) + 2 * side + way, unit, 0.0), axis=1, keepdims=True)
            for way, step in enumerate((-1, 1))
        ]
        plain = closed(flow_ref[2 + side], came[0], came[1], cells)
        filtered = edge_cut_ref[side][:, 0:1] >= 0.0
        s = jnp.where(filtered, smooth[side * levels : (side + 1) * levels], plain)
        step_ref[side] = (southward if side == 0 else northward)(s, edge_v_ref[side])
    filtered = filtered_column(cut_row_ref)
    for i in range(steps):
        smooth = rebuild(both_halves(coef_ref, slice(i * GROUP * rows, (i + 1) * GROUP * rows)), back_ref[...])
        for copy in group_copies((u_ref, v_ref), (u_buf, v_buf), sem, first, i):
            copy.wait()
        group_copies((hbm_in_ref,), (moved_buf,), in_sem, 0, i)[0].wait()
        for g in range(GROUP):
            level = i * GROUP + g
            row = slice(level, level + 1)
            moved_buf[level, 0:1, :] = moved_buf[level, 0:1, :] + flow_ref[0, row, :]
            moved_buf[level, rows - 1 : rows, :] = moved_buf[level, rows - 1 : rows, :] + flow_ref[1, row, :]
            plain = closed(moved_buf[level], west[:, row], east[:, row], cells)
            s = jnp.where(filtered, smooth[g * rows : (g + 1) * rows], plain)
            out_ref[level] = moved_rows(s, padded(u_buf[level], width), padded(v_buf[level], width))
            out_ref[level, 0:1, :] = out_ref[level, 0:1, :] + step_ref[0, row, :]
            out_ref[level, rows - 1 : rows, :] = out_ref[level, rows - 1 : rows, :] + step_ref[1, row, :]
            place_ref[row, :] = outflow(out_ref[level], cells)
        group_stores(out_ref, hbm_out_ref, out_sem, 0, i).start()
        if i == 0:
            loads[1].wait()
        x = out_ref[i * GROUP : (i + 1) * GROUP].reshape(GROUP * rows, width)
        put_halves(sum_ref, slice(i * GROUP * rows, (i + 1) * GROUP * rows), project(x, table_ref[...]))
    put_slots(pay_ref, 0, ways, lon, place_ref[0:SUB, :])
    pack_rows(cut_ref, sum_ref, ways, pay_ref)
    for i in range(steps):
        group_stores(out_ref, hbm_out_ref, out_sem, 0, i).wait()


def third_kernel(
    first, total, cells, ways, info_ref, cut_ref, cut_row_ref, a_ref, b_ref, hbm_in_ref, backs_ref, *refs
):
    out_ref, coef_ref, place_ref, moved_buf, buffer, back_ref, in_sem, out_sem, table_sem = refs[-9:]
    rows = cut_ref.shape[0]
    levels = moved_buf.shape[0]
    steps = levels // GROUP
    lon = info_ref[0]
    ready = pltpu.make_async_copy(backs_ref.at[lon], back_ref, table_sem)
    ready.start()
    for i in range(steps):
        group_copies((hbm_in_ref,), (moved_buf,), in_sem, 0, i)[0].start()
    place_ref[...] = jnp.zeros_like(place_ref)
    unpack_rows(cut_ref, a_ref, b_ref, ways, total, coef_ref)
    west, east = inflow(a_ref, b_ref, 0, ways, lon, rows, place_ref)
    filtered = filtered_column(cut_row_ref)
    ready.wait()
    for i in range(steps):
        smooth = rebuild(both_halves(coef_ref, slice(i * GROUP * rows, (i + 1) * GROUP * rows)), back_ref[...])
        group_copies((hbm_in_ref,), (moved_buf,), in_sem, 0, i)[0].wait()
        for g in range(GROUP):
            level = i * GROUP + g
            row = slice(level, level + 1)
            plain = closed(moved_buf[level], west[:, row], east[:, row], cells)
            buffer[level] = jnp.where(filtered, smooth[g * rows : (g + 1) * rows], plain)[:, :cells]
        group_stores(buffer, out_ref, out_sem, first, i).start()
    for i in range(steps):
        group_stores(buffer, out_ref, out_sem, first, i).wait()


SMEM = pl.BlockSpec(memory_space=pltpu.SMEM)
VMEM = pl.BlockSpec(memory_space=pltpu.VMEM)
HBM = pl.BlockSpec(memory_space=pltpu.HBM)


def shape(*dims, dtype=F32):
    return jax.ShapeDtypeStruct(dims, dtype)


def call(kernel, inputs, outputs, scratch, mib, aliases=None):
    return pl.pallas_call(
        kernel,
        in_specs=[spec for _, spec in inputs],
        out_specs=[spec for _, spec in outputs],
        out_shape=[what for what, _ in outputs],
        scratch_shapes=scratch,
        input_output_aliases=aliases or {},
        compiler_params=pltpu.CompilerParams(vmem_limit_bytes=mib * MIB),
    )(*[array for array, _ in inputs])


def swap(x, bit):
    count = lax.axis_size("lon")
    return lax.ppermute(x, "lon", [(i, i ^ (1 << bit)) for i in range(count)])


def sum_over_lon(x, upward):
    bits = lax.axis_size("lon").bit_length() - 1
    for i in range(bits):
        got = swap(x, i if upward else bits - 1 - i)
        if i == bits - 1:
            return x, got
        x = x + got


def lat_ring(bands, ways, turn):
    pairs = []
    for band in range(bands):
        for l in range(ways):
            east = l < ways // 2
            other = (l + ways // 2) % ways
            step = 1 if east == (turn == 0) else -1
            to = (band + step, l) if 0 <= band + step < bands else (band, other)
            pairs.append((l * bands + band, to[1] * bands + to[0]))
    return pairs


def on_device(tracer, zonal, meridional, cutoff_wave, polar_mask):
    levels, rows, cells = tracer.shape
    ways, bands = lax.axis_size("lon"), lax.axis_size("lat")
    width = wide(cells)
    total = cells * ways
    tables, backs = (jnp.asarray(x) for x in wave_tables(cells, ways))
    lon, band = lax.axis_index("lon"), lax.axis_index("lat")
    info = jnp.stack([lon, jnp.int32(ways), band, jnp.int32(bands)]).astype(jnp.int32)
    parts = levels // SUB
    steps = SUB // GROUP
    winds = (tracer, zonal, meridional)

    top = pl.BlockSpec((levels, SUB, cells), lambda i: (0, 0, 0))
    bottom = pl.BlockSpec((levels, SUB, cells), lambda i: (0, rows // SUB - 1, 0))
    full = pl.BlockSpec((4, levels, width), lambda i: (0, 0, 0))
    ring0, ring1, own = pl.pallas_call(
        edge_kernel,
        grid=(1,),
        in_specs=[SMEM, SMEM, SMEM, top, top, top, bottom, bottom, bottom],
        out_specs=[full, full, pl.BlockSpec((2, levels, width), lambda i: (0, 0, 0))],
        out_shape=[shape(4, levels, width), shape(4, levels, width), shape(2, levels, width)],
        compiler_params=pltpu.CompilerParams(vmem_limit_bytes=VMEM_MIB * MIB),
    )(info, cutoff_wave, polar_mask, *winds, *winds)
    ring = ("lon", "lat")
    got0 = lax.ppermute(ring0, ring, lat_ring(bands, ways, 0))
    got1 = lax.ppermute(ring1, ring, lat_ring(bands, ways, 1))
    cut = jnp.where(polar_mask == 1, cutoff_wave, -1)
    kept = jnp.sum((cut >= 0).astype(jnp.int32) + (cut >= HALF).astype(jnp.int32))
    cut_row = cut[None, :]

    grid = shape(SUB, rows, width)
    coef = shape(2, SUB * rows, KMAX)
    edge = shape(SUB, KMAX)
    flows = [(shape(4, SUB, width), VMEM), (shape(2, SUB, width), VMEM), (shape(2, SUB, KMAX), VMEM)]
    head = 5 + ways

    def room(what):
        return pltpu.VMEM(what.shape, what.dtype)

    buffer = pltpu.VMEM((SUB, rows, cells), F32)
    table, back = room(shape(*tables.shape[1:], dtype=BF16)), room(shape(*backs.shape[1:], dtype=BF16))
    sems = pltpu.SemaphoreType.DMA
    first_scratch = [buffer, buffer, buffer, room(grid), table]
    moved_a, coef_a, edge_a = call(
        functools.partial(first_kernel, 0, cells),
        [(info, SMEM), *[(x, HBM) for x in winds], (tables, HBM)],
        [(grid, HBM), (coef, VMEM), (edge, VMEM)],
        [*first_scratch, sems((3, steps)), sems((steps,)), sems(())],
        VMEM_MIB,
    )

    def rest(limit, info, cut, cut_row, tracer, zonal, meridional, own, got0, got1, moved_a, coef_a, edge_a):
        pay = (shape(limit + head + 2, SUB, KMAX), VMEM)
        around = [(x, VMEM) for x in (own, got0, got1)]
        scalars = [(info, SMEM), (cut, SMEM)]
        joined = [(moved_a, *call(
            functools.partial(join_kernel, 0, cells, ways),
            [*scalars, (coef_a, VMEM), (edge_a, VMEM), *around, (tables, HBM)],
            [*flows, pay],
            [room(coef), table, sems(())],
            VMEM_MIB,
        ))]
        sums = [sum_over_lon(joined[0][4], True)]
        for part in range(1, parts):
            joined.append(call(
                functools.partial(first_join_kernel, part * SUB, cells, ways),
                [*scalars, *[(x, HBM) for x in (tracer, zonal, meridional)], *around, (tables, HBM)],
                [(grid, HBM), *flows, pay],
                [*first_scratch, room(coef), room(edge), sems((3, steps)), sems((steps,)), sems(())],
                VMEM_MIB,
            ))
            sums.append(sum_over_lon(joined[part][4], part % 2 == 0))
        seconds = []
        for part in range(parts):
            moved, flow, edge_v, edge_cut, _ = joined[part]
            seconds.append(call(
                functools.partial(second_kernel, part * SUB, total, cells, ways),
                [*scalars, *[(x, VMEM) for x in (cut_row, *sums[part], flow, edge_v, edge_cut)],
                 *[(x, HBM) for x in (moved, tables, backs, zonal, meridional)]],
                [(grid, HBM), (shape(limit + ways + 2, SUB, KMAX), VMEM)],
                [room(grid), room(grid), room(coef), room(coef), pltpu.VMEM((2, SUB, width), F32),
                 pltpu.VMEM((2 * SUB, 2 * KMAX), F32), pltpu.VMEM((KMAX, KMAX), F32), buffer, buffer, table, back,
                 sems((2, steps)), sems((1, steps)), sems((steps,)), sems((2,))],
                VMEM_MIB,
            ))
        sums = [sum_over_lon(x[1], part % 2 == 0) for part, x in enumerate(seconds)]
        out = []
        for part in range(parts):
            out = call(
                functools.partial(third_kernel, part * SUB, total, cells, ways),
                [*scalars, *[(x, VMEM) for x in (cut_row, *sums[part])],
                 *[(x, HBM) for x in (seconds[part][0], backs, *out)]],
                [(shape(levels, rows, cells), HBM)],
                [room(coef), pltpu.VMEM((KMAX, KMAX), F32), room(grid), buffer, back,
                 sems((1, steps)), sems((steps,)), sems(())],
                VMEM_MIB,
                {7: 0} if part else None,
            )
        return out[0]

    limits = sorted({min(-(-x * rows // 64), 2 * rows) for x in LIMITS})
    choice = sum((kept > x).astype(jnp.int32) for x in limits[:-1])
    return lax.switch(
        choice, [functools.partial(rest, x) for x in limits],
        info, cut, cut_row, tracer, zonal, meridional, own, got0, got1, moved_a, coef_a, edge_a,
    )


def solution(mesh):
    placed = (
        P(None, "lat", "lon"),
        P(None, "lat", "lon"),
        P(None, "lat", "lon"),
        P("lat"),
        P("lat"),
    )
    return jax.shard_map(
        on_device, mesh=mesh, in_specs=placed, out_specs=P(None, "lat", "lon"), check_vma=False
    )
```

```python
import functools

import jax
import jax.numpy as jnp
import ml_dtypes
import numpy as np
from jax import lax
from jax.experimental import pallas as pl
from jax.experimental.pallas import tpu as pltpu
from jax.sharding import PartitionSpec as P

KMAX = 128
HALF = KMAX // 2
DIFFUSION = 0.1
GROUP = 4
SUB = 8
FIRST_MIB = 52
LIMITS = (92, 128)
F32 = jnp.float32
BF16 = jnp.bfloat16
MIB = 1024 * 1024


def wide(cells):
    return -(-(cells + 2) // 128) * 128


def split_np(values):
    high = values.astype(ml_dtypes.bfloat16)
    low = (values - high.astype(np.float64)).astype(ml_dtypes.bfloat16)
    return high, low


@functools.lru_cache(maxsize=None)
def wave_tables(cells, ways):
    total = cells * ways
    width = wide(cells)
    lane = np.arange(width)
    start = np.arange(ways)[:, None] * cells
    place = np.where(lane == width - 1, -1, lane)[None, :] + start
    used = (lane <= cells) | (lane == width - 1)
    column = np.arange(2 * KMAX)
    wave = column // KMAX * HALF + column % HALF
    sine = column % KMAX // HALF
    angle = (place[:, :, None] * wave[None, None, :] % total) * (2.0 * np.pi / total)
    table = np.where(sine == 1, np.sin(angle), np.cos(angle))
    project = split_np(np.where(used[None, :, None], table, 0.0))
    inside = np.where((lane < cells)[None, :, None], table, 0.0).transpose(0, 2, 1)
    rebuild = split_np(inside)
    return np.concatenate(project, axis=2), np.concatenate(rebuild, axis=1)


def split(x):
    high = x.astype(BF16)
    return high, (x - high.astype(F32)).astype(BF16)


def project(x, table):
    high, low = split(x)
    both = jnp.dot(high, table, preferred_element_type=F32)
    cross = jnp.dot(low, table[:, : 2 * KMAX], preferred_element_type=F32)
    return both[:, : 2 * KMAX] + both[:, 2 * KMAX :] + cross


def rebuild(coefficients, table):
    high, low = split(coefficients)
    both = jnp.dot(jnp.concatenate([high, high], axis=1), table, preferred_element_type=F32)
    return both + jnp.dot(low, table[: 2 * KMAX], preferred_element_type=F32)


def padded(x, width):
    return jnp.concatenate([x, jnp.zeros((x.shape[0], width - x.shape[1]), F32)], axis=1)


def along_lon(s, u):
    width = s.shape[1]
    spread = DIFFUSION * s
    carry = (0.5 * u) * s
    return (
        (1.0 - 4.0 * DIFFUSION) * s
        + pltpu.roll(spread - carry, width - 1, 1)
        + pltpu.roll(spread + carry, 1, 1)
    )


def moved_rows(s, u, v):
    rows = s.shape[0]
    spread = DIFFUSION * s
    carry = (0.5 * v) * s
    row = lax.broadcasted_iota(jnp.int32, s.shape, 0)
    from_next = jnp.where(row == rows - 1, 0.0, pltpu.roll(spread - carry, rows - 1, 0))
    from_last = jnp.where(row == 0, 0.0, pltpu.roll(spread + carry, 1, 0))
    return along_lon(s, u) + from_next + from_last


def put_halves(ref, at, value):
    for half in range(2):
        ref[half, at, :] = value[:, half * KMAX : (half + 1) * KMAX]


def both_halves(ref, at):
    return jnp.concatenate([ref[0, at, :], ref[1, at, :]], axis=1)


def southward(s, v):
    return DIFFUSION * s + (0.5 * v) * s


def northward(s, v):
    return DIFFUSION * s - (0.5 * v) * s


def edge_kernel(
    info_ref, cut_row_ref, s0_ref, u0_ref, v0_ref, s1_ref, u1_ref, v1_ref, ring0_ref, ring1_ref, own_ref,
):
    levels, width = own_ref.shape[1:]
    rows = cut_row_ref.shape[1]
    near = info_ref[0] < info_ref[1] // 2
    last = s1_ref.shape[1] - 1
    sides = []
    for refs, at, beyond, flow, row in (
        ((s0_ref, u0_ref, v0_ref), 0, 1, northward, 0),
        ((s1_ref, u1_ref, v1_ref), last, last - 1, southward, rows - 1),
    ):
        cut = cut_row_ref[:, row : row + 1]
        s, u, v = (ref[:, at, :] for ref in refs)
        tail = jnp.broadcast_to(cut.astype(F32), (levels, width - s.shape[1]))
        parts = [padded(u, width), padded(v, width), padded(flow(refs[0][:, beyond, :], refs[2][:, beyond, :]), width)]
        sides.append([jnp.concatenate([s, tail], axis=1), *parts])
    own_ref[0] = padded(northward(s0_ref[:, 0, :], v0_ref[:, 0, :]), width)
    own_ref[1] = padded(southward(s1_ref[:, last, :], v1_ref[:, last, :]), width)
    for i in range(4):
        ring0_ref[i] = jnp.where(near, sides[1][i], sides[0][i])
        ring1_ref[i] = jnp.where(near, sides[0][i], sides[1][i])


def level_copies(hbm_refs, buffers, sem, first, level):
    return [
        pltpu.make_async_copy(h.at[first + level], b.at[level], sem.at[q, level])
        for q, (h, b) in enumerate(zip(hbm_refs, buffers))
    ]


def every(copies, act):
    for copy in copies:
        getattr(copy, act)()


def group_store(buffer, hbm_ref, sem, first, i):
    return pltpu.make_async_copy(
        buffer.at[pl.ds(i * GROUP, GROUP)], hbm_ref.at[pl.ds(first + i * GROUP, GROUP)], sem.at[i]
    )


def is_diagonal(rows, lanes):
    lane = lax.broadcasted_iota(jnp.int32, (rows, lanes), 1)
    return lax.broadcasted_iota(jnp.int32, (rows, lanes), 0) == lax.rem(lane, rows)


def outflow(tile, cells, width):
    rows = tile.shape[0]
    at = cells - (width - 128)
    lane = lax.broadcasted_iota(jnp.int32, tile.shape, 1)
    both = jnp.where(lane < rows, tile[:, at : at + 1], tile[:, 127:128])
    return jnp.sum(jnp.where(is_diagonal(*tile.shape), both, 0.0), axis=0, keepdims=True)


def column(row):
    rows = row.shape[1]
    spread = jnp.broadcast_to(row, (rows, rows))
    return jnp.sum(jnp.where(is_diagonal(rows, rows), spread, 0.0), axis=1, keepdims=True)


def pack_rows(cut_ref, source_ref, first, out_ref):
    rows = cut_ref.shape[0]

    def body(r, unit):
        cut = cut_ref[r]
        for half in range(2):
            out_ref[unit + half] = source_ref[half, pl.ds(r, SUB, stride=rows), :]
        return unit + (cut >= 0).astype(jnp.int32) + (cut >= HALF).astype(jnp.int32)

    lax.fori_loop(0, rows, body, first, unroll=8)


def scaled(x, half, cut, total):
    lane = lax.broadcasted_iota(jnp.int32, (SUB, KMAX), 1)
    wave = half * HALF + lane % HALF
    scale = jnp.where(wave == 0, 1.0 / total, 2.0 / total)
    return jnp.where(wave <= cut, x * scale, 0.0)


def unpack_rows(cut_ref, a_ref, b_ref, first, total, out_ref):
    rows = cut_ref.shape[0]
    last = a_ref.shape[0] - 1

    def body(r, unit):
        cut = cut_ref[r]
        for half in range(2):
            at = jnp.minimum(unit + half, last)
            out_ref[half, pl.ds(r, SUB, stride=rows), :] = scaled(a_ref[at] + b_ref[at], half, cut, total)
        return unit + (cut >= 0).astype(jnp.int32) + (cut >= HALF).astype(jnp.int32)

    lax.fori_loop(0, rows, body, first, unroll=8)


def put_slots(out_ref, first, ways, lon, value):
    for i in range(ways):
        out_ref[first + i] = jnp.zeros(value.shape, F32)
    out_ref[first + lon] = value


def inflow(a_ref, b_ref, first, ways, lon, rows, place_ref):
    west, east = first + lax.rem(lon + ways - 1, ways), first + lax.rem(lon + 1, ways)
    lane = lax.broadcasted_iota(jnp.int32, (SUB, 2 * rows), 1)
    place_ref[...] = jnp.where(lane < rows, a_ref[west] + b_ref[west], a_ref[east] + b_ref[east])


def loop(count, body):
    def step(i, _):
        body(i)
        return 0

    lax.fori_loop(0, count, step, 0)


def project_groups(x_ref, table_ref, coef_ref):
    levels, rows, width = x_ref.shape

    def body(i):
        x = x_ref[pl.ds(i * GROUP, GROUP)].reshape(GROUP * rows, width)
        put_halves(coef_ref, pl.ds(i * GROUP * rows, GROUP * rows), project(x, table_ref[...]))

    loop(levels // GROUP, body)


def first_body(first, cells, hbm_refs, buffers, sem, moved_ref, coef_ref, edge_ref, table_ref, ready=None):
    levels, rows, width = moved_ref.shape

    def one(level):
        every(level_copies(hbm_refs, buffers, sem, first, level), "wait")
        moved_ref[level] = moved_rows(*[padded(b[level], width) for b in buffers])
        edge_ref[pl.ds(level, 1), :] = outflow(moved_ref[level, :, width - 128 :], cells, width)

    loop(levels, one)
    if ready is not None:
        ready.wait()
    project_groups(moved_ref, table_ref, coef_ref)


def first_kernel(
    first, cells, info_ref, s_ref, u_ref, v_ref, tables_ref, backs_ref,
    moved_ref, coef_ref, edge_ref, table_ref, back_ref, s_buf, u_buf, v_buf, sem, table_sem,
):
    hbm_refs, buffers = (s_ref, u_ref, v_ref), (s_buf, u_buf, v_buf)
    lon = info_ref[0]
    ready = pltpu.make_async_copy(tables_ref.at[lon], table_ref, table_sem.at[0])
    later = pltpu.make_async_copy(backs_ref.at[lon], back_ref, table_sem.at[1])
    loop(SUB, lambda level: every(level_copies(hbm_refs, buffers, sem, first, level), "start"))
    ready.start()
    later.start()
    first_body(first, cells, hbm_refs, buffers, sem, moved_ref, coef_ref, edge_ref, table_ref, ready)
    later.wait()


def join_flows(first, cells, info_ref, own_ref, ring0_ref, ring1_ref, flow_ref, edge_v_ref, edge_cut_ref):
    levels, width = flow_ref.shape[1:]
    at = slice(first, first + levels)
    near = info_ref[0] < info_ref[1] // 2
    lane = lax.broadcasted_iota(jnp.int32, (levels, width), 1)
    for side in range(2):
        got = [jnp.where(near == (side == 0), ring0_ref[i, at, :], ring1_ref[i, at, :]) for i in range(4)]
        edge_cut_ref[side] = jnp.broadcast_to(got[0][:, cells : cells + 1], (levels, KMAX))
        s = jnp.where(lane < cells, got[0], 0.0)
        pole = info_ref[2] == (0 if side == 0 else info_ref[3] - 1)
        v = jnp.where(pole, -got[2], got[2])
        edge_v_ref[side] = v
        flow_ref[side] = southward(s, v) if side == 0 else northward(s, v)
        flow_ref[2 + side] = along_lon(s, got[1]) + got[3] + own_ref[side, at, :]


def join_body(cells, info_ref, cut_ref, ways, coef_ref, edge_ref, flow_ref, table_ref, out_ref):
    rows = cut_ref.shape[0]
    levels, width = flow_ref.shape[1:]
    lon = info_ref[0]
    extra = project(flow_ref[...].reshape(4 * levels, width), table_ref[...])
    first = pl.ds(0, SUB, stride=rows)
    last = pl.ds(rows - 1, SUB, stride=rows)
    for half in range(2):
        part = extra[:, half * KMAX : (half + 1) * KMAX]
        coef_ref[half, first, :] = coef_ref[half, first, :] + part[:levels]
        coef_ref[half, last, :] = coef_ref[half, last, :] + part[levels : 2 * levels]
        out_ref[half] = part[2 * levels : 3 * levels]
        out_ref[2 + half] = part[3 * levels :]
    put_slots(out_ref, 4, ways, lon, edge_ref[...])
    lane = lax.broadcasted_iota(jnp.int32, (SUB, KMAX), 1)
    unit = jnp.zeros((SUB, KMAX), F32)
    for side in range(2):
        for way, at in enumerate((cells, width - 1)):
            unit = jnp.where(lane == 4 * lon + 2 * side + way, flow_ref[2 + side][:, at : at + 1], unit)
    out_ref[4 + ways] = unit
    pack_rows(cut_ref, coef_ref, 5 + ways, out_ref)


def join_kernel(
    first, cells, ways,
    info_ref, cut_ref, coef_in_ref, edge_ref, own_ref, ring0_ref, ring1_ref, table_ref,
    flow_ref, edge_v_ref, edge_cut_ref, out_ref, coef_ref,
):
    coef_ref[...] = coef_in_ref[...]
    join_flows(first, cells, info_ref, own_ref, ring0_ref, ring1_ref, flow_ref, edge_v_ref, edge_cut_ref)
    join_body(cells, info_ref, cut_ref, ways, coef_ref, edge_ref, flow_ref, table_ref, out_ref)


def first_join_kernel(
    first, cells, ways,
    info_ref, cut_ref, s_ref, u_ref, v_ref, own_ref, ring0_ref, ring1_ref, table_ref,
    moved_ref, flow_ref, edge_v_ref, edge_cut_ref, out_ref,
    s_buf, u_buf, v_buf, coef_ref, edge_ref, sem,
):
    hbm_refs, buffers = (s_ref, u_ref, v_ref), (s_buf, u_buf, v_buf)
    loop(SUB, lambda level: every(level_copies(hbm_refs, buffers, sem, first, level), "start"))
    join_flows(first, cells, info_ref, own_ref, ring0_ref, ring1_ref, flow_ref, edge_v_ref, edge_cut_ref)
    first_body(first, cells, hbm_refs, buffers, sem, moved_ref, coef_ref, edge_ref, table_ref)
    join_body(cells, info_ref, cut_ref, ways, coef_ref, edge_ref, flow_ref, table_ref, out_ref)


def closed(x, west, east, cells):
    end = x.shape[1] - 128
    lane = lax.broadcasted_iota(jnp.int32, (x.shape[0], 128), 1)
    head = x[:, :128] + jnp.where(lane == 0, west, 0.0)
    tail = x[:, end:] + jnp.where(lane == cells - 1 - end, east, 0.0)
    return jnp.concatenate([head, x[:, 128:end], jnp.where(lane < cells - end, tail, 0.0)], axis=1)


def closed_groups(cells, cut_row_ref, in_ref, coef_ref, back_ref, moved_ref, flow_ref, out_ref, after=None):
    levels, rows, width = moved_ref.shape
    filtered = column(cut_row_ref[...].astype(F32)) >= 0.0
    row = lax.broadcasted_iota(jnp.int32, (8, width), 0)

    def body(i):
        smooth = rebuild(both_halves(coef_ref, pl.ds(i * GROUP * rows, GROUP * rows)), back_ref[...])
        for g in range(GROUP):
            level = i * GROUP + g
            came = in_ref[pl.ds(level, 1), :]
            plain = closed(moved_ref[level], column(came[:, :rows]), column(came[:, rows:]), cells)
            s = jnp.where(filtered, smooth[g * rows : (g + 1) * rows], plain)
            out_ref[level] = s[:, : out_ref.shape[2]]
            if flow_ref is not None:
                for side, at, edge in ((0, 0, 0), (1, rows - 8, 7)):
                    plain_edge = (row == edge) & jnp.logical_not(filtered[at : at + 8])
                    out_ref[level, at : at + 8, :] = out_ref[level, at : at + 8, :] + jnp.where(
                        plain_edge, flow_ref[side, pl.ds(level, 1), :], 0.0
                    )
        if after is not None:
            after(i)

    loop(levels // GROUP, body)


def second_kernel(
    first, total, cells, ways,
    info_ref, cut_ref, cut_row_ref, a_ref, b_ref, flow_ref, edge_v_ref, edge_cut_ref,
    moved_ref, table_ref, back_ref, u_ref, v_ref,
    out_ref, pay_ref,
    coef_ref, sum_ref, step_ref, edge_ref, in_ref, place_ref, s_ref, u_buf, v_buf, sem,
):
    rows = cut_ref.shape[0]
    levels, _, width = out_ref.shape
    lon = info_ref[0]

    def copies(level):
        return level_copies((u_ref, v_ref), (u_buf, v_buf), sem, first, level)

    loop(levels, lambda level: every(copies(level), "start"))
    unpack_rows(cut_ref, a_ref, b_ref, 5 + ways, total, coef_ref)
    for side in range(2):
        for half in range(2):
            at = 2 * side + half
            cut = edge_cut_ref[side].astype(jnp.int32)
            edge_ref[side * levels : (side + 1) * levels, half * KMAX : (half + 1) * KMAX] = scaled(
                a_ref[at] + b_ref[at], half, cut, total
            )
    inflow(a_ref, b_ref, 4, ways, lon, rows, in_ref)
    unit = a_ref[4 + ways] + b_ref[4 + ways]
    lane = lax.broadcasted_iota(jnp.int32, (SUB, KMAX), 1)
    smooth = rebuild(edge_ref[...], back_ref[...])
    for side in range(2):
        came = [
            jnp.sum(jnp.where(lane == 4 * lax.rem(lon + ways + step, ways) + 2 * side + way, unit, 0.0), axis=1, keepdims=True)
            for way, step in enumerate((-1, 1))
        ]
        plain = closed(flow_ref[2 + side], came[0], came[1], cells)
        filtered = edge_cut_ref[side][:, 0:1] >= 0.0
        s = jnp.where(filtered, smooth[side * levels : (side + 1) * levels], plain)
        step_ref[side] = (southward if side == 0 else northward)(s, edge_v_ref[side])
    closed_groups(cells, cut_row_ref, in_ref, coef_ref, back_ref, moved_ref, flow_ref, s_ref)

    def one(level):
        row = pl.ds(level, 1)
        every(copies(level), "wait")
        out_ref[level] = moved_rows(s_ref[level], padded(u_buf[level], width), padded(v_buf[level], width))
        out_ref[level, 0:1, :] = out_ref[level, 0:1, :] + step_ref[0, row, :]
        out_ref[level, rows - 1 : rows, :] = out_ref[level, rows - 1 : rows, :] + step_ref[1, row, :]
        place_ref[row, :] = outflow(out_ref[level, :, width - 128 :], cells, width)

    loop(levels, one)
    project_groups(out_ref, table_ref, sum_ref)
    put_slots(pay_ref, 0, ways, lon, place_ref[...])
    pack_rows(cut_ref, sum_ref, ways, pay_ref)


def third_kernel(
    first, total, cells, ways, info_ref, cut_ref, cut_row_ref, a_ref, b_ref, moved_ref, back_ref, *refs
):
    out_ref, coef_ref, in_ref, buffer, out_sem = refs[-5:]
    rows = cut_ref.shape[0]
    levels = moved_ref.shape[0]
    unpack_rows(cut_ref, a_ref, b_ref, ways, total, coef_ref)
    inflow(a_ref, b_ref, 0, ways, info_ref[0], rows, in_ref)
    closed_groups(
        cells, cut_row_ref, in_ref, coef_ref, back_ref, moved_ref, None, buffer,
        lambda i: group_store(buffer, out_ref, out_sem, first, i).start(),
    )
    loop(levels // GROUP, lambda i: group_store(buffer, out_ref, out_sem, first, i).wait())


SMEM = pl.BlockSpec(memory_space=pltpu.SMEM)
VMEM = pl.BlockSpec(memory_space=pltpu.VMEM)
HBM = pl.BlockSpec(memory_space=pltpu.HBM)


def shape(*dims, dtype=F32):
    return jax.ShapeDtypeStruct(dims, dtype)


def call(kernel, inputs, outputs, scratch, mib, aliases=None):
    return pl.pallas_call(
        kernel,
        in_specs=[spec for _, spec in inputs],
        out_specs=[spec for _, spec in outputs],
        out_shape=[what for what, _ in outputs],
        scratch_shapes=scratch,
        input_output_aliases=aliases or {},
        compiler_params=pltpu.CompilerParams(vmem_limit_bytes=mib * MIB),
    )(*[array for array, _ in inputs])


def swap(x, bit):
    count = lax.axis_size("lon")
    return lax.ppermute(x, "lon", [(i, i ^ (1 << bit)) for i in range(count)])


def sum_over_lon(x, upward):
    bits = lax.axis_size("lon").bit_length() - 1
    for i in range(bits):
        got = swap(x, i if upward else bits - 1 - i)
        if i == bits - 1:
            return x, got
        x = x + got


def lat_ring(bands, ways, turn):
    pairs = []
    for band in range(bands):
        for l in range(ways):
            east = l < ways // 2
            other = (l + ways // 2) % ways
            step = 1 if east == (turn == 0) else -1
            to = (band + step, l) if 0 <= band + step < bands else (band, other)
            pairs.append((l * bands + band, to[1] * bands + to[0]))
    return pairs


def on_device(tracer, zonal, meridional, cutoff_wave, polar_mask):
    levels, rows, cells = tracer.shape
    ways, bands = lax.axis_size("lon"), lax.axis_size("lat")
    width = wide(cells)
    total = cells * ways
    tables, backs = (jnp.asarray(x) for x in wave_tables(cells, ways))
    lon, band = lax.axis_index("lon"), lax.axis_index("lat")
    info = jnp.stack([lon, jnp.int32(ways), band, jnp.int32(bands)]).astype(jnp.int32)
    parts = levels // SUB
    steps = SUB // GROUP
    winds = (tracer, zonal, meridional)
    cut = jnp.where(polar_mask == 1, cutoff_wave, -1)
    cut_row = cut[None, :]

    top = pl.BlockSpec((levels, SUB, cells), lambda i: (0, 0, 0))
    bottom = pl.BlockSpec((levels, SUB, cells), lambda i: (0, rows // SUB - 1, 0))
    full = pl.BlockSpec((4, levels, width), lambda i: (0, 0, 0))
    ring0, ring1, own = pl.pallas_call(
        edge_kernel,
        grid=(1,),
        in_specs=[SMEM, pl.BlockSpec((1, rows), lambda i: (0, 0)), top, top, top, bottom, bottom, bottom],
        out_specs=[full, full, pl.BlockSpec((2, levels, width), lambda i: (0, 0, 0))],
        out_shape=[shape(4, levels, width), shape(4, levels, width), shape(2, levels, width)],
        compiler_params=pltpu.CompilerParams(vmem_limit_bytes=FIRST_MIB * MIB),
    )(info, cut_row, *winds, *winds)
    later, ring0 = lax.optimization_barrier((cut_row, ring0))
    kept = jnp.sum((later >= 0).astype(jnp.int32) + (later >= HALF).astype(jnp.int32))
    ring = ("lon", "lat")
    got0 = lax.ppermute(ring0, ring, lat_ring(bands, ways, 0))
    got1 = lax.ppermute(ring1, ring, lat_ring(bands, ways, 1))

    grid = shape(SUB, rows, width)
    coef = shape(2, SUB * rows, KMAX)
    edge = shape(SUB, KMAX)
    flows = [(shape(4, SUB, width), VMEM), (shape(2, SUB, width), VMEM), (shape(2, SUB, KMAX), VMEM)]
    head = 5 + ways

    def room(what):
        return pltpu.VMEM(what.shape, what.dtype)

    buffer = pltpu.VMEM((SUB, rows, cells), F32)
    table_shape, back_shape = (shape(*x.shape[1:], dtype=BF16) for x in (tables, backs))
    sems = pltpu.SemaphoreType.DMA
    moved_a, coef_a, edge_a, table, back = call(
        functools.partial(first_kernel, 0, cells),
        [(info, SMEM), *[(x, HBM) for x in (*winds, tables, backs)]],
        [(x, VMEM) for x in (grid, coef, edge, table_shape, back_shape)],
        [buffer, buffer, buffer, sems((3, SUB)), sems((2,))],
        FIRST_MIB,
    )

    def rest(limit, info, cut, cut_row, tracer, zonal, meridional, own, got0, got1, moved_a, coef_a, edge_a, table, back):
        pay = (shape(limit + head + 2, SUB, KMAX), VMEM)
        around = [(x, VMEM) for x in (own, got0, got1, table)]
        scalars = [(info, SMEM), (cut, SMEM)]
        joined = [(moved_a, *call(
            functools.partial(join_kernel, 0, cells, ways),
            [*scalars, (coef_a, VMEM), (edge_a, VMEM), *around],
            [*flows, pay],
            [room(coef)],
            8,
        ))]
        sums = [sum_over_lon(joined[0][4], True)]
        for part in range(1, parts):
            joined.append(call(
                functools.partial(first_join_kernel, part * SUB, cells, ways),
                [*scalars, *[(x, HBM) for x in (tracer, zonal, meridional)], *around],
                [(grid, VMEM), *flows, pay],
                [buffer, buffer, buffer, room(coef), room(edge), sems((3, SUB))],
                20,
            ))
            sums.append(sum_over_lon(joined[part][4], True))
        seconds = []
        for part in range(parts):
            moved, flow, edge_v, edge_cut, _ = joined[part]
            seconds.append(call(
                functools.partial(second_kernel, part * SUB, total, cells, ways),
                [*scalars, *[(x, VMEM) for x in (cut_row, *sums[part], flow, edge_v, edge_cut, moved, table, back)],
                 (zonal, HBM), (meridional, HBM)],
                [(grid, VMEM), (shape(limit + ways + 2, SUB, KMAX), VMEM)],
                [room(coef), room(coef), pltpu.VMEM((2, SUB, width), F32),
                 pltpu.VMEM((2 * SUB, 2 * KMAX), F32), room(edge), room(edge), room(grid), buffer, buffer, sems((2, SUB))],
                20,
            ))
        sums = [sum_over_lon(x[1], True) for x in seconds]
        out = []
        for part in range(parts):
            out = call(
                functools.partial(third_kernel, part * SUB, total, cells, ways),
                [*scalars, *[(x, VMEM) for x in (cut_row, *sums[part], seconds[part][0], back)],
                 *[(x, HBM) for x in out]],
                [(shape(levels, rows, cells), HBM)],
                [room(coef), room(edge), buffer, sems((steps,))],
                12,
                {7: 0} if part else None,
            )
        return out[0]

    limits = sorted({min(-(-x * rows // 64), 2 * rows) for x in LIMITS})
    choice = sum((kept > x).astype(jnp.int32) for x in limits[:-1])
    return lax.switch(
        choice, [functools.partial(rest, x) for x in limits],
        info, cut, cut_row, tracer, zonal, meridional, own, got0, got1, moved_a, coef_a, edge_a, table, back,
    )


def solution(mesh):
    placed = (
        P(None, "lat", "lon"),
        P(None, "lat", "lon"),
        P(None, "lat", "lon"),
        P("lat"),
        P("lat"),
    )
    return jax.shard_map(
        on_device, mesh=mesh, in_specs=placed, out_specs=P(None, "lat", "lon"), check_vma=False
    )
```

```python
import functools

import jax
import jax.numpy as jnp
import ml_dtypes
import numpy as np
from jax import lax
from jax.experimental import pallas as pl
from jax.experimental.pallas import tpu as pltpu
from jax.sharding import PartitionSpec as P

KMAX = 128
HALF = KMAX // 2
DIFFUSION = 0.1
GROUP = 4
SUB = 8
FIRST_MIB = 52
LIMITS = (88, 128)
F32 = jnp.float32
BF16 = jnp.bfloat16
MIB = 1024 * 1024


def wide(cells):
    return -(-(cells + 2) // 128) * 128


def split_np(values):
    high = values.astype(ml_dtypes.bfloat16)
    low = (values - high.astype(np.float64)).astype(ml_dtypes.bfloat16)
    return high, low


@functools.lru_cache(maxsize=None)
def wave_tables(cells, ways):
    total = cells * ways
    width = wide(cells)
    lane = np.arange(width)
    start = np.arange(ways)[:, None] * cells
    place = np.where(lane == width - 1, -1, lane)[None, :] + start
    used = (lane <= cells) | (lane == width - 1)
    column = np.arange(2 * KMAX)
    wave = column // KMAX * HALF + column % HALF
    sine = column % KMAX // HALF
    angle = (place[:, :, None] * wave[None, None, :] % total) * (2.0 * np.pi / total)
    table = np.where(sine == 1, np.sin(angle), np.cos(angle))
    project = split_np(np.where(used[None, :, None], table, 0.0))
    inside = np.where((lane < cells)[None, :, None], table, 0.0).transpose(0, 2, 1)
    rebuild = split_np(inside)
    return np.concatenate(project, axis=2), np.concatenate(rebuild, axis=1)


def split(x):
    high = x.astype(BF16)
    return high, (x - high.astype(F32)).astype(BF16)


def project(x, table):
    high, low = split(x)
    both = jnp.dot(high, table, preferred_element_type=F32)
    cross = jnp.dot(low, table[:, : 2 * KMAX], preferred_element_type=F32)
    return both[:, : 2 * KMAX] + both[:, 2 * KMAX :] + cross


def rebuild(coefficients, table):
    high, low = split(coefficients)
    both = jnp.dot(jnp.concatenate([high, high], axis=1), table, preferred_element_type=F32)
    return both + jnp.dot(low, table[: 2 * KMAX], preferred_element_type=F32)


def padded(x, width):
    return jnp.concatenate([x, jnp.zeros((x.shape[0], width - x.shape[1]), F32)], axis=1)


def along_lon(s, u):
    width = s.shape[1]
    spread = DIFFUSION * s
    carry = (0.5 * u) * s
    return (
        (1.0 - 4.0 * DIFFUSION) * s
        + pltpu.roll(spread - carry, width - 1, 1)
        + pltpu.roll(spread + carry, 1, 1)
    )


def moved_rows(s, u, v):
    rows = s.shape[0]
    spread = DIFFUSION * s
    carry = (0.5 * v) * s
    row = lax.broadcasted_iota(jnp.int32, s.shape, 0)
    from_next = jnp.where(row == rows - 1, 0.0, pltpu.roll(spread - carry, rows - 1, 0))
    from_last = jnp.where(row == 0, 0.0, pltpu.roll(spread + carry, 1, 0))
    return along_lon(s, u) + from_next + from_last


def put_halves(ref, at, value):
    for half in range(2):
        ref[half, at, :] = value[:, half * KMAX : (half + 1) * KMAX]


def both_halves(ref, at):
    return jnp.concatenate([ref[0, at, :], ref[1, at, :]], axis=1)


def southward(s, v):
    return DIFFUSION * s + (0.5 * v) * s


def northward(s, v):
    return DIFFUSION * s - (0.5 * v) * s


def edge_kernel(
    info_ref, cutoff_ref, mask_ref, s_ref, u_ref, v_ref,
    ring0_ref, ring1_ref, own_ref, cut_ref, rows_ref, cuts_ref, sem,
):
    levels, width = own_ref.shape[1:]
    rows = cut_ref.shape[1]
    near = info_ref[0] < info_ref[1] // 2
    wanted = [(h, at) for at in (0, rows - 1) for h in (s_ref, u_ref, v_ref)]
    wanted += [(h, at) for at in (1, rows - 2) for h in (s_ref, v_ref)]
    copies = [
        pltpu.make_async_copy(h.at[:, at, :], rows_ref.at[i], sem.at[i]) for i, (h, at) in enumerate(wanted)
    ]
    for i, h in enumerate((cutoff_ref, mask_ref)):
        copies.append(pltpu.make_async_copy(h, cuts_ref.at[i], sem.at[len(wanted) + i]))
    every(copies, "start")
    every(copies, "wait")
    cut = jnp.where(cuts_ref[1] == 1, cuts_ref[0], -1)
    cut_ref[...] = cut
    sides = []
    for side, (flow, row) in enumerate(((northward, 0), (southward, rows - 1))):
        s, u, v = (rows_ref[3 * side + i] for i in range(3))
        tail = jnp.broadcast_to(cut[:, row : row + 1].astype(F32), (levels, width - s.shape[1]))
        beyond = flow(rows_ref[6 + 2 * side], rows_ref[7 + 2 * side])
        sides.append([jnp.concatenate([s, tail], axis=1), padded(u, width), padded(v, width), padded(beyond, width)])
        own_ref[side] = padded(flow(s, v), width)
    for i in range(4):
        ring0_ref[i] = jnp.where(near, sides[1][i], sides[0][i])
        ring1_ref[i] = jnp.where(near, sides[0][i], sides[1][i])


def level_copies(hbm_refs, buffers, sem, first, level):
    return [
        pltpu.make_async_copy(h.at[first + level], b.at[level], sem.at[q, level])
        for q, (h, b) in enumerate(zip(hbm_refs, buffers))
    ]


def every(copies, act):
    for copy in copies:
        getattr(copy, act)()


def group_store(buffer, hbm_ref, sem, first, i):
    return pltpu.make_async_copy(
        buffer.at[pl.ds(i * GROUP, GROUP)], hbm_ref.at[pl.ds(first + i * GROUP, GROUP)], sem.at[i]
    )


def is_diagonal(rows, lanes):
    lane = lax.broadcasted_iota(jnp.int32, (rows, lanes), 1)
    return lax.broadcasted_iota(jnp.int32, (rows, lanes), 0) == lax.rem(lane, rows)


def outflow(tile, cells, width):
    rows = tile.shape[0]
    at = cells - (width - 128)
    lane = lax.broadcasted_iota(jnp.int32, tile.shape, 1)
    both = jnp.where(lane < rows, tile[:, at : at + 1], tile[:, 127:128])
    return jnp.sum(jnp.where(is_diagonal(*tile.shape), both, 0.0), axis=0, keepdims=True)


def column(row):
    rows = row.shape[1]
    spread = jnp.broadcast_to(row, (rows, rows))
    return jnp.sum(jnp.where(is_diagonal(rows, rows), spread, 0.0), axis=1, keepdims=True)


def pack_rows(cut_ref, source_ref, first, out_ref):
    rows = cut_ref.shape[0]

    def body(r, unit):
        cut = cut_ref[r]
        for half in range(2):
            out_ref[unit + half] = source_ref[half, pl.ds(r, SUB, stride=rows), :]
        return unit + (cut >= 0).astype(jnp.int32) + (cut >= HALF).astype(jnp.int32)

    lax.fori_loop(0, rows, body, first, unroll=8)


def scaled(x, half, cut, total):
    lane = lax.broadcasted_iota(jnp.int32, (SUB, KMAX), 1)
    wave = half * HALF + lane % HALF
    scale = jnp.where(wave == 0, 1.0 / total, 2.0 / total)
    return jnp.where(wave <= cut, x * scale, 0.0)


def unpack_rows(cut_ref, a_ref, b_ref, first, total, out_ref):
    rows = cut_ref.shape[0]
    last = a_ref.shape[0] - 1

    def body(r, unit):
        cut = cut_ref[r]
        for half in range(2):
            at = jnp.minimum(unit + half, last)
            out_ref[half, pl.ds(r, SUB, stride=rows), :] = scaled(a_ref[at] + b_ref[at], half, cut, total)
        return unit + (cut >= 0).astype(jnp.int32) + (cut >= HALF).astype(jnp.int32)

    lax.fori_loop(0, rows, body, first, unroll=8)


def put_slots(out_ref, first, ways, lon, value):
    for i in range(ways):
        out_ref[first + i] = jnp.zeros(value.shape, F32)
    out_ref[first + lon] = value


def inflow(a_ref, b_ref, first, ways, lon, rows, place_ref):
    west, east = first + lax.rem(lon + ways - 1, ways), first + lax.rem(lon + 1, ways)
    lane = lax.broadcasted_iota(jnp.int32, (SUB, 2 * rows), 1)
    place_ref[...] = jnp.where(lane < rows, a_ref[west] + b_ref[west], a_ref[east] + b_ref[east])


def loop(count, body):
    def step(i, _):
        body(i)
        return 0

    lax.fori_loop(0, count, step, 0)


def project_groups(x_ref, table_ref, coef_ref):
    levels, rows, width = x_ref.shape

    def body(i):
        x = x_ref[pl.ds(i * GROUP, GROUP)].reshape(GROUP * rows, width)
        put_halves(coef_ref, pl.ds(i * GROUP * rows, GROUP * rows), project(x, table_ref[...]))

    loop(levels // GROUP, body)


def first_body(first, cells, hbm_refs, buffers, sem, moved_ref, coef_ref, edge_ref, table_ref, ready=None):
    levels, rows, width = moved_ref.shape

    def one(level):
        every(level_copies(hbm_refs, buffers, sem, first, level), "wait")
        moved_ref[level] = moved_rows(*[padded(b[level], width) for b in buffers])
        edge_ref[pl.ds(level, 1), :] = outflow(moved_ref[level, :, width - 128 :], cells, width)

    loop(levels, one)
    if ready is not None:
        ready.wait()
    project_groups(moved_ref, table_ref, coef_ref)


def first_kernel(
    first, cells, info_ref, cut_row_ref, s_ref, u_ref, v_ref, tables_ref, backs_ref,
    moved_ref, coef_ref, edge_ref, table_ref, back_ref, kept_ref, s_buf, u_buf, v_buf, sem, table_sem,
):
    hbm_refs, buffers = (s_ref, u_ref, v_ref), (s_buf, u_buf, v_buf)
    lon = info_ref[0]
    ready = pltpu.make_async_copy(tables_ref.at[lon], table_ref, table_sem.at[0])
    later = pltpu.make_async_copy(backs_ref.at[lon], back_ref, table_sem.at[1])
    loop(SUB, lambda level: every(level_copies(hbm_refs, buffers, sem, first, level), "start"))
    ready.start()
    later.start()
    cut = cut_row_ref[...]
    kept_ref[0] = jnp.sum((cut >= 0).astype(jnp.int32) + (cut >= HALF).astype(jnp.int32))
    first_body(first, cells, hbm_refs, buffers, sem, moved_ref, coef_ref, edge_ref, table_ref, ready)
    later.wait()


def join_flows(first, cells, info_ref, own_ref, ring0_ref, ring1_ref, flow_ref, edge_v_ref, edge_cut_ref):
    levels, width = flow_ref.shape[1:]
    at = slice(first, first + levels)
    near = info_ref[0] < info_ref[1] // 2
    lane = lax.broadcasted_iota(jnp.int32, (levels, width), 1)
    for side in range(2):
        got = [jnp.where(near == (side == 0), ring0_ref[i, at, :], ring1_ref[i, at, :]) for i in range(4)]
        edge_cut_ref[side] = jnp.broadcast_to(got[0][:, cells : cells + 1], (levels, KMAX))
        s = jnp.where(lane < cells, got[0], 0.0)
        pole = info_ref[2] == (0 if side == 0 else info_ref[3] - 1)
        v = jnp.where(pole, -got[2], got[2])
        edge_v_ref[side] = v
        flow_ref[side] = southward(s, v) if side == 0 else northward(s, v)
        flow_ref[2 + side] = along_lon(s, got[1]) + got[3] + own_ref[side, at, :]


def join_body(cells, info_ref, cut_ref, ways, coef_ref, edge_ref, flow_ref, table_ref, out_ref):
    rows = cut_ref.shape[0]
    levels, width = flow_ref.shape[1:]
    lon = info_ref[0]
    extra = project(flow_ref[...].reshape(4 * levels, width), table_ref[...])
    first = pl.ds(0, SUB, stride=rows)
    last = pl.ds(rows - 1, SUB, stride=rows)
    for half in range(2):
        part = extra[:, half * KMAX : (half + 1) * KMAX]
        coef_ref[half, first, :] = coef_ref[half, first, :] + part[:levels]
        coef_ref[half, last, :] = coef_ref[half, last, :] + part[levels : 2 * levels]
        out_ref[half] = part[2 * levels : 3 * levels]
        out_ref[2 + half] = part[3 * levels :]
    put_slots(out_ref, 4, ways, lon, edge_ref[...])
    lane = lax.broadcasted_iota(jnp.int32, (SUB, KMAX), 1)
    unit = jnp.zeros((SUB, KMAX), F32)
    for side in range(2):
        for way, at in enumerate((cells, width - 1)):
            unit = jnp.where(lane == 4 * lon + 2 * side + way, flow_ref[2 + side][:, at : at + 1], unit)
    out_ref[4 + ways] = unit
    pack_rows(cut_ref, coef_ref, 5 + ways, out_ref)


def join_kernel(
    first, cells, ways,
    info_ref, cut_ref, coef_in_ref, edge_ref, own_ref, ring0_ref, ring1_ref, table_ref,
    flow_ref, edge_v_ref, edge_cut_ref, out_ref, coef_ref,
):
    coef_ref[...] = coef_in_ref[...]
    join_flows(first, cells, info_ref, own_ref, ring0_ref, ring1_ref, flow_ref, edge_v_ref, edge_cut_ref)
    join_body(cells, info_ref, cut_ref, ways, coef_ref, edge_ref, flow_ref, table_ref, out_ref)


def first_join_kernel(
    first, cells, ways,
    info_ref, cut_ref, s_ref, u_ref, v_ref, own_ref, ring0_ref, ring1_ref, table_ref,
    moved_ref, flow_ref, edge_v_ref, edge_cut_ref, out_ref,
    s_buf, u_buf, v_buf, coef_ref, edge_ref, sem,
):
    hbm_refs, buffers = (s_ref, u_ref, v_ref), (s_buf, u_buf, v_buf)
    loop(SUB, lambda level: every(level_copies(hbm_refs, buffers, sem, first, level), "start"))
    join_flows(first, cells, info_ref, own_ref, ring0_ref, ring1_ref, flow_ref, edge_v_ref, edge_cut_ref)
    first_body(first, cells, hbm_refs, buffers, sem, moved_ref, coef_ref, edge_ref, table_ref)
    join_body(cells, info_ref, cut_ref, ways, coef_ref, edge_ref, flow_ref, table_ref, out_ref)


def closed(x, west, east, cells):
    end = x.shape[1] - 128
    lane = lax.broadcasted_iota(jnp.int32, (x.shape[0], 128), 1)
    head = x[:, :128] + jnp.where(lane == 0, west, 0.0)
    tail = x[:, end:] + jnp.where(lane == cells - 1 - end, east, 0.0)
    return jnp.concatenate([head, x[:, 128:end], jnp.where(lane < cells - end, tail, 0.0)], axis=1)


def closed_groups(cells, cut_row_ref, in_ref, coef_ref, back_ref, moved_ref, flow_ref, out_ref, after=None):
    levels, rows, width = moved_ref.shape
    filtered = column(cut_row_ref[...].astype(F32)) >= 0.0
    row = lax.broadcasted_iota(jnp.int32, (8, width), 0)

    def body(i):
        smooth = rebuild(both_halves(coef_ref, pl.ds(i * GROUP * rows, GROUP * rows)), back_ref[...])
        for g in range(GROUP):
            level = i * GROUP + g
            came = in_ref[pl.ds(level, 1), :]
            plain = closed(moved_ref[level], column(came[:, :rows]), column(came[:, rows:]), cells)
            s = jnp.where(filtered, smooth[g * rows : (g + 1) * rows], plain)
            out_ref[level] = s[:, : out_ref.shape[2]]
            if flow_ref is not None:
                for side, at, edge in ((0, 0, 0), (1, rows - 8, 7)):
                    plain_edge = (row == edge) & jnp.logical_not(filtered[at : at + 8])
                    out_ref[level, at : at + 8, :] = out_ref[level, at : at + 8, :] + jnp.where(
                        plain_edge, flow_ref[side, pl.ds(level, 1), :], 0.0
                    )
        if after is not None:
            after(i)

    loop(levels // GROUP, body)


def second_kernel(
    first, total, cells, ways,
    info_ref, cut_ref, cut_row_ref, a_ref, b_ref, flow_ref, edge_v_ref, edge_cut_ref,
    moved_ref, table_ref, back_ref, u_ref, v_ref,
    out_ref, pay_ref,
    coef_ref, sum_ref, step_ref, edge_ref, in_ref, place_ref, s_ref, u_buf, v_buf, sem,
):
    rows = cut_ref.shape[0]
    levels, _, width = out_ref.shape
    lon = info_ref[0]

    def copies(level):
        return level_copies((u_ref, v_ref), (u_buf, v_buf), sem, first, level)

    loop(levels, lambda level: every(copies(level), "start"))
    unpack_rows(cut_ref, a_ref, b_ref, 5 + ways, total, coef_ref)
    for side in range(2):
        for half in range(2):
            at = 2 * side + half
            cut = edge_cut_ref[side].astype(jnp.int32)
            edge_ref[side * levels : (side + 1) * levels, half * KMAX : (half + 1) * KMAX] = scaled(
                a_ref[at] + b_ref[at], half, cut, total
            )
    inflow(a_ref, b_ref, 4, ways, lon, rows, in_ref)
    unit = a_ref[4 + ways] + b_ref[4 + ways]
    lane = lax.broadcasted_iota(jnp.int32, (SUB, KMAX), 1)
    smooth = rebuild(edge_ref[...], back_ref[...])
    for side in range(2):
        came = [
            jnp.sum(jnp.where(lane == 4 * lax.rem(lon + ways + step, ways) + 2 * side + way, unit, 0.0), axis=1, keepdims=True)
            for way, step in enumerate((-1, 1))
        ]
        plain = closed(flow_ref[2 + side], came[0], came[1], cells)
        filtered = edge_cut_ref[side][:, 0:1] >= 0.0
        s = jnp.where(filtered, smooth[side * levels : (side + 1) * levels], plain)
        step_ref[side] = (southward if side == 0 else northward)(s, edge_v_ref[side])
    closed_groups(cells, cut_row_ref, in_ref, coef_ref, back_ref, moved_ref, flow_ref, s_ref)

    def one(level):
        row = pl.ds(level, 1)
        every(copies(level), "wait")
        out_ref[level] = moved_rows(s_ref[level], padded(u_buf[level], width), padded(v_buf[level], width))
        out_ref[level, 0:1, :] = out_ref[level, 0:1, :] + step_ref[0, row, :]
        out_ref[level, rows - 1 : rows, :] = out_ref[level, rows - 1 : rows, :] + step_ref[1, row, :]
        place_ref[row, :] = outflow(out_ref[level, :, width - 128 :], cells, width)

    loop(levels, one)
    project_groups(out_ref, table_ref, sum_ref)
    put_slots(pay_ref, 0, ways, lon, place_ref[...])
    pack_rows(cut_ref, sum_ref, ways, pay_ref)


def third_kernel(
    first, total, cells, ways, info_ref, cut_ref, cut_row_ref, a_ref, b_ref, moved_ref, back_ref, *refs
):
    out_ref, coef_ref, in_ref, buffer, out_sem = refs[-5:]
    rows = cut_ref.shape[0]
    levels = moved_ref.shape[0]
    unpack_rows(cut_ref, a_ref, b_ref, ways, total, coef_ref)
    inflow(a_ref, b_ref, 0, ways, info_ref[0], rows, in_ref)
    closed_groups(
        cells, cut_row_ref, in_ref, coef_ref, back_ref, moved_ref, None, buffer,
        lambda i: group_store(buffer, out_ref, out_sem, first, i).start(),
    )
    loop(levels // GROUP, lambda i: group_store(buffer, out_ref, out_sem, first, i).wait())


SMEM = pl.BlockSpec(memory_space=pltpu.SMEM)
VMEM = pl.BlockSpec(memory_space=pltpu.VMEM)
HBM = pl.BlockSpec(memory_space=pltpu.HBM)


def shape(*dims, dtype=F32):
    return jax.ShapeDtypeStruct(dims, dtype)


def call(kernel, inputs, outputs, scratch, mib, aliases=None):
    return pl.pallas_call(
        kernel,
        in_specs=[spec for _, spec in inputs],
        out_specs=[spec for _, spec in outputs],
        out_shape=[what for what, _ in outputs],
        scratch_shapes=scratch,
        input_output_aliases=aliases or {},
        compiler_params=pltpu.CompilerParams(vmem_limit_bytes=mib * MIB),
    )(*[array for array, _ in inputs])


def swap(x, bit):
    count = lax.axis_size("lon")
    return lax.ppermute(x, "lon", [(i, i ^ (1 << bit)) for i in range(count)])


def sum_over_lon(x, upward):
    bits = lax.axis_size("lon").bit_length() - 1
    for i in range(bits):
        got = swap(x, i if upward else bits - 1 - i)
        if i == bits - 1:
            return x, got
        x = x + got


def lat_ring(bands, ways, turn):
    pairs = []
    for band in range(bands):
        for l in range(ways):
            east = l < ways // 2
            other = (l + ways // 2) % ways
            step = 1 if east == (turn == 0) else -1
            to = (band + step, l) if 0 <= band + step < bands else (band, other)
            pairs.append((l * bands + band, to[1] * bands + to[0]))
    return pairs


def on_device(tracer, zonal, meridional, cutoff_wave, polar_mask):
    levels, rows, cells = tracer.shape
    ways, bands = lax.axis_size("lon"), lax.axis_size("lat")
    width = wide(cells)
    total = cells * ways
    tables, backs = (jnp.asarray(x) for x in wave_tables(cells, ways))
    lon, band = lax.axis_index("lon"), lax.axis_index("lat")
    info = jnp.stack([lon, jnp.int32(ways), band, jnp.int32(bands)]).astype(jnp.int32)
    parts = levels // SUB
    steps = SUB // GROUP
    winds = (tracer, zonal, meridional)
    ring0, ring1, own, cut_row = call(
        edge_kernel,
        [(info, SMEM), (cutoff_wave[None, :], HBM), (polar_mask[None, :], HBM), *[(x, HBM) for x in winds]],
        [(shape(4, levels, width), VMEM), (shape(4, levels, width), VMEM), (shape(2, levels, width), VMEM),
         (shape(1, rows, dtype=jnp.int32), VMEM)],
        [pltpu.VMEM((10, levels, cells), F32), pltpu.VMEM((2, 1, rows), jnp.int32), pltpu.SemaphoreType.DMA((12,))],
        FIRST_MIB,
    )
    cut = cut_row[0]
    ring = ("lon", "lat")
    got0 = lax.ppermute(ring0, ring, lat_ring(bands, ways, 0))
    got1 = lax.ppermute(ring1, ring, lat_ring(bands, ways, 1))

    grid = shape(SUB, rows, width)
    coef = shape(2, SUB * rows, KMAX)
    edge = shape(SUB, KMAX)
    flows = [(shape(4, SUB, width), VMEM), (shape(2, SUB, width), VMEM), (shape(2, SUB, KMAX), VMEM)]
    head = 5 + ways

    def room(what):
        return pltpu.VMEM(what.shape, what.dtype)

    buffer = pltpu.VMEM((SUB, rows, cells), F32)
    table_shape, back_shape = (shape(*x.shape[1:], dtype=BF16) for x in (tables, backs))
    sems = pltpu.SemaphoreType.DMA
    moved_a, coef_a, edge_a, table, back, kept = call(
        functools.partial(first_kernel, 0, cells),
        [(info, SMEM), (cut_row, VMEM), *[(x, HBM) for x in (*winds, tables, backs)]],
        [*[(x, VMEM) for x in (grid, coef, edge, table_shape, back_shape)], (shape(1, dtype=jnp.int32), SMEM)],
        [buffer, buffer, buffer, sems((3, SUB)), sems((2,))],
        FIRST_MIB,
    )

    def rest(limit, info, cut, cut_row, tracer, zonal, meridional, own, got0, got1, moved_a, coef_a, edge_a, table, back):
        pay = (shape(limit + head + 2, SUB, KMAX), VMEM)
        around = [(x, VMEM) for x in (own, got0, got1, table)]
        scalars = [(info, SMEM), (cut, SMEM)]
        joined = [(moved_a, *call(
            functools.partial(join_kernel, 0, cells, ways),
            [*scalars, (coef_a, VMEM), (edge_a, VMEM), *around],
            [*flows, pay],
            [room(coef)],
            8,
        ))]
        sums = [sum_over_lon(joined[0][4], True)]
        for part in range(1, parts):
            joined.append(call(
                functools.partial(first_join_kernel, part * SUB, cells, ways),
                [*scalars, *[(x, HBM) for x in (tracer, zonal, meridional)], *around],
                [(grid, VMEM), *flows, pay],
                [buffer, buffer, buffer, room(coef), room(edge), sems((3, SUB))],
                20,
            ))
            sums.append(sum_over_lon(joined[part][4], True))
        seconds = []
        for part in range(parts):
            moved, flow, edge_v, edge_cut, _ = joined[part]
            seconds.append(call(
                functools.partial(second_kernel, part * SUB, total, cells, ways),
                [*scalars, *[(x, VMEM) for x in (cut_row, *sums[part], flow, edge_v, edge_cut, moved, table, back)],
                 (zonal, HBM), (meridional, HBM)],
                [(grid, VMEM), (shape(limit + ways + 2, SUB, KMAX), VMEM)],
                [room(coef), room(coef), pltpu.VMEM((2, SUB, width), F32),
                 pltpu.VMEM((2 * SUB, 2 * KMAX), F32), room(edge), room(edge), room(grid), buffer, buffer, sems((2, SUB))],
                20,
            ))
        sums = [sum_over_lon(x[1], True) for x in seconds]
        out = []
        for part in range(parts):
            out = call(
                functools.partial(third_kernel, part * SUB, total, cells, ways),
                [*scalars, *[(x, VMEM) for x in (cut_row, *sums[part], seconds[part][0], back)],
                 *[(x, HBM) for x in out]],
                [(shape(levels, rows, cells), HBM)],
                [room(coef), room(edge), buffer, sems((steps,))],
                12,
                {7: 0} if part else None,
            )
        return out[0]

    limits = sorted({min(-(-x * rows // 64), 2 * rows) for x in LIMITS})
    choice = sum((kept[0] > x).astype(jnp.int32) for x in limits[:-1])
    return lax.switch(
        choice, [functools.partial(rest, x) for x in limits],
        info, cut, cut_row, tracer, zonal, meridional, own, got0, got1, moved_a, coef_a, edge_a, table, back,
    )


def solution(mesh):
    placed = (
        P(None, "lat", "lon"),
        P(None, "lat", "lon"),
        P(None, "lat", "lon"),
        P("lat"),
        P("lat"),
    )
    return jax.shard_map(
        on_device, mesh=mesh, in_specs=placed, out_specs=P(None, "lat", "lon"), check_vma=False
    )
```

```python
import functools

import jax
import jax.numpy as jnp
import ml_dtypes
import numpy as np
from jax import lax
from jax.experimental import pallas as pl
from jax.experimental.pallas import tpu as pltpu
from jax.sharding import PartitionSpec as P

KMAX = 128
HALF = KMAX // 2
DIFFUSION = 0.1
GROUP = 4
SUB = 8
FIRST_MIB = 52
LIMITS = (88, 128)
F32 = jnp.float32
BF16 = jnp.bfloat16
MIB = 1024 * 1024


def wide(cells):
    return -(-(cells + 2) // 128) * 128


def split_np(values):
    high = values.astype(ml_dtypes.bfloat16)
    low = (values - high.astype(np.float64)).astype(ml_dtypes.bfloat16)
    return high, low


@functools.lru_cache(maxsize=None)
def wave_tables(cells, ways):
    total = cells * ways
    width = wide(cells)
    lane = np.arange(width)
    start = np.arange(ways)[:, None] * cells
    place = np.where(lane == width - 1, -1, lane)[None, :] + start
    used = (lane <= cells) | (lane == width - 1)
    column = np.arange(2 * KMAX)
    wave = column // KMAX * HALF + column % HALF
    sine = column % KMAX // HALF
    angle = (place[:, :, None] * wave[None, None, :] % total) * (2.0 * np.pi / total)
    table = np.where(sine == 1, np.sin(angle), np.cos(angle))
    project = split_np(np.where(used[None, :, None], table, 0.0))
    inside = np.where((lane < cells)[None, :, None], table, 0.0).transpose(0, 2, 1)
    rebuild = split_np(inside)
    return np.concatenate(project, axis=2), np.concatenate(rebuild, axis=1)


def split(x):
    high = x.astype(BF16)
    return high, (x - high.astype(F32)).astype(BF16)


def project(x, table):
    high, low = split(x)
    both = jnp.dot(high, table, preferred_element_type=F32)
    cross = jnp.dot(low, table[:, : 2 * KMAX], preferred_element_type=F32)
    return both[:, : 2 * KMAX] + both[:, 2 * KMAX :] + cross


def rebuild(coefficients, table):
    high, low = split(coefficients)
    both = jnp.dot(jnp.concatenate([high, high], axis=1), table, preferred_element_type=F32)
    return both + jnp.dot(low, table[: 2 * KMAX], preferred_element_type=F32)


def padded(x, width):
    return jnp.concatenate([x, jnp.zeros((x.shape[0], width - x.shape[1]), F32)], axis=1)


def along_lon(s, u):
    width = s.shape[1]
    spread = DIFFUSION * s
    carry = (0.5 * u) * s
    return (
        (1.0 - 4.0 * DIFFUSION) * s
        + pltpu.roll(spread - carry, width - 1, 1)
        + pltpu.roll(spread + carry, 1, 1)
    )


def moved_rows(s, u, v):
    rows = s.shape[0]
    spread = DIFFUSION * s
    carry = (0.5 * v) * s
    row = lax.broadcasted_iota(jnp.int32, s.shape, 0)
    from_next = jnp.where(row == rows - 1, 0.0, pltpu.roll(spread - carry, rows - 1, 0))
    from_last = jnp.where(row == 0, 0.0, pltpu.roll(spread + carry, 1, 0))
    return along_lon(s, u) + from_next + from_last


def put_halves(ref, at, value):
    for half in range(2):
        ref[half, at, :] = value[:, half * KMAX : (half + 1) * KMAX]


def both_halves(ref, at):
    return jnp.concatenate([ref[0, at, :], ref[1, at, :]], axis=1)


def southward(s, v):
    return DIFFUSION * s + (0.5 * v) * s


def northward(s, v):
    return DIFFUSION * s - (0.5 * v) * s


def edge_kernel(
    info_ref, cut_ref, s_ref, u_ref, v_ref, ring0_ref, ring1_ref, own_ref, rows_ref, sem,
):
    levels, width = own_ref.shape[1:]
    rows = cut_ref.shape[1]
    near = info_ref[0] < info_ref[1] // 2
    wanted = [(h, at) for at in (0, rows - 1) for h in (s_ref, u_ref, v_ref)]
    wanted += [(h, at) for at in (1, rows - 2) for h in (s_ref, v_ref)]
    copies = [
        pltpu.make_async_copy(h.at[:, at, :], rows_ref.at[i], sem.at[i]) for i, (h, at) in enumerate(wanted)
    ]
    every(copies, "start")
    every(copies, "wait")
    cut = cut_ref[...]
    sides = []
    for side, (flow, row) in enumerate(((northward, 0), (southward, rows - 1))):
        s, u, v = (rows_ref[3 * side + i] for i in range(3))
        tail = jnp.broadcast_to(cut[:, row : row + 1].astype(F32), (levels, width - s.shape[1]))
        beyond = flow(rows_ref[6 + 2 * side], rows_ref[7 + 2 * side])
        sides.append([jnp.concatenate([s, tail], axis=1), padded(u, width), padded(v, width), padded(beyond, width)])
        own_ref[side] = padded(flow(s, v), width)
    for i in range(4):
        ring0_ref[i] = jnp.where(near, sides[1][i], sides[0][i])
        ring1_ref[i] = jnp.where(near, sides[0][i], sides[1][i])


def level_copies(hbm_refs, buffers, sem, first, level):
    return [
        pltpu.make_async_copy(h.at[first + level], b.at[level], sem.at[q, level])
        for q, (h, b) in enumerate(zip(hbm_refs, buffers))
    ]


def every(copies, act):
    for copy in copies:
        getattr(copy, act)()


def group_store(buffer, hbm_ref, sem, first, i):
    return pltpu.make_async_copy(
        buffer.at[pl.ds(i * GROUP, GROUP)], hbm_ref.at[pl.ds(first + i * GROUP, GROUP)], sem.at[i]
    )


def is_diagonal(rows, lanes):
    lane = lax.broadcasted_iota(jnp.int32, (rows, lanes), 1)
    return lax.broadcasted_iota(jnp.int32, (rows, lanes), 0) == lax.rem(lane, rows)


def outflow(tile, cells, width):
    rows = tile.shape[0]
    at = cells - (width - 128)
    lane = lax.broadcasted_iota(jnp.int32, tile.shape, 1)
    both = jnp.where(lane < rows, tile[:, at : at + 1], tile[:, 127:128])
    return jnp.sum(jnp.where(is_diagonal(*tile.shape), both, 0.0), axis=0, keepdims=True)


def column(row):
    rows = row.shape[1]
    spread = jnp.broadcast_to(row, (rows, rows))
    return jnp.sum(jnp.where(is_diagonal(rows, rows), spread, 0.0), axis=1, keepdims=True)


def pack_rows(cut_ref, source_ref, first, out_ref):
    rows = cut_ref.shape[0]

    def body(r, unit):
        cut = cut_ref[r]
        for half in range(2):
            out_ref[unit + half] = source_ref[half, pl.ds(r, SUB, stride=rows), :]
        return unit + (cut >= 0).astype(jnp.int32) + (cut >= HALF).astype(jnp.int32)

    lax.fori_loop(0, rows, body, first, unroll=8)


def scaled(x, half, cut, total):
    lane = lax.broadcasted_iota(jnp.int32, (SUB, KMAX), 1)
    wave = half * HALF + lane % HALF
    scale = jnp.where(wave == 0, 1.0 / total, 2.0 / total)
    return jnp.where(wave <= cut, x * scale, 0.0)


def unpack_rows(cut_ref, a_ref, b_ref, first, total, out_ref):
    rows = cut_ref.shape[0]
    last = a_ref.shape[0] - 1

    def body(r, unit):
        cut = cut_ref[r]
        for half in range(2):
            at = jnp.minimum(unit + half, last)
            out_ref[half, pl.ds(r, SUB, stride=rows), :] = scaled(a_ref[at] + b_ref[at], half, cut, total)
        return unit + (cut >= 0).astype(jnp.int32) + (cut >= HALF).astype(jnp.int32)

    lax.fori_loop(0, rows, body, first, unroll=8)


def put_slots(out_ref, first, ways, lon, value):
    for i in range(ways):
        out_ref[first + i] = jnp.zeros(value.shape, F32)
    out_ref[first + lon] = value


def inflow(a_ref, b_ref, first, ways, lon, rows, place_ref):
    west, east = first + lax.rem(lon + ways - 1, ways), first + lax.rem(lon + 1, ways)
    lane = lax.broadcasted_iota(jnp.int32, (SUB, 2 * rows), 1)
    place_ref[...] = jnp.where(lane < rows, a_ref[west] + b_ref[west], a_ref[east] + b_ref[east])


def loop(count, body):
    def step(i, _):
        body(i)
        return 0

    lax.fori_loop(0, count, step, 0)


def project_groups(x_ref, table_ref, coef_ref):
    levels, rows, width = x_ref.shape

    def body(i):
        x = x_ref[pl.ds(i * GROUP, GROUP)].reshape(GROUP * rows, width)
        put_halves(coef_ref, pl.ds(i * GROUP * rows, GROUP * rows), project(x, table_ref[...]))

    loop(levels // GROUP, body)


def first_body(first, cells, hbm_refs, buffers, sem, moved_ref, coef_ref, edge_ref, table_ref, ready=None):
    levels, rows, width = moved_ref.shape

    def one(level):
        every(level_copies(hbm_refs, buffers, sem, first, level), "wait")
        moved_ref[level] = moved_rows(*[padded(b[level], width) for b in buffers])
        edge_ref[pl.ds(level, 1), :] = outflow(moved_ref[level, :, width - 128 :], cells, width)

    loop(levels, one)
    if ready is not None:
        ready.wait()
    project_groups(moved_ref, table_ref, coef_ref)


def first_kernel(
    first, cells, info_ref, cut_row_ref, s_ref, u_ref, v_ref, tables_ref, backs_ref,
    moved_ref, coef_ref, edge_ref, table_ref, back_ref, kept_ref, s_buf, u_buf, v_buf, sem, table_sem,
):
    hbm_refs, buffers = (s_ref, u_ref, v_ref), (s_buf, u_buf, v_buf)
    lon = info_ref[0]
    ready = pltpu.make_async_copy(tables_ref.at[lon], table_ref, table_sem.at[0])
    later = pltpu.make_async_copy(backs_ref.at[lon], back_ref, table_sem.at[1])
    loop(SUB, lambda level: every(level_copies(hbm_refs, buffers, sem, first, level), "start"))
    ready.start()
    later.start()
    cut = cut_row_ref[...]
    kept_ref[0] = jnp.sum((cut >= 0).astype(jnp.int32) + (cut >= HALF).astype(jnp.int32))
    first_body(first, cells, hbm_refs, buffers, sem, moved_ref, coef_ref, edge_ref, table_ref, ready)
    later.wait()


def join_flows(first, cells, info_ref, own_ref, ring0_ref, ring1_ref, flow_ref, edge_v_ref, edge_cut_ref):
    levels, width = flow_ref.shape[1:]
    at = slice(first, first + levels)
    near = info_ref[0] < info_ref[1] // 2
    lane = lax.broadcasted_iota(jnp.int32, (levels, width), 1)
    for side in range(2):
        got = [jnp.where(near == (side == 0), ring0_ref[i, at, :], ring1_ref[i, at, :]) for i in range(4)]
        edge_cut_ref[side] = jnp.broadcast_to(got[0][:, cells : cells + 1], (levels, KMAX))
        s = jnp.where(lane < cells, got[0], 0.0)
        pole = info_ref[2] == (0 if side == 0 else info_ref[3] - 1)
        v = jnp.where(pole, -got[2], got[2])
        edge_v_ref[side] = v
        flow_ref[side] = southward(s, v) if side == 0 else northward(s, v)
        flow_ref[2 + side] = along_lon(s, got[1]) + got[3] + own_ref[side, at, :]


def join_body(cells, info_ref, cut_ref, ways, coef_ref, edge_ref, flow_ref, table_ref, out_ref):
    rows = cut_ref.shape[0]
    levels, width = flow_ref.shape[1:]
    lon = info_ref[0]
    extra = project(flow_ref[...].reshape(4 * levels, width), table_ref[...])
    first = pl.ds(0, SUB, stride=rows)
    last = pl.ds(rows - 1, SUB, stride=rows)
    for half in range(2):
        part = extra[:, half * KMAX : (half + 1) * KMAX]
        coef_ref[half, first, :] = coef_ref[half, first, :] + part[:levels]
        coef_ref[half, last, :] = coef_ref[half, last, :] + part[levels : 2 * levels]
        out_ref[half] = part[2 * levels : 3 * levels]
        out_ref[2 + half] = part[3 * levels :]
    put_slots(out_ref, 4, ways, lon, edge_ref[...])
    lane = lax.broadcasted_iota(jnp.int32, (SUB, KMAX), 1)
    unit = jnp.zeros((SUB, KMAX), F32)
    for side in range(2):
        for way, at in enumerate((cells, width - 1)):
            unit = jnp.where(lane == 4 * lon + 2 * side + way, flow_ref[2 + side][:, at : at + 1], unit)
    out_ref[4 + ways] = unit
    pack_rows(cut_ref, coef_ref, 5 + ways, out_ref)


def join_kernel(
    first, cells, ways,
    info_ref, cut_ref, coef_in_ref, edge_ref, own_ref, ring0_ref, ring1_ref, table_ref,
    flow_ref, edge_v_ref, edge_cut_ref, out_ref, coef_ref,
):
    coef_ref[...] = coef_in_ref[...]
    join_flows(first, cells, info_ref, own_ref, ring0_ref, ring1_ref, flow_ref, edge_v_ref, edge_cut_ref)
    join_body(cells, info_ref, cut_ref, ways, coef_ref, edge_ref, flow_ref, table_ref, out_ref)


def first_join_kernel(
    first, cells, ways,
    info_ref, cut_ref, s_ref, u_ref, v_ref, own_ref, ring0_ref, ring1_ref, table_ref,
    moved_ref, flow_ref, edge_v_ref, edge_cut_ref, out_ref,
    s_buf, u_buf, v_buf, coef_ref, edge_ref, sem,
):
    hbm_refs, buffers = (s_ref, u_ref, v_ref), (s_buf, u_buf, v_buf)
    loop(SUB, lambda level: every(level_copies(hbm_refs, buffers, sem, first, level), "start"))
    join_flows(first, cells, info_ref, own_ref, ring0_ref, ring1_ref, flow_ref, edge_v_ref, edge_cut_ref)
    first_body(first, cells, hbm_refs, buffers, sem, moved_ref, coef_ref, edge_ref, table_ref)
    join_body(cells, info_ref, cut_ref, ways, coef_ref, edge_ref, flow_ref, table_ref, out_ref)


def closed(x, west, east, cells):
    end = x.shape[1] - 128
    lane = lax.broadcasted_iota(jnp.int32, (x.shape[0], 128), 1)
    head = x[:, :128] + jnp.where(lane == 0, west, 0.0)
    tail = x[:, end:] + jnp.where(lane == cells - 1 - end, east, 0.0)
    return jnp.concatenate([head, x[:, 128:end], jnp.where(lane < cells - end, tail, 0.0)], axis=1)


def closed_groups(cells, cut_row_ref, in_ref, coef_ref, back_ref, moved_ref, flow_ref, out_ref, after=None):
    levels, rows, width = moved_ref.shape
    filtered = column(cut_row_ref[...].astype(F32)) >= 0.0
    row = lax.broadcasted_iota(jnp.int32, (8, width), 0)

    def body(i):
        smooth = rebuild(both_halves(coef_ref, pl.ds(i * GROUP * rows, GROUP * rows)), back_ref[...])
        for g in range(GROUP):
            level = i * GROUP + g
            came = in_ref[pl.ds(level, 1), :]
            plain = closed(moved_ref[level], column(came[:, :rows]), column(came[:, rows:]), cells)
            s = jnp.where(filtered, smooth[g * rows : (g + 1) * rows], plain)
            out_ref[level] = s[:, : out_ref.shape[2]]
            if flow_ref is not None:
                for side, at, edge in ((0, 0, 0), (1, rows - 8, 7)):
                    plain_edge = (row == edge) & jnp.logical_not(filtered[at : at + 8])
                    out_ref[level, at : at + 8, :] = out_ref[level, at : at + 8, :] + jnp.where(
                        plain_edge, flow_ref[side, pl.ds(level, 1), :], 0.0
                    )
        if after is not None:
            after(i)

    loop(levels // GROUP, body)


def second_kernel(
    first, total, cells, ways,
    info_ref, cut_ref, cut_row_ref, a_ref, b_ref, flow_ref, edge_v_ref, edge_cut_ref,
    moved_ref, table_ref, back_ref, u_ref, v_ref,
    out_ref, pay_ref,
    coef_ref, sum_ref, step_ref, edge_ref, in_ref, place_ref, s_ref,
):
    rows = cut_ref.shape[0]
    levels, _, width = out_ref.shape
    lon = info_ref[0]

    unpack_rows(cut_ref, a_ref, b_ref, 5 + ways, total, coef_ref)
    for side in range(2):
        for half in range(2):
            at = 2 * side + half
            cut = edge_cut_ref[side].astype(jnp.int32)
            edge_ref[side * levels : (side + 1) * levels, half * KMAX : (half + 1) * KMAX] = scaled(
                a_ref[at] + b_ref[at], half, cut, total
            )
    inflow(a_ref, b_ref, 4, ways, lon, rows, in_ref)
    unit = a_ref[4 + ways] + b_ref[4 + ways]
    lane = lax.broadcasted_iota(jnp.int32, (SUB, KMAX), 1)
    smooth = rebuild(edge_ref[...], back_ref[...])
    for side in range(2):
        came = [
            jnp.sum(jnp.where(lane == 4 * lax.rem(lon + ways + step, ways) + 2 * side + way, unit, 0.0), axis=1, keepdims=True)
            for way, step in enumerate((-1, 1))
        ]
        plain = closed(flow_ref[2 + side], came[0], came[1], cells)
        filtered = edge_cut_ref[side][:, 0:1] >= 0.0
        s = jnp.where(filtered, smooth[side * levels : (side + 1) * levels], plain)
        step_ref[side] = (southward if side == 0 else northward)(s, edge_v_ref[side])
    closed_groups(cells, cut_row_ref, in_ref, coef_ref, back_ref, moved_ref, flow_ref, s_ref)

    def one(level):
        row = pl.ds(level, 1)
        out_ref[level] = moved_rows(s_ref[level], padded(u_ref[first + level], width), padded(v_ref[first + level], width))
        out_ref[level, 0:1, :] = out_ref[level, 0:1, :] + step_ref[0, row, :]
        out_ref[level, rows - 1 : rows, :] = out_ref[level, rows - 1 : rows, :] + step_ref[1, row, :]
        place_ref[row, :] = outflow(out_ref[level, :, width - 128 :], cells, width)

    loop(levels, one)
    project_groups(out_ref, table_ref, sum_ref)
    put_slots(pay_ref, 0, ways, lon, place_ref[...])
    pack_rows(cut_ref, sum_ref, ways, pay_ref)


def third_kernel(
    first, total, cells, ways, info_ref, cut_ref, cut_row_ref, a_ref, b_ref, moved_ref, back_ref, *refs
):
    out_ref, coef_ref, in_ref, buffer, out_sem = refs[-5:]
    rows = cut_ref.shape[0]
    levels = moved_ref.shape[0]
    unpack_rows(cut_ref, a_ref, b_ref, ways, total, coef_ref)
    inflow(a_ref, b_ref, 0, ways, info_ref[0], rows, in_ref)
    closed_groups(
        cells, cut_row_ref, in_ref, coef_ref, back_ref, moved_ref, None, buffer,
        lambda i: group_store(buffer, out_ref, out_sem, first, i).start(),
    )
    loop(levels // GROUP, lambda i: group_store(buffer, out_ref, out_sem, first, i).wait())


SMEM = pl.BlockSpec(memory_space=pltpu.SMEM)
VMEM = pl.BlockSpec(memory_space=pltpu.VMEM)
HBM = pl.BlockSpec(memory_space=pltpu.HBM)


def shape(*dims, dtype=F32):
    return jax.ShapeDtypeStruct(dims, dtype)


def call(kernel, inputs, outputs, scratch, mib, aliases=None):
    return pl.pallas_call(
        kernel,
        in_specs=[spec for _, spec in inputs],
        out_specs=[spec for _, spec in outputs],
        out_shape=[what for what, _ in outputs],
        scratch_shapes=scratch,
        input_output_aliases=aliases or {},
        compiler_params=pltpu.CompilerParams(vmem_limit_bytes=mib * MIB),
    )(*[array for array, _ in inputs])


def swap(x, bit):
    count = lax.axis_size("lon")
    return lax.ppermute(x, "lon", [(i, i ^ (1 << bit)) for i in range(count)])


def sum_over_lon(x, upward):
    bits = lax.axis_size("lon").bit_length() - 1
    for i in range(bits):
        got = swap(x, i if upward else bits - 1 - i)
        if i == bits - 1:
            return x, got
        x = x + got


def lat_ring(bands, ways, turn):
    pairs = []
    for band in range(bands):
        for l in range(ways):
            east = l < ways // 2
            other = (l + ways // 2) % ways
            step = 1 if east == (turn == 0) else -1
            to = (band + step, l) if 0 <= band + step < bands else (band, other)
            pairs.append((l * bands + band, to[1] * bands + to[0]))
    return pairs


def on_device(tracer, zonal, meridional, cutoff_wave, polar_mask):
    levels, rows, cells = tracer.shape
    ways, bands = lax.axis_size("lon"), lax.axis_size("lat")
    width = wide(cells)
    total = cells * ways
    tables, backs = (jnp.asarray(x) for x in wave_tables(cells, ways))
    lon, band = lax.axis_index("lon"), lax.axis_index("lat")
    info = jnp.stack([lon, jnp.int32(ways), band, jnp.int32(bands)]).astype(jnp.int32)
    parts = levels // SUB
    steps = SUB // GROUP
    winds = (tracer, zonal, meridional)
    cut = jnp.where(polar_mask == 1, cutoff_wave, -1)
    cut_row = cut[None, :]
    ring0, ring1, own = call(
        edge_kernel,
        [(info, SMEM), (cut_row, VMEM), *[(x, HBM) for x in winds]],
        [(shape(4, levels, width), VMEM), (shape(4, levels, width), VMEM), (shape(2, levels, width), VMEM)],
        [pltpu.VMEM((10, levels, cells), F32), pltpu.SemaphoreType.DMA((10,))],
        FIRST_MIB,
    )
    ring = ("lon", "lat")
    got0 = lax.ppermute(ring0, ring, lat_ring(bands, ways, 0))
    got1 = lax.ppermute(ring1, ring, lat_ring(bands, ways, 1))

    grid = shape(SUB, rows, width)
    coef = shape(2, SUB * rows, KMAX)
    edge = shape(SUB, KMAX)
    flows = [(shape(4, SUB, width), VMEM), (shape(2, SUB, width), VMEM), (shape(2, SUB, KMAX), VMEM)]
    head = 5 + ways

    def room(what):
        return pltpu.VMEM(what.shape, what.dtype)

    buffer = pltpu.VMEM((SUB, rows, cells), F32)
    table_shape, back_shape = (shape(*x.shape[1:], dtype=BF16) for x in (tables, backs))
    sems = pltpu.SemaphoreType.DMA
    moved_a, coef_a, edge_a, table, back, kept = call(
        functools.partial(first_kernel, 0, cells),
        [(info, SMEM), (cut_row, VMEM), *[(x, HBM) for x in (*winds, tables, backs)]],
        [*[(x, VMEM) for x in (grid, coef, edge, table_shape, back_shape)], (shape(1, dtype=jnp.int32), SMEM)],
        [buffer, buffer, buffer, sems((3, SUB)), sems((2,))],
        FIRST_MIB,
    )

    def rest(limit, info, cut, cut_row, tracer, zonal, meridional, own, got0, got1, moved_a, coef_a, edge_a, table, back):
        pay = (shape(limit + head + 2, SUB, KMAX), VMEM)
        around = [(x, VMEM) for x in (own, got0, got1, table)]
        scalars = [(info, SMEM), (cut, SMEM)]
        joined = [(moved_a, *call(
            functools.partial(join_kernel, 0, cells, ways),
            [*scalars, (coef_a, VMEM), (edge_a, VMEM), *around],
            [*flows, pay],
            [room(coef)],
            8,
        ))]
        sums = [sum_over_lon(joined[0][4], True)]
        for part in range(1, parts):
            joined.append(call(
                functools.partial(first_join_kernel, part * SUB, cells, ways),
                [*scalars, *[(x, HBM) for x in (tracer, zonal, meridional)], *around],
                [(grid, VMEM), *flows, pay],
                [buffer, buffer, buffer, room(coef), room(edge), sems((3, SUB))],
                20,
            ))
            sums.append(sum_over_lon(joined[part][4], True))
        seconds = []
        for part in range(parts):
            moved, flow, edge_v, edge_cut, _ = joined[part]
            seconds.append(call(
                functools.partial(second_kernel, part * SUB, total, cells, ways),
                [*scalars, *[(x, VMEM) for x in (cut_row, *sums[part], flow, edge_v, edge_cut, moved, table, back)],
                 (zonal, VMEM), (meridional, VMEM)],
                [(grid, VMEM), (shape(limit + ways + 2, SUB, KMAX), VMEM)],
                [room(coef), room(coef), pltpu.VMEM((2, SUB, width), F32),
                 pltpu.VMEM((2 * SUB, 2 * KMAX), F32), room(edge), room(edge), room(grid)],
                20,
            ))
        sums = [sum_over_lon(x[1], True) for x in seconds]
        out = []
        for part in range(parts):
            out = call(
                functools.partial(third_kernel, part * SUB, total, cells, ways),
                [*scalars, *[(x, VMEM) for x in (cut_row, *sums[part], seconds[part][0], back)],
                 *[(x, HBM) for x in out]],
                [(shape(levels, rows, cells), HBM)],
                [room(coef), room(edge), buffer, sems((steps,))],
                12,
                {7: 0} if part else None,
            )
        return out[0]

    limits = sorted({min(-(-x * rows // 64), 2 * rows) for x in LIMITS})
    choice = sum((kept[0] > x).astype(jnp.int32) for x in limits[:-1])
    return lax.switch(
        choice, [functools.partial(rest, x) for x in limits],
        info, cut, cut_row, tracer, zonal, meridional, own, got0, got1, moved_a, coef_a, edge_a, table, back,
    )


def solution(mesh):
    placed = (
        P(None, "lat", "lon"),
        P(None, "lat", "lon"),
        P(None, "lat", "lon"),
        P("lat"),
        P("lat"),
    )
    return jax.shard_map(
        on_device, mesh=mesh, in_specs=placed, out_specs=P(None, "lat", "lon"), check_vma=False
    )
```

```python
import functools

import jax
import jax.numpy as jnp
import ml_dtypes
import numpy as np
from jax import lax
from jax.experimental import pallas as pl
from jax.experimental.pallas import tpu as pltpu
from jax.sharding import PartitionSpec as P

KMAX = 128
HALF = KMAX // 2
DIFFUSION = 0.1
GROUP = 4
SUB = 8
FIRST_MIB = 52
LIMITS = (88, 128)
F32 = jnp.float32
BF16 = jnp.bfloat16
MIB = 1024 * 1024


def wide(cells):
    return -(-(cells + 2) // 128) * 128


def split_np(values):
    high = values.astype(ml_dtypes.bfloat16)
    low = (values - high.astype(np.float64)).astype(ml_dtypes.bfloat16)
    return high, low


@functools.lru_cache(maxsize=None)
def wave_tables(cells, ways):
    total = cells * ways
    width = wide(cells)
    lane = np.arange(width)
    start = np.arange(ways)[:, None] * cells
    place = np.where(lane == width - 1, -1, lane)[None, :] + start
    used = (lane <= cells) | (lane == width - 1)
    column = np.arange(2 * KMAX)
    wave = column // KMAX * HALF + column % HALF
    sine = column % KMAX // HALF
    angle = (place[:, :, None] * wave[None, None, :] % total) * (2.0 * np.pi / total)
    table = np.where(sine == 1, np.sin(angle), np.cos(angle))
    project = split_np(np.where(used[None, :, None], table, 0.0))
    inside = np.where((lane < cells)[None, :, None], table, 0.0).transpose(0, 2, 1)
    rebuild = split_np(inside)
    return np.concatenate(project, axis=2), np.concatenate(rebuild, axis=1)


def split(x):
    high = x.astype(BF16)
    return high, (x - high.astype(F32)).astype(BF16)


def project(x, table):
    high, low = split(x)
    both = jnp.dot(high, table, preferred_element_type=F32)
    cross = jnp.dot(low, table[:, : 2 * KMAX], preferred_element_type=F32)
    return both[:, : 2 * KMAX] + both[:, 2 * KMAX :] + cross


def rebuild(coefficients, table):
    high, low = split(coefficients)
    both = jnp.dot(jnp.concatenate([high, high], axis=1), table, preferred_element_type=F32)
    return both + jnp.dot(low, table[: 2 * KMAX], preferred_element_type=F32)


def padded(x, width):
    return jnp.concatenate([x, jnp.zeros((x.shape[0], width - x.shape[1]), F32)], axis=1)


def along_lon(s, u):
    width = s.shape[1]
    spread = DIFFUSION * s
    carry = (0.5 * u) * s
    return (
        (1.0 - 4.0 * DIFFUSION) * s
        + pltpu.roll(spread - carry, width - 1, 1)
        + pltpu.roll(spread + carry, 1, 1)
    )


def moved_rows(s, u, v):
    rows = s.shape[0]
    spread = DIFFUSION * s
    carry = (0.5 * v) * s
    row = lax.broadcasted_iota(jnp.int32, s.shape, 0)
    from_next = jnp.where(row == rows - 1, 0.0, pltpu.roll(spread - carry, rows - 1, 0))
    from_last = jnp.where(row == 0, 0.0, pltpu.roll(spread + carry, 1, 0))
    return along_lon(s, u) + from_next + from_last


def put_halves(ref, at, value):
    for half in range(2):
        ref[half, at, :] = value[:, half * KMAX : (half + 1) * KMAX]


def both_halves(ref, at):
    return jnp.concatenate([ref[0, at, :], ref[1, at, :]], axis=1)


def southward(s, v):
    return DIFFUSION * s + (0.5 * v) * s


def northward(s, v):
    return DIFFUSION * s - (0.5 * v) * s


def edge_kernel(
    info_ref, cut_ref, s_ref, u_ref, v_ref, ring0_ref, ring1_ref, own_ref, rows_ref, sem,
):
    levels, width = own_ref.shape[1:]
    rows = cut_ref.shape[1]
    near = info_ref[0] < info_ref[1] // 2
    wanted = [(h, at) for at in (0, rows - 1) for h in (s_ref, u_ref, v_ref)]
    wanted += [(h, at) for at in (1, rows - 2) for h in (s_ref, v_ref)]
    copies = [
        pltpu.make_async_copy(h.at[:, at, :], rows_ref.at[i], sem.at[i]) for i, (h, at) in enumerate(wanted)
    ]
    every(copies, "start")
    every(copies, "wait")
    cut = cut_ref[...]
    sides = []
    for side, (flow, row) in enumerate(((northward, 0), (southward, rows - 1))):
        s, u, v = (rows_ref[3 * side + i] for i in range(3))
        tail = jnp.broadcast_to(cut[:, row : row + 1].astype(F32), (levels, width - s.shape[1]))
        beyond = flow(rows_ref[6 + 2 * side], rows_ref[7 + 2 * side])
        sides.append([jnp.concatenate([s, tail], axis=1), padded(u, width), padded(v, width), padded(beyond, width)])
        own_ref[side] = padded(flow(s, v), width)
    for i in range(4):
        ring0_ref[i] = jnp.where(near, sides[1][i], sides[0][i])
        ring1_ref[i] = jnp.where(near, sides[0][i], sides[1][i])


def level_copies(hbm_refs, buffers, sem, first, level):
    return [
        pltpu.make_async_copy(h.at[first + level], b.at[level], sem.at[q, level])
        for q, (h, b) in enumerate(zip(hbm_refs, buffers))
    ]


def every(copies, act):
    for copy in copies:
        getattr(copy, act)()


def group_store(buffer, hbm_ref, sem, first, i):
    return pltpu.make_async_copy(
        buffer.at[pl.ds(i * GROUP, GROUP)], hbm_ref.at[pl.ds(first + i * GROUP, GROUP)], sem.at[i]
    )


def is_diagonal(rows, lanes):
    lane = lax.broadcasted_iota(jnp.int32, (rows, lanes), 1)
    return lax.broadcasted_iota(jnp.int32, (rows, lanes), 0) == lax.rem(lane, rows)


def outflow(tile, cells, width):
    rows = tile.shape[0]
    at = cells - (width - 128)
    lane = lax.broadcasted_iota(jnp.int32, tile.shape, 1)
    both = jnp.where(lane < rows, tile[:, at : at + 1], tile[:, 127:128])
    return jnp.sum(jnp.where(is_diagonal(*tile.shape), both, 0.0), axis=0, keepdims=True)


def column(row):
    rows = row.shape[1]
    spread = jnp.broadcast_to(row, (rows, rows))
    return jnp.sum(jnp.where(is_diagonal(rows, rows), spread, 0.0), axis=1, keepdims=True)


def pack_rows(cut_ref, source_ref, first, out_ref):
    rows = cut_ref.shape[0]

    def body(r, unit):
        cut = cut_ref[r]
        for half in range(2):
            out_ref[unit + half] = source_ref[half, pl.ds(r, SUB, stride=rows), :]
        return unit + (cut >= 0).astype(jnp.int32) + (cut >= HALF).astype(jnp.int32)

    lax.fori_loop(0, rows, body, first, unroll=8)


def scaled(x, half, cut, total):
    lane = lax.broadcasted_iota(jnp.int32, (SUB, KMAX), 1)
    wave = half * HALF + lane % HALF
    scale = jnp.where(wave == 0, 1.0 / total, 2.0 / total)
    return jnp.where(wave <= cut, x * scale, 0.0)


def unpack_rows(cut_ref, a_ref, b_ref, first, total, out_ref):
    rows = cut_ref.shape[0]
    last = a_ref.shape[0] - 1

    def body(r, unit):
        cut = cut_ref[r]
        for half in range(2):
            at = jnp.minimum(unit + half, last)
            out_ref[half, pl.ds(r, SUB, stride=rows), :] = scaled(a_ref[at] + b_ref[at], half, cut, total)
        return unit + (cut >= 0).astype(jnp.int32) + (cut >= HALF).astype(jnp.int32)

    lax.fori_loop(0, rows, body, first, unroll=8)


def put_slots(out_ref, first, ways, lon, value):
    for i in range(ways):
        out_ref[first + i] = jnp.zeros(value.shape, F32)
    out_ref[first + lon] = value


def inflow(a_ref, b_ref, first, ways, lon, rows, place_ref):
    west, east = first + lax.rem(lon + ways - 1, ways), first + lax.rem(lon + 1, ways)
    lane = lax.broadcasted_iota(jnp.int32, (SUB, 2 * rows), 1)
    place_ref[...] = jnp.where(lane < rows, a_ref[west] + b_ref[west], a_ref[east] + b_ref[east])


def loop(count, body):
    def step(i, _):
        body(i)
        return 0

    lax.fori_loop(0, count, step, 0)


def project_groups(x_ref, table_ref, coef_ref):
    levels, rows, width = x_ref.shape

    def body(i):
        x = x_ref[pl.ds(i * GROUP, GROUP)].reshape(GROUP * rows, width)
        put_halves(coef_ref, pl.ds(i * GROUP * rows, GROUP * rows), project(x, table_ref[...]))

    loop(levels // GROUP, body)


def first_body(first, cells, hbm_refs, buffers, sem, moved_ref, coef_ref, edge_ref, table_ref, ready=None):
    levels, rows, width = moved_ref.shape

    def one(level):
        every(level_copies(hbm_refs, buffers, sem, first, level), "wait")
        moved_ref[level] = moved_rows(*[padded(b[level], width) for b in buffers])
        edge_ref[pl.ds(level, 1), :] = outflow(moved_ref[level, :, width - 128 :], cells, width)

    loop(levels, one)
    if ready is not None:
        ready.wait()
    project_groups(moved_ref, table_ref, coef_ref)


def first_kernel(
    first, cells, info_ref, cut_row_ref, s_ref, u_ref, v_ref, tables_ref, backs_ref,
    moved_ref, coef_ref, edge_ref, table_ref, back_ref, kept_ref, s_buf, u_buf, v_buf, sem, table_sem,
):
    hbm_refs, buffers = (s_ref, u_ref, v_ref), (s_buf, u_buf, v_buf)
    lon = info_ref[0]
    ready = pltpu.make_async_copy(tables_ref.at[lon], table_ref, table_sem.at[0])
    later = pltpu.make_async_copy(backs_ref.at[lon], back_ref, table_sem.at[1])
    half = SUB // 2
    loop(half, lambda level: every(level_copies(hbm_refs, buffers, sem, first, level), "start"))
    ready.start()
    loop(half, lambda level: every(level_copies(hbm_refs, buffers, sem, first, level + half), "start"))
    later.start()
    cut = cut_row_ref[...]
    kept_ref[0] = jnp.sum((cut >= 0).astype(jnp.int32) + (cut >= HALF).astype(jnp.int32))
    first_body(first, cells, hbm_refs, buffers, sem, moved_ref, coef_ref, edge_ref, table_ref, ready)
    later.wait()


def join_flows(first, cells, info_ref, own_ref, ring0_ref, ring1_ref, flow_ref, edge_v_ref, edge_cut_ref):
    levels, width = flow_ref.shape[1:]
    at = slice(first, first + levels)
    near = info_ref[0] < info_ref[1] // 2
    lane = lax.broadcasted_iota(jnp.int32, (levels, width), 1)
    for side in range(2):
        got = [jnp.where(near == (side == 0), ring0_ref[i, at, :], ring1_ref[i, at, :]) for i in range(4)]
        edge_cut_ref[side] = jnp.broadcast_to(got[0][:, cells : cells + 1], (levels, KMAX))
        s = jnp.where(lane < cells, got[0], 0.0)
        pole = info_ref[2] == (0 if side == 0 else info_ref[3] - 1)
        v = jnp.where(pole, -got[2], got[2])
        edge_v_ref[side] = v
        flow_ref[side] = southward(s, v) if side == 0 else northward(s, v)
        flow_ref[2 + side] = along_lon(s, got[1]) + got[3] + own_ref[side, at, :]


def join_body(cells, info_ref, cut_ref, ways, coef_ref, edge_ref, flow_ref, table_ref, out_ref):
    rows = cut_ref.shape[0]
    levels, width = flow_ref.shape[1:]
    lon = info_ref[0]
    extra = project(flow_ref[...].reshape(4 * levels, width), table_ref[...])
    first = pl.ds(0, SUB, stride=rows)
    last = pl.ds(rows - 1, SUB, stride=rows)
    for half in range(2):
        part = extra[:, half * KMAX : (half + 1) * KMAX]
        coef_ref[half, first, :] = coef_ref[half, first, :] + part[:levels]
        coef_ref[half, last, :] = coef_ref[half, last, :] + part[levels : 2 * levels]
        out_ref[half] = part[2 * levels : 3 * levels]
        out_ref[2 + half] = part[3 * levels :]
    put_slots(out_ref, 4, ways, lon, edge_ref[...])
    lane = lax.broadcasted_iota(jnp.int32, (SUB, KMAX), 1)
    unit = jnp.zeros((SUB, KMAX), F32)
    for side in range(2):
        for way, at in enumerate((cells, width - 1)):
            unit = jnp.where(lane == 4 * lon + 2 * side + way, flow_ref[2 + side][:, at : at + 1], unit)
    out_ref[4 + ways] = unit
    pack_rows(cut_ref, coef_ref, 5 + ways, out_ref)


def join_kernel(
    first, cells, ways,
    info_ref, cut_ref, coef_in_ref, edge_ref, own_ref, ring0_ref, ring1_ref, table_ref,
    flow_ref, edge_v_ref, edge_cut_ref, out_ref, coef_ref,
):
    coef_ref[...] = coef_in_ref[...]
    join_flows(first, cells, info_ref, own_ref, ring0_ref, ring1_ref, flow_ref, edge_v_ref, edge_cut_ref)
    join_body(cells, info_ref, cut_ref, ways, coef_ref, edge_ref, flow_ref, table_ref, out_ref)


def first_join_kernel(
    first, cells, ways,
    info_ref, cut_ref, s_ref, u_ref, v_ref, own_ref, ring0_ref, ring1_ref, table_ref,
    moved_ref, flow_ref, edge_v_ref, edge_cut_ref, out_ref,
    s_buf, u_buf, v_buf, coef_ref, edge_ref, sem,
):
    hbm_refs, buffers = (s_ref, u_ref, v_ref), (s_buf, u_buf, v_buf)
    loop(SUB, lambda level: every(level_copies(hbm_refs, buffers, sem, first, level), "start"))
    join_flows(first, cells, info_ref, own_ref, ring0_ref, ring1_ref, flow_ref, edge_v_ref, edge_cut_ref)
    first_body(first, cells, hbm_refs, buffers, sem, moved_ref, coef_ref, edge_ref, table_ref)
    join_body(cells, info_ref, cut_ref, ways, coef_ref, edge_ref, flow_ref, table_ref, out_ref)


def closed(x, west, east, cells):
    end = x.shape[1] - 128
    lane = lax.broadcasted_iota(jnp.int32, (x.shape[0], 128), 1)
    head = x[:, :128] + jnp.where(lane == 0, west, 0.0)
    tail = x[:, end:] + jnp.where(lane == cells - 1 - end, east, 0.0)
    return jnp.concatenate([head, x[:, 128:end], jnp.where(lane < cells - end, tail, 0.0)], axis=1)


def closed_groups(cells, cut_row_ref, in_ref, coef_ref, back_ref, moved_ref, flow_ref, out_ref, after=None):
    levels, rows, width = moved_ref.shape
    filtered = column(cut_row_ref[...].astype(F32)) >= 0.0
    row = lax.broadcasted_iota(jnp.int32, (8, width), 0)

    def body(i):
        smooth = rebuild(both_halves(coef_ref, pl.ds(i * GROUP * rows, GROUP * rows)), back_ref[...])
        for g in range(GROUP):
            level = i * GROUP + g
            came = in_ref[pl.ds(level, 1), :]
            plain = closed(moved_ref[level], column(came[:, :rows]), column(came[:, rows:]), cells)
            s = jnp.where(filtered, smooth[g * rows : (g + 1) * rows], plain)
            out_ref[level] = s[:, : out_ref.shape[2]]
            if flow_ref is not None:
                for side, at, edge in ((0, 0, 0), (1, rows - 8, 7)):
                    plain_edge = (row == edge) & jnp.logical_not(filtered[at : at + 8])
                    out_ref[level, at : at + 8, :] = out_ref[level, at : at + 8, :] + jnp.where(
                        plain_edge, flow_ref[side, pl.ds(level, 1), :], 0.0
                    )
        if after is not None:
            after(i)

    loop(levels // GROUP, body)


def second_kernel(
    first, total, cells, ways,
    info_ref, cut_ref, cut_row_ref, a_ref, b_ref, flow_ref, edge_v_ref, edge_cut_ref,
    moved_ref, table_ref, back_ref, u_ref, v_ref,
    out_ref, pay_ref,
    coef_ref, sum_ref, step_ref, edge_ref, in_ref, place_ref, s_ref,
):
    rows = cut_ref.shape[0]
    levels, _, width = out_ref.shape
    lon = info_ref[0]

    unpack_rows(cut_ref, a_ref, b_ref, 5 + ways, total, coef_ref)
    for side in range(2):
        for half in range(2):
            at = 2 * side + half
            cut = edge_cut_ref[side].astype(jnp.int32)
            edge_ref[side * levels : (side + 1) * levels, half * KMAX : (half + 1) * KMAX] = scaled(
                a_ref[at] + b_ref[at], half, cut, total
            )
    inflow(a_ref, b_ref, 4, ways, lon, rows, in_ref)
    unit = a_ref[4 + ways] + b_ref[4 + ways]
    lane = lax.broadcasted_iota(jnp.int32, (SUB, KMAX), 1)
    smooth = rebuild(edge_ref[...], back_ref[...])
    for side in range(2):
        came = [
            jnp.sum(jnp.where(lane == 4 * lax.rem(lon + ways + step, ways) + 2 * side + way, unit, 0.0), axis=1, keepdims=True)
            for way, step in enumerate((-1, 1))
        ]
        plain = closed(flow_ref[2 + side], came[0], came[1], cells)
        filtered = edge_cut_ref[side][:, 0:1] >= 0.0
        s = jnp.where(filtered, smooth[side * levels : (side + 1) * levels], plain)
        step_ref[side] = (southward if side == 0 else northward)(s, edge_v_ref[side])
    closed_groups(cells, cut_row_ref, in_ref, coef_ref, back_ref, moved_ref, flow_ref, s_ref)

    def one(level):
        row = pl.ds(level, 1)
        out_ref[level] = moved_rows(s_ref[level], padded(u_ref[first + level], width), padded(v_ref[first + level], width))
        out_ref[level, 0:1, :] = out_ref[level, 0:1, :] + step_ref[0, row, :]
        out_ref[level, rows - 1 : rows, :] = out_ref[level, rows - 1 : rows, :] + step_ref[1, row, :]
        place_ref[row, :] = outflow(out_ref[level, :, width - 128 :], cells, width)

    lax.fori_loop(0, levels, lambda i, _: (one(i), 0)[1], 0, unroll=2)
    project_groups(out_ref, table_ref, sum_ref)
    put_slots(pay_ref, 0, ways, lon, place_ref[...])
    pack_rows(cut_ref, sum_ref, ways, pay_ref)


def third_kernel(
    first, total, cells, ways, info_ref, cut_ref, cut_row_ref, a_ref, b_ref, moved_ref, back_ref, *refs
):
    out_ref, coef_ref, in_ref, buffer, out_sem = refs[-5:]
    rows = cut_ref.shape[0]
    levels = moved_ref.shape[0]
    unpack_rows(cut_ref, a_ref, b_ref, ways, total, coef_ref)
    inflow(a_ref, b_ref, 0, ways, info_ref[0], rows, in_ref)
    closed_groups(
        cells, cut_row_ref, in_ref, coef_ref, back_ref, moved_ref, None, buffer,
        lambda i: group_store(buffer, out_ref, out_sem, first, i).start(),
    )
    loop(levels // GROUP, lambda i: group_store(buffer, out_ref, out_sem, first, i).wait())


SMEM = pl.BlockSpec(memory_space=pltpu.SMEM)
VMEM = pl.BlockSpec(memory_space=pltpu.VMEM)
HBM = pl.BlockSpec(memory_space=pltpu.HBM)


def shape(*dims, dtype=F32):
    return jax.ShapeDtypeStruct(dims, dtype)


def call(kernel, inputs, outputs, scratch, mib, aliases=None):
    return pl.pallas_call(
        kernel,
        in_specs=[spec for _, spec in inputs],
        out_specs=[spec for _, spec in outputs],
        out_shape=[what for what, _ in outputs],
        scratch_shapes=scratch,
        input_output_aliases=aliases or {},
        compiler_params=pltpu.CompilerParams(vmem_limit_bytes=mib * MIB),
    )(*[array for array, _ in inputs])


def swap(x, bit):
    count = lax.axis_size("lon")
    return lax.ppermute(x, "lon", [(i, i ^ (1 << bit)) for i in range(count)])


def sum_over_lon(x, upward):
    bits = lax.axis_size("lon").bit_length() - 1
    for i in range(bits):
        got = swap(x, i if upward else bits - 1 - i)
        if i == bits - 1:
            return x, got
        x = x + got


def lat_ring(bands, ways, turn):
    pairs = []
    for band in range(bands):
        for l in range(ways):
            east = l < ways // 2
            other = (l + ways // 2) % ways
            step = 1 if east == (turn == 0) else -1
            to = (band + step, l) if 0 <= band + step < bands else (band, other)
            pairs.append((l * bands + band, to[1] * bands + to[0]))
    return pairs


def on_device(tracer, zonal, meridional, cutoff_wave, polar_mask):
    levels, rows, cells = tracer.shape
    ways, bands = lax.axis_size("lon"), lax.axis_size("lat")
    width = wide(cells)
    total = cells * ways
    tables, backs = (jnp.asarray(x) for x in wave_tables(cells, ways))
    lon, band = lax.axis_index("lon"), lax.axis_index("lat")
    info = jnp.stack([lon, jnp.int32(ways), band, jnp.int32(bands)]).astype(jnp.int32)
    parts = levels // SUB
    steps = SUB // GROUP
    winds = (tracer, zonal, meridional)
    cut = jnp.where(polar_mask == 1, cutoff_wave, -1)
    cut_row = cut[None, :]
    ring0, ring1, own = call(
        edge_kernel,
        [(info, SMEM), (cut_row, VMEM), *[(x, HBM) for x in winds]],
        [(shape(4, levels, width), VMEM), (shape(4, levels, width), VMEM), (shape(2, levels, width), VMEM)],
        [pltpu.VMEM((10, levels, cells), F32), pltpu.SemaphoreType.DMA((10,))],
        FIRST_MIB,
    )
    ring = ("lon", "lat")
    got0 = lax.ppermute(ring0, ring, lat_ring(bands, ways, 0))
    got1 = lax.ppermute(ring1, ring, lat_ring(bands, ways, 1))

    grid = shape(SUB, rows, width)
    coef = shape(2, SUB * rows, KMAX)
    edge = shape(SUB, KMAX)
    flows = [(shape(4, SUB, width), VMEM), (shape(2, SUB, width), VMEM), (shape(2, SUB, KMAX), VMEM)]
    head = 5 + ways

    def room(what):
        return pltpu.VMEM(what.shape, what.dtype)

    buffer = pltpu.VMEM((SUB, rows, cells), F32)
    table_shape, back_shape = (shape(*x.shape[1:], dtype=BF16) for x in (tables, backs))
    sems = pltpu.SemaphoreType.DMA
    moved_a, coef_a, edge_a, table, back, kept = call(
        functools.partial(first_kernel, 0, cells),
        [(info, SMEM), (cut_row, VMEM), *[(x, HBM) for x in (*winds, tables, backs)]],
        [*[(x, VMEM) for x in (grid, coef, edge, table_shape, back_shape)], (shape(1, dtype=jnp.int32), SMEM)],
        [buffer, buffer, buffer, sems((3, SUB)), sems((2,))],
        FIRST_MIB,
    )

    def rest(limit, info, cut, cut_row, tracer, zonal, meridional, own, got0, got1, moved_a, coef_a, edge_a, table, back):
        pay = (shape(limit + head + 2, SUB, KMAX), VMEM)
        around = [(x, VMEM) for x in (own, got0, got1, table)]
        scalars = [(info, SMEM), (cut, SMEM)]
        joined = [(moved_a, *call(
            functools.partial(join_kernel, 0, cells, ways),
            [*scalars, (coef_a, VMEM), (edge_a, VMEM), *around],
            [*flows, pay],
            [room(coef)],
            8,
        ))]
        sums = [sum_over_lon(joined[0][4], True)]
        for part in range(1, parts):
            joined.append(call(
                functools.partial(first_join_kernel, part * SUB, cells, ways),
                [*scalars, *[(x, HBM) for x in (tracer, zonal, meridional)], *around],
                [(grid, VMEM), *flows, pay],
                [buffer, buffer, buffer, room(coef), room(edge), sems((3, SUB))],
                20,
            ))
            sums.append(sum_over_lon(joined[part][4], True))
        seconds = []
        for part in range(parts):
            moved, flow, edge_v, edge_cut, _ = joined[part]
            seconds.append(call(
                functools.partial(second_kernel, part * SUB, total, cells, ways),
                [*scalars, *[(x, VMEM) for x in (cut_row, *sums[part], flow, edge_v, edge_cut, moved, table, back)],
                 (zonal, VMEM), (meridional, VMEM)],
                [(grid, VMEM), (shape(limit + ways + 2, SUB, KMAX), VMEM)],
                [room(coef), room(coef), pltpu.VMEM((2, SUB, width), F32),
                 pltpu.VMEM((2 * SUB, 2 * KMAX), F32), room(edge), room(edge), room(grid)],
                20,
            ))
        sums = [sum_over_lon(x[1], True) for x in seconds]
        out = []
        for part in range(parts):
            out = call(
                functools.partial(third_kernel, part * SUB, total, cells, ways),
                [*scalars, *[(x, VMEM) for x in (cut_row, *sums[part], seconds[part][0], back)],
                 *[(x, HBM) for x in out]],
                [(shape(levels, rows, cells), HBM)],
                [room(coef), room(edge), buffer, sems((steps,))],
                12,
                {7: 0} if part else None,
            )
        return out[0]

    limits = sorted({min(-(-x * rows // 64), 2 * rows) for x in LIMITS})
    choice = sum((kept[0] > x).astype(jnp.int32) for x in limits[:-1])
    return lax.switch(
        choice, [functools.partial(rest, x) for x in limits],
        info, cut, cut_row, tracer, zonal, meridional, own, got0, got1, moved_a, coef_a, edge_a, table, back,
    )


def solution(mesh):
    placed = (
        P(None, "lat", "lon"),
        P(None, "lat", "lon"),
        P(None, "lat", "lon"),
        P("lat"),
        P("lat"),
    )
    return jax.shard_map(
        on_device, mesh=mesh, in_specs=placed, out_specs=P(None, "lat", "lon"), check_vma=False
    )
```

```python
import functools

import jax
import jax.numpy as jnp
import ml_dtypes
import numpy as np
from jax import lax
from jax.experimental import pallas as pl
from jax.experimental.pallas import tpu as pltpu
from jax.sharding import PartitionSpec as P

KMAX = 128
HALF = KMAX // 2
DIFFUSION = 0.1
GROUP = 4
SUB = 8
FIRST_MIB = 52
LIMITS = (86, 128)
F32 = jnp.float32
BF16 = jnp.bfloat16
MIB = 1024 * 1024


def wide(cells):
    return -(-(cells + 2) // 128) * 128


def split_np(values):
    high = values.astype(ml_dtypes.bfloat16)
    low = (values - high.astype(np.float64)).astype(ml_dtypes.bfloat16)
    return high, low


@functools.lru_cache(maxsize=None)
def wave_tables(cells, ways):
    total = cells * ways
    width = wide(cells)
    lane = np.arange(width)
    start = np.arange(ways)[:, None] * cells
    place = np.where(lane == width - 1, -1, lane)[None, :] + start
    used = (lane <= cells) | (lane == width - 1)
    column = np.arange(2 * KMAX)
    wave = column // KMAX * HALF + column % HALF
    sine = column % KMAX // HALF
    angle = (place[:, :, None] * wave[None, None, :] % total) * (2.0 * np.pi / total)
    table = np.where(sine == 1, np.sin(angle), np.cos(angle))
    project = split_np(np.where(used[None, :, None], table, 0.0))
    inside = np.where((lane < cells)[None, :, None], table, 0.0).transpose(0, 2, 1)
    rebuild = split_np(inside)
    return np.concatenate(project, axis=2), np.concatenate(rebuild, axis=1)


def split(x):
    high = x.astype(BF16)
    return high, (x - high.astype(F32)).astype(BF16)


def project(x, table):
    high, low = split(x)
    both = jnp.dot(high, table, preferred_element_type=F32)
    cross = jnp.dot(low, table[:, : 2 * KMAX], preferred_element_type=F32)
    return both[:, : 2 * KMAX] + both[:, 2 * KMAX :] + cross


def rebuild(coefficients, table):
    high, low = split(coefficients)
    both = jnp.dot(jnp.concatenate([high, high], axis=1), table, preferred_element_type=F32)
    return both + jnp.dot(low, table[: 2 * KMAX], preferred_element_type=F32)


def padded(x, width):
    return jnp.concatenate([x, jnp.zeros((x.shape[0], width - x.shape[1]), F32)], axis=1)


def along_lon(s, u):
    width = s.shape[1]
    spread = DIFFUSION * s
    carry = (0.5 * u) * s
    return (
        (1.0 - 4.0 * DIFFUSION) * s
        + pltpu.roll(spread - carry, width - 1, 1)
        + pltpu.roll(spread + carry, 1, 1)
    )


def moved_rows(s, u, v):
    rows = s.shape[0]
    spread = DIFFUSION * s
    carry = (0.5 * v) * s
    row = lax.broadcasted_iota(jnp.int32, s.shape, 0)
    from_next = jnp.where(row == rows - 1, 0.0, pltpu.roll(spread - carry, rows - 1, 0))
    from_last = jnp.where(row == 0, 0.0, pltpu.roll(spread + carry, 1, 0))
    return along_lon(s, u) + from_next + from_last


def put_halves(ref, at, value):
    for half in range(2):
        ref[half, at, :] = value[:, half * KMAX : (half + 1) * KMAX]


def both_halves(ref, at):
    return jnp.concatenate([ref[0, at, :], ref[1, at, :]], axis=1)


def southward(s, v):
    return DIFFUSION * s + (0.5 * v) * s


def northward(s, v):
    return DIFFUSION * s - (0.5 * v) * s


def edge_kernel(
    info_ref, cut_ref, s_ref, u_ref, v_ref, ring0_ref, ring1_ref, own_ref, rows_ref, sem,
):
    levels, width = own_ref.shape[1:]
    rows = cut_ref.shape[1]
    near = info_ref[0] < info_ref[1] // 2
    wanted = [(h, at) for at in (0, rows - 1) for h in (s_ref, u_ref, v_ref)]
    wanted += [(h, at) for at in (1, rows - 2) for h in (s_ref, v_ref)]
    copies = [
        pltpu.make_async_copy(h.at[:, at, :], rows_ref.at[i], sem.at[i]) for i, (h, at) in enumerate(wanted)
    ]
    every(copies, "start")
    every(copies, "wait")
    cut = cut_ref[...]
    sides = []
    for side, (flow, row) in enumerate(((northward, 0), (southward, rows - 1))):
        s, u, v = (rows_ref[3 * side + i] for i in range(3))
        tail = jnp.broadcast_to(cut[:, row : row + 1].astype(F32), (levels, width - s.shape[1]))
        beyond = flow(rows_ref[6 + 2 * side], rows_ref[7 + 2 * side])
        sides.append([jnp.concatenate([s, tail], axis=1), padded(u, width), padded(v, width), padded(beyond, width)])
        own_ref[side] = padded(flow(s, v), width)
    for i in range(4):
        ring0_ref[i] = jnp.where(near, sides[1][i], sides[0][i])
        ring1_ref[i] = jnp.where(near, sides[0][i], sides[1][i])


def level_copies(hbm_refs, buffers, sem, first, level):
    return [
        pltpu.make_async_copy(h.at[first + level], b.at[level], sem.at[q, level])
        for q, (h, b) in enumerate(zip(hbm_refs, buffers))
    ]


def every(copies, act):
    for copy in copies:
        getattr(copy, act)()


def group_store(buffer, hbm_ref, sem, first, i):
    return pltpu.make_async_copy(
        buffer.at[pl.ds(i * GROUP, GROUP)], hbm_ref.at[pl.ds(first + i * GROUP, GROUP)], sem.at[i]
    )


def is_diagonal(rows, lanes):
    lane = lax.broadcasted_iota(jnp.int32, (rows, lanes), 1)
    return lax.broadcasted_iota(jnp.int32, (rows, lanes), 0) == lax.rem(lane, rows)


def outflow(tile, cells, width):
    rows = tile.shape[0]
    at = cells - (width - 128)
    lane = lax.broadcasted_iota(jnp.int32, tile.shape, 1)
    both = jnp.where(lane < rows, tile[:, at : at + 1], tile[:, 127:128])
    return jnp.sum(jnp.where(is_diagonal(*tile.shape), both, 0.0), axis=0, keepdims=True)


def column(row):
    rows = row.shape[1]
    spread = jnp.broadcast_to(row, (rows, rows))
    return jnp.sum(jnp.where(is_diagonal(rows, rows), spread, 0.0), axis=1, keepdims=True)


def pack_rows(cut_ref, source_ref, first, out_ref):
    rows = cut_ref.shape[0]

    def body(r, unit):
        cut = cut_ref[r]
        for half in range(2):
            out_ref[unit + half] = source_ref[half, pl.ds(r, SUB, stride=rows), :]
        return unit + (cut >= 0).astype(jnp.int32) + (cut >= HALF).astype(jnp.int32)

    lax.fori_loop(0, rows, body, first, unroll=8)


def scaled(x, half, cut, total):
    lane = lax.broadcasted_iota(jnp.int32, (SUB, KMAX), 1)
    wave = half * HALF + lane % HALF
    scale = jnp.where(wave == 0, 1.0 / total, 2.0 / total)
    return jnp.where(wave <= cut, x * scale, 0.0)


def unpack_rows(cut_ref, a_ref, b_ref, first, total, out_ref):
    rows = cut_ref.shape[0]
    last = a_ref.shape[0] - 1

    def body(r, unit):
        cut = cut_ref[r]
        for half in range(2):
            at = jnp.minimum(unit + half, last)
            out_ref[half, pl.ds(r, SUB, stride=rows), :] = scaled(a_ref[at] + b_ref[at], half, cut, total)
        return unit + (cut >= 0).astype(jnp.int32) + (cut >= HALF).astype(jnp.int32)

    lax.fori_loop(0, rows, body, first, unroll=8)


def put_slots(out_ref, first, ways, lon, value):
    for i in range(ways):
        out_ref[first + i] = jnp.zeros(value.shape, F32)
    out_ref[first + lon] = value


def inflow(a_ref, b_ref, first, ways, lon, rows, place_ref):
    west, east = first + lax.rem(lon + ways - 1, ways), first + lax.rem(lon + 1, ways)
    lane = lax.broadcasted_iota(jnp.int32, (SUB, 2 * rows), 1)
    place_ref[...] = jnp.where(lane < rows, a_ref[west] + b_ref[west], a_ref[east] + b_ref[east])


def loop(count, body):
    def step(i, _):
        body(i)
        return 0

    lax.fori_loop(0, count, step, 0)


def project_groups(x_ref, table_ref, coef_ref):
    levels, rows, width = x_ref.shape

    def body(i):
        x = x_ref[pl.ds(i * GROUP, GROUP)].reshape(GROUP * rows, width)
        put_halves(coef_ref, pl.ds(i * GROUP * rows, GROUP * rows), project(x, table_ref[...]))

    loop(levels // GROUP, body)


def first_body(first, cells, hbm_refs, buffers, sem, moved_ref, coef_ref, edge_ref, table_ref, ready=None):
    levels, rows, width = moved_ref.shape

    def one(level):
        every(level_copies(hbm_refs, buffers, sem, first, level), "wait")
        moved_ref[level] = moved_rows(*[padded(b[level], width) for b in buffers])
        edge_ref[pl.ds(level, 1), :] = outflow(moved_ref[level, :, width - 128 :], cells, width)

    loop(levels, one)
    if ready is not None:
        ready.wait()
    project_groups(moved_ref, table_ref, coef_ref)


def first_kernel(
    first, cells, info_ref, cut_row_ref, s_ref, u_ref, v_ref, tables_ref, backs_ref,
    moved_ref, coef_ref, edge_ref, table_ref, back_ref, kept_ref, s_buf, u_buf, v_buf, sem, table_sem,
):
    hbm_refs, buffers = (s_ref, u_ref, v_ref), (s_buf, u_buf, v_buf)
    lon = info_ref[0]
    ready = pltpu.make_async_copy(tables_ref.at[lon], table_ref, table_sem.at[0])
    later = pltpu.make_async_copy(backs_ref.at[lon], back_ref, table_sem.at[1])
    loop(SUB, lambda level: every(level_copies(hbm_refs, buffers, sem, first, level), "start"))
    ready.start()
    later.start()
    cut = cut_row_ref[...]
    kept_ref[0] = jnp.sum((cut >= 0).astype(jnp.int32) + (cut >= HALF).astype(jnp.int32))
    first_body(first, cells, hbm_refs, buffers, sem, moved_ref, coef_ref, edge_ref, table_ref, ready)
    later.wait()


def join_flows(first, cells, info_ref, own_ref, ring0_ref, ring1_ref, flow_ref, edge_v_ref, edge_cut_ref):
    levels, width = flow_ref.shape[1:]
    at = slice(first, first + levels)
    near = info_ref[0] < info_ref[1] // 2
    lane = lax.broadcasted_iota(jnp.int32, (levels, width), 1)
    for side in range(2):
        got = [jnp.where(near == (side == 0), ring0_ref[i, at, :], ring1_ref[i, at, :]) for i in range(4)]
        edge_cut_ref[side] = jnp.broadcast_to(got[0][:, cells : cells + 1], (levels, KMAX))
        s = jnp.where(lane < cells, got[0], 0.0)
        pole = info_ref[2] == (0 if side == 0 else info_ref[3] - 1)
        v = jnp.where(pole, -got[2], got[2])
        edge_v_ref[side] = v
        flow_ref[side] = southward(s, v) if side == 0 else northward(s, v)
        flow_ref[2 + side] = along_lon(s, got[1]) + got[3] + own_ref[side, at, :]


def join_body(cells, info_ref, cut_ref, ways, coef_ref, edge_ref, flow_ref, table_ref, out_ref):
    rows = cut_ref.shape[0]
    levels, width = flow_ref.shape[1:]
    lon = info_ref[0]
    extra = project(flow_ref[...].reshape(4 * levels, width), table_ref[...])
    first = pl.ds(0, SUB, stride=rows)
    last = pl.ds(rows - 1, SUB, stride=rows)
    for half in range(2):
        part = extra[:, half * KMAX : (half + 1) * KMAX]
        coef_ref[half, first, :] = coef_ref[half, first, :] + part[:levels]
        coef_ref[half, last, :] = coef_ref[half, last, :] + part[levels : 2 * levels]
        out_ref[half] = part[2 * levels : 3 * levels]
        out_ref[2 + half] = part[3 * levels :]
    put_slots(out_ref, 4, ways, lon, edge_ref[...])
    lane = lax.broadcasted_iota(jnp.int32, (SUB, KMAX), 1)
    unit = jnp.zeros((SUB, KMAX), F32)
    for side in range(2):
        for way, at in enumerate((cells, width - 1)):
            unit = jnp.where(lane == 4 * lon + 2 * side + way, flow_ref[2 + side][:, at : at + 1], unit)
    out_ref[4 + ways] = unit
    pack_rows(cut_ref, coef_ref, 5 + ways, out_ref)


def join_kernel(
    first, cells, ways,
    info_ref, cut_ref, coef_in_ref, edge_ref, own_ref, ring0_ref, ring1_ref, table_ref,
    flow_ref, edge_v_ref, edge_cut_ref, out_ref, coef_ref,
):
    coef_ref[...] = coef_in_ref[...]
    join_flows(first, cells, info_ref, own_ref, ring0_ref, ring1_ref, flow_ref, edge_v_ref, edge_cut_ref)
    join_body(cells, info_ref, cut_ref, ways, coef_ref, edge_ref, flow_ref, table_ref, out_ref)


def first_join_kernel(
    first, cells, ways,
    info_ref, cut_ref, s_ref, u_ref, v_ref, own_ref, ring0_ref, ring1_ref, table_ref,
    moved_ref, flow_ref, edge_v_ref, edge_cut_ref, out_ref,
    s_buf, u_buf, v_buf, coef_ref, edge_ref, sem,
):
    hbm_refs, buffers = (s_ref, u_ref, v_ref), (s_buf, u_buf, v_buf)
    loop(SUB, lambda level: every(level_copies(hbm_refs, buffers, sem, first, level), "start"))
    join_flows(first, cells, info_ref, own_ref, ring0_ref, ring1_ref, flow_ref, edge_v_ref, edge_cut_ref)
    first_body(first, cells, hbm_refs, buffers, sem, moved_ref, coef_ref, edge_ref, table_ref)
    join_body(cells, info_ref, cut_ref, ways, coef_ref, edge_ref, flow_ref, table_ref, out_ref)


def closed(x, west, east, cells):
    end = x.shape[1] - 128
    lane = lax.broadcasted_iota(jnp.int32, (x.shape[0], 128), 1)
    head = x[:, :128] + jnp.where(lane == 0, west, 0.0)
    tail = x[:, end:] + jnp.where(lane == cells - 1 - end, east, 0.0)
    return jnp.concatenate([head, x[:, 128:end], jnp.where(lane < cells - end, tail, 0.0)], axis=1)


def closed_groups(cells, cut_row_ref, in_ref, coef_ref, back_ref, moved_ref, flow_ref, out_ref, after=None):
    levels, rows, width = moved_ref.shape
    filtered = column(cut_row_ref[...].astype(F32)) >= 0.0
    row = lax.broadcasted_iota(jnp.int32, (8, width), 0)

    def body(i):
        smooth = rebuild(both_halves(coef_ref, pl.ds(i * GROUP * rows, GROUP * rows)), back_ref[...])
        for g in range(GROUP):
            level = i * GROUP + g
            came = in_ref[pl.ds(level, 1), :]
            plain = closed(moved_ref[level], column(came[:, :rows]), column(came[:, rows:]), cells)
            s = jnp.where(filtered, smooth[g * rows : (g + 1) * rows], plain)
            out_ref[level] = s[:, : out_ref.shape[2]]
            if flow_ref is not None:
                for side, at, edge in ((0, 0, 0), (1, rows - 8, 7)):
                    plain_edge = (row == edge) & jnp.logical_not(filtered[at : at + 8])
                    out_ref[level, at : at + 8, :] = out_ref[level, at : at + 8, :] + jnp.where(
                        plain_edge, flow_ref[side, pl.ds(level, 1), :], 0.0
                    )
        if after is not None:
            after(i)

    loop(levels // GROUP, body)


def second_kernel(
    first, total, cells, ways,
    info_ref, cut_ref, cut_row_ref, a_ref, b_ref, flow_ref, edge_v_ref, edge_cut_ref,
    moved_ref, table_ref, back_ref, u_ref, v_ref,
    out_ref, pay_ref,
    coef_ref, sum_ref, step_ref, edge_ref, in_ref, place_ref, s_ref,
):
    rows = cut_ref.shape[0]
    levels, _, width = out_ref.shape
    lon = info_ref[0]

    unpack_rows(cut_ref, a_ref, b_ref, 5 + ways, total, coef_ref)
    for side in range(2):
        for half in range(2):
            at = 2 * side + half
            cut = edge_cut_ref[side].astype(jnp.int32)
            edge_ref[side * levels : (side + 1) * levels, half * KMAX : (half + 1) * KMAX] = scaled(
                a_ref[at] + b_ref[at], half, cut, total
            )
    inflow(a_ref, b_ref, 4, ways, lon, rows, in_ref)
    unit = a_ref[4 + ways] + b_ref[4 + ways]
    lane = lax.broadcasted_iota(jnp.int32, (SUB, KMAX), 1)
    smooth = rebuild(edge_ref[...], back_ref[...])
    for side in range(2):
        came = [
            jnp.sum(jnp.where(lane == 4 * lax.rem(lon + ways + step, ways) + 2 * side + way, unit, 0.0), axis=1, keepdims=True)
            for way, step in enumerate((-1, 1))
        ]
        plain = closed(flow_ref[2 + side], came[0], came[1], cells)
        filtered = edge_cut_ref[side][:, 0:1] >= 0.0
        s = jnp.where(filtered, smooth[side * levels : (side + 1) * levels], plain)
        step_ref[side] = (southward if side == 0 else northward)(s, edge_v_ref[side])
    closed_groups(cells, cut_row_ref, in_ref, coef_ref, back_ref, moved_ref, flow_ref, s_ref)

    def one(level):
        row = pl.ds(level, 1)
        out_ref[level] = moved_rows(s_ref[level], padded(u_ref[first + level], width), padded(v_ref[first + level], width))
        out_ref[level, 0:1, :] = out_ref[level, 0:1, :] + step_ref[0, row, :]
        out_ref[level, rows - 1 : rows, :] = out_ref[level, rows - 1 : rows, :] + step_ref[1, row, :]
        place_ref[row, :] = outflow(out_ref[level, :, width - 128 :], cells, width)

    loop(levels, one)
    project_groups(out_ref, table_ref, sum_ref)
    put_slots(pay_ref, 0, ways, lon, place_ref[...])
    pack_rows(cut_ref, sum_ref, ways, pay_ref)


def third_kernel(
    first, total, cells, ways, info_ref, cut_ref, cut_row_ref, a_ref, b_ref, moved_ref, back_ref, *refs
):
    out_ref, coef_ref, in_ref, buffer, out_sem = refs[-5:]
    rows = cut_ref.shape[0]
    levels = moved_ref.shape[0]
    unpack_rows(cut_ref, a_ref, b_ref, ways, total, coef_ref)
    inflow(a_ref, b_ref, 0, ways, info_ref[0], rows, in_ref)
    closed_groups(
        cells, cut_row_ref, in_ref, coef_ref, back_ref, moved_ref, None, buffer,
        lambda i: group_store(buffer, out_ref, out_sem, first, i).start(),
    )
    loop(levels // GROUP, lambda i: group_store(buffer, out_ref, out_sem, first, i).wait())


SMEM = pl.BlockSpec(memory_space=pltpu.SMEM)
VMEM = pl.BlockSpec(memory_space=pltpu.VMEM)
HBM = pl.BlockSpec(memory_space=pltpu.HBM)


def shape(*dims, dtype=F32):
    return jax.ShapeDtypeStruct(dims, dtype)


def call(kernel, inputs, outputs, scratch, mib, aliases=None):
    return pl.pallas_call(
        kernel,
        in_specs=[spec for _, spec in inputs],
        out_specs=[spec for _, spec in outputs],
        out_shape=[what for what, _ in outputs],
        scratch_shapes=scratch,
        input_output_aliases=aliases or {},
        compiler_params=pltpu.CompilerParams(vmem_limit_bytes=mib * MIB),
    )(*[array for array, _ in inputs])


def swap(x, bit):
    count = lax.axis_size("lon")
    return lax.ppermute(x, "lon", [(i, i ^ (1 << bit)) for i in range(count)])


def sum_over_lon(x, upward):
    bits = lax.axis_size("lon").bit_length() - 1
    for i in range(bits):
        got = swap(x, i if upward else bits - 1 - i)
        if i == bits - 1:
            return x, got
        x = x + got


def lat_ring(bands, ways, turn):
    pairs = []
    for band in range(bands):
        for l in range(ways):
            east = l < ways // 2
            other = (l + ways // 2) % ways
            step = 1 if east == (turn == 0) else -1
            to = (band + step, l) if 0 <= band + step < bands else (band, other)
            pairs.append((l * bands + band, to[1] * bands + to[0]))
    return pairs


def on_device(tracer, zonal, meridional, cutoff_wave, polar_mask):
    levels, rows, cells = tracer.shape
    ways, bands = lax.axis_size("lon"), lax.axis_size("lat")
    width = wide(cells)
    total = cells * ways
    tables, backs = (jnp.asarray(x) for x in wave_tables(cells, ways))
    lon, band = lax.axis_index("lon"), lax.axis_index("lat")
    info = jnp.stack([lon, jnp.int32(ways), band, jnp.int32(bands)]).astype(jnp.int32)
    parts = levels // SUB
    steps = SUB // GROUP
    winds = (tracer, zonal, meridional)
    cut = jnp.where(polar_mask == 1, cutoff_wave, -1)
    cut_row = cut[None, :]
    ring0, ring1, own = call(
        edge_kernel,
        [(info, SMEM), (cut_row, VMEM), *[(x, HBM) for x in winds]],
        [(shape(4, levels, width), VMEM), (shape(4, levels, width), VMEM), (shape(2, levels, width), VMEM)],
        [pltpu.VMEM((10, levels, cells), F32), pltpu.SemaphoreType.DMA((10,))],
        FIRST_MIB,
    )
    ring = ("lon", "lat")
    got0 = lax.ppermute(ring0, ring, lat_ring(bands, ways, 0))
    got1 = lax.ppermute(ring1, ring, lat_ring(bands, ways, 1))

    grid = shape(SUB, rows, width)
    coef = shape(2, SUB * rows, KMAX)
    edge = shape(SUB, KMAX)
    flows = [(shape(4, SUB, width), VMEM), (shape(2, SUB, width), VMEM), (shape(2, SUB, KMAX), VMEM)]
    head = 5 + ways

    def room(what):
        return pltpu.VMEM(what.shape, what.dtype)

    buffer = pltpu.VMEM((SUB, rows, cells), F32)
    table_shape, back_shape = (shape(*x.shape[1:], dtype=BF16) for x in (tables, backs))
    sems = pltpu.SemaphoreType.DMA
    moved_a, coef_a, edge_a, table, back, kept = call(
        functools.partial(first_kernel, 0, cells),
        [(info, SMEM), (cut_row, VMEM), *[(x, HBM) for x in (*winds, tables, backs)]],
        [*[(x, VMEM) for x in (grid, coef, edge, table_shape, back_shape)], (shape(1, dtype=jnp.int32), SMEM)],
        [buffer, buffer, buffer, sems((3, SUB)), sems((2,))],
        FIRST_MIB,
    )

    def rest(limit, info, cut, cut_row, tracer, zonal, meridional, own, got0, got1, moved_a, coef_a, edge_a, table, back):
        pay = (shape(limit + head + 2, SUB, KMAX), VMEM)
        around = [(x, VMEM) for x in (own, got0, got1, table)]
        scalars = [(info, SMEM), (cut, SMEM)]
        joined = [(moved_a, *call(
            functools.partial(join_kernel, 0, cells, ways),
            [*scalars, (coef_a, VMEM), (edge_a, VMEM), *around],
            [*flows, pay],
            [room(coef)],
            8,
        ))]
        sums = [sum_over_lon(joined[0][4], True)]
        for part in range(1, parts):
            joined.append(call(
                functools.partial(first_join_kernel, part * SUB, cells, ways),
                [*scalars, *[(x, HBM) for x in (tracer, zonal, meridional)], *around],
                [(grid, VMEM), *flows, pay],
                [buffer, buffer, buffer, room(coef), room(edge), sems((3, SUB))],
                20,
            ))
            sums.append(sum_over_lon(joined[part][4], True))
        seconds = []
        for part in range(parts):
            moved, flow, edge_v, edge_cut, _ = joined[part]
            seconds.append(call(
                functools.partial(second_kernel, part * SUB, total, cells, ways),
                [*scalars, *[(x, VMEM) for x in (cut_row, *sums[part], flow, edge_v, edge_cut, moved, table, back)],
                 (zonal, VMEM), (meridional, VMEM)],
                [(grid, VMEM), (shape(limit + ways + 2, SUB, KMAX), VMEM)],
                [room(coef), room(coef), pltpu.VMEM((2, SUB, width), F32),
                 pltpu.VMEM((2 * SUB, 2 * KMAX), F32), room(edge), room(edge), room(grid)],
                20,
            ))
        sums = [sum_over_lon(x[1], True) for x in seconds]
        out = []
        for part in range(parts):
            out = call(
                functools.partial(third_kernel, part * SUB, total, cells, ways),
                [*scalars, *[(x, VMEM) for x in (cut_row, *sums[part], seconds[part][0], back)],
                 *[(x, HBM) for x in out]],
                [(shape(levels, rows, cells), HBM)],
                [room(coef), room(edge), buffer, sems((steps,))],
                12,
                {7: 0} if part else None,
            )
        return out[0]

    limits = sorted({min(-(-x * rows // 64), 2 * rows) for x in LIMITS})
    choice = sum((kept[0] > x).astype(jnp.int32) for x in limits[:-1])
    return lax.switch(
        choice, [functools.partial(rest, x) for x in limits],
        info, cut, cut_row, tracer, zonal, meridional, own, got0, got1, moved_a, coef_a, edge_a, table, back,
    )


def solution(mesh):
    placed = (
        P(None, "lat", "lon"),
        P(None, "lat", "lon"),
        P(None, "lat", "lon"),
        P("lat"),
        P("lat"),
    )
    return jax.shard_map(
        on_device, mesh=mesh, in_specs=placed, out_specs=P(None, "lat", "lon"), check_vma=False
    )
```
